256 devices in a mesh: dp: 4 (over x), segment: 2 (over core), band: 32 (over z, y).
Axes of the slice: x: 4, y: 4, z: 8, core: 2. Of those that a mesh axis runs over, the one named last changes fastest.
Arguments:
- fields: bfloat16 [4, 2, 256, 16, 512], P('dp', None, 'band'), may hold values from -6 to 6
- cell_mask: int32 [4, 2, 256, 16], P('dp', None, 'band'), may hold values 0 or 1
- merge_weight: bfloat16 [2, 1024, 512], P('segment', 'dp'), may hold values from -0.1875 to 0.1875
- qkv_weight: bfloat16 [2, 512, 1536], P('segment', 'dp')
- out_weight: bfloat16 [2, 512, 512], P('segment', 'dp'), may hold values from -1 to 1
- norm_gain: bfloat16 [2, 512], P('segment', 'dp'), may hold values from 0.099609375 to 1.8984375
- out_cotangent: bfloat16 [4, 2, 256, 16, 512], P('dp', None, 'band'), may hold values from -6 to 6
Outputs:
- section_out: bfloat16 [2, 4, 2, 256, 16, 512], P('segment', 'dp', None, 'band')
- merge_grad: float32 [2, 1024, 512], P('segment', 'dp')
- qkv_grad: float32 [2, 512, 1536], P('segment', 'dp')
- out_grad: float32 [2, 512, 512], P('segment', 'dp')
- gain_grad: float32 [2, 512], P('segment', 'dp')
The draws below stay inside these ranges and needn't reach their ends.
Inputs may be any that keep to these rules, and one draw needn't show every extreme that they name: `cell_mask`: 1 marks a cell whose keys may be attended.
All inputs are finite; a program needn't handle non-finite values. No bound on the sum of `cell_mask` on one device may be relied on, other than what follows from the above.
Results may differ from the reference program's by a relative error of at most 0.03.
Values may be sent and summed in bfloat16 or wider, within the bound.
A program may use at most 128 MiB of HBM per device.

```python
import jax
import jax.numpy as jnp
from jax import lax

D = 512
HEADS = 8
WH = 8
WW = 16
SH = 4
SW = 8
W_LON = 16
MICRO = 2
SECTIONS = 2
SAMPLES = 4
NLAT = 256
N_BAND = 32


def draw_qkv_weight(key, part):
    first_key = jax.random.fold_in(key, 0)
    drawn = jax.random.normal(first_key, (SECTIONS, D, 3 * D), jnp.float32) * D ** (-0.5)
    return drawn.astype(jnp.bfloat16)


def set_ends(values, key, low, high):
    index_at = [jax.random.randint(jax.random.fold_in(key, axis), (), 0, length) for axis, length in enumerate(values.shape)]
    main_axis = values.shape.index(max(values.shape))
    next_to = index_at[:main_axis] + [(index_at[main_axis] + 1) % values.shape[main_axis]] + index_at[main_axis + 1:]
    return values.at[tuple(index_at)].set(low).at[tuple(next_to)].set(high)


def levels(key, shape, pieces, least, top_value):
    gain = 1.0
    for axis_at, blocks in pieces:
        heights = jax.random.uniform(jax.random.fold_in(jax.random.fold_in(key, 6), axis_at), (blocks,), jnp.float32, least / len(pieces), top_value / len(pieces))
        gain = gain * jnp.repeat(jnp.exp(heights), shape[axis_at] // blocks).reshape((-1,) + (1,) * (len(shape) - 1 - axis_at))
    return gain


def centred(own_key, extent, scale, reach, shards=(), kind=jnp.bfloat16):
    values = scale * jax.random.normal(own_key, extent, jnp.float32)
    if shards:
        values = values * levels(own_key, extent, shards, -0.22, 0.18)
    return jnp.clip(values, -reach, reach).astype(kind)


def setup_inputs(seed: int = 0) -> dict:
    splits = jax.random.split(jax.random.key(seed), 8)
    fields = centred(splits[0], (SAMPLES, MICRO, NLAT, W_LON, D), 1.0, 6.0, ((0, 4), (2, 32)))
    cell_mask = set_ends((jax.random.randint(splits[1], (SAMPLES, MICRO, NLAT, W_LON), 0, 8) < 7).astype(jnp.int32), jax.random.fold_in(splits[1], 1), 0, 1)
    merge_weight = centred(splits[2], (SECTIONS, 2 * D, D), (2 * D) ** -0.5, 0.1875, ((0, 2), (1, 4)))
    qkv_weight = draw_qkv_weight(jax.random.fold_in(splits[7], 71), 0)
    out_weight = centred(splits[4], (SECTIONS, D, D), (D // 16) ** -0.5, 1.0, ((0, 2), (1, 4)))
    norm_gain = jnp.clip(1.0 + 0.18 * jax.random.normal(splits[5], (SECTIONS, D), jnp.float32), 0.099609375, 1.8984375).astype(jnp.bfloat16)
    out_cotangent = centred(splits[6], (SAMPLES, MICRO, NLAT, W_LON, D), 1.0, 6.0, ((0, 4), (2, 32)))
    return dict(fields=fields, cell_mask=cell_mask, merge_weight=merge_weight, qkv_weight=qkv_weight, out_weight=out_weight, norm_gain=norm_gain, out_cotangent=out_cotangent)


EPSILON = 1e-05
MASKED = -1e+30

def normalize(update):
    average = lax.optimization_barrier(jnp.mean(update, axis=-1, keepdims=True))
    centered = update - average
    spread = lax.optimization_barrier(jnp.mean(centered * centered, axis=-1, keepdims=True))
    inverse = lax.rsqrt(spread + EPSILON)
    return (centered * inverse, inverse)

def window_pattern(lon_count):
    query_index = jnp.arange(WH * lon_count, dtype=jnp.int32)
    key_index = jnp.arange(2 * WH * lon_count, dtype=jnp.int32)
    query_row = query_index // lon_count
    query_col = query_index % lon_count
    key_row = key_index // lon_count
    key_col = key_index % lon_count
    lat_same = ((query_row + SH) // WH)[:, None] == (key_row // WH)[None, :]
    lon_same = ((query_col + SW) // WW)[:, None] == ((key_col + SW) // WW)[None, :]
    self_key = ((query_row + SH)[:, None] == key_row[None, :]) & (query_col[:, None] == key_col[None, :])
    return (lat_same & lon_same, self_key)

def attend(queries, keyvals, usable):
    row_count, lon_count, feature = queries.shape
    blocks = row_count // WH
    head_dim = feature // HEADS
    query_blocks = queries.reshape(blocks, WH * lon_count, HEADS, head_dim).astype(jnp.float32)
    kv_blocks = keyvals.reshape(blocks + 1, WH * lon_count, 2, HEADS, head_dim)
    key_pairs = jnp.concatenate([kv_blocks[:-1], kv_blocks[1:]], axis=1).astype(jnp.float32)
    use_blocks = usable.reshape(blocks + 1, WH * lon_count)
    use_pairs = jnp.concatenate([use_blocks[:-1], use_blocks[1:]], axis=1)
    inside, self_key = window_pattern(lon_count)
    allowed = inside[None] & (use_pairs[:, None, :] | self_key[None])
    scores = jnp.einsum('nqhd,nkhd->nhqk', query_blocks, key_pairs[:, :, 0]) * head_dim ** (-0.5)
    scores = jnp.where(allowed[:, None], scores, MASKED)
    highest = lax.optimization_barrier(jnp.max(scores, axis=-1, keepdims=True))
    weights = jnp.exp(scores - highest)
    attn_prob = (weights / lax.optimization_barrier(jnp.sum(weights, axis=-1, keepdims=True))).astype(jnp.bfloat16)
    mixture = jnp.einsum('nhqk,nkhd->nqhd', attn_prob.astype(jnp.float32), key_pairs[:, :, 1])
    return mixture.reshape(row_count, lon_count, feature).astype(jnp.bfloat16)

def band_terms(left, right):
    left_bands = left.reshape(MICRO, N_BAND, -1, left.shape[-1]).astype(jnp.float32)
    right_bands = right.reshape(MICRO, N_BAND, -1, right.shape[-1]).astype(jnp.float32)
    return jnp.einsum('mbta,mbtc->bac', left_bands, right_bands)

def rounded_sum(partials):
    return lax.optimization_barrier(jnp.sum(lax.optimization_barrier(partials.astype(jnp.bfloat16)).astype(jnp.float32), axis=0))

def reference(fields, cell_mask, merge_weight, qkv_weight, out_weight, norm_gain, out_cotangent):
    sections = merge_weight.shape[0]
    half_count = sections // 2

    def forward_section(index, chain_in, side_in, usable):
        joined = jnp.concatenate([chain_in, side_in], axis=-1)
        update = jnp.dot(joined, merge_weight[index], preferred_element_type=jnp.float32)
        normed, inverse = normalize(update)
        hidden = (normed * norm_gain[index].astype(jnp.float32)).astype(jnp.bfloat16)
        projected = jnp.dot(hidden, qkv_weight[index], preferred_element_type=jnp.float32)
        queries = projected[..., :D].astype(jnp.bfloat16)
        keyvals = projected[..., D:].astype(jnp.bfloat16)
        padded = jnp.pad(keyvals, ((SH, SH), (0, 0), (0, 0)))
        mixture = attend(queries, padded, usable)
        result = (update + jnp.dot(mixture, out_weight[index], preferred_element_type=jnp.float32)).astype(jnp.bfloat16)
        return (result, (joined, normed, inverse, hidden, queries, padded, mixture))

    def backward_section(index, grad_out, record, usable):
        joined, normed, inverse, hidden, queries, padded, mixture = record
        row_total = queries.shape[0]
        grad_mixture = jnp.dot(grad_out, out_weight[index].T, preferred_element_type=jnp.float32).astype(jnp.bfloat16)
        unused, pull_back = jax.vjp(lambda query_in, keyval_in: attend(query_in, keyval_in, usable), queries, padded)
        grad_query, grad_keyval = pull_back(grad_mixture)
        grad_proj = jnp.concatenate([grad_query, grad_keyval[SH:SH + row_total]], axis=-1)
        grad_hidden = jnp.dot(grad_proj, qkv_weight[index].T, preferred_element_type=jnp.float32)
        grad_normed = grad_hidden * norm_gain[index].astype(jnp.float32)
        grad_update = (grad_out.astype(jnp.float32) + inverse * (grad_normed - lax.optimization_barrier(jnp.mean(grad_normed, axis=-1, keepdims=True)) - normed * lax.optimization_barrier(jnp.mean(grad_normed * normed, axis=-1, keepdims=True)))).astype(jnp.bfloat16)
        grad_joined = jnp.dot(grad_update, merge_weight[index].T, preferred_element_type=jnp.float32)
        terms = (joined, grad_update, hidden, grad_proj, mixture, grad_out, grad_hidden, normed)
        return (grad_joined, terms)

    def run_micro(inputs, usable, cotangent):
        outputs = []
        records = []
        for index in range(sections):
            chain_in = inputs if index == 0 else outputs[index - 1]
            side_in = inputs if index < half_count else outputs[sections - 1 - index]
            result, record = forward_section(index, chain_in, side_in, usable)
            outputs.append(result)
            records.append(record)
        flows = [None] * sections
        terms_all = [None] * sections
        for index in range(sections - 1, -1, -1):
            grad_out = cotangent if index == sections - 1 else flows[index].astype(jnp.bfloat16)
            grad_joined, terms = backward_section(index, grad_out, records[index], usable)
            grad_chain = grad_joined[..., :D].astype(jnp.bfloat16).astype(jnp.float32)
            grad_side = grad_joined[..., D:].astype(jnp.bfloat16).astype(jnp.float32)
            if index > 0:
                flows[index - 1] = grad_chain if flows[index - 1] is None else flows[index - 1] + grad_chain
            if index >= half_count:
                target = sections - 1 - index
                flows[target] = grad_side if flows[target] is None else flows[target] + grad_side
            terms_all[index] = terms
        return (jnp.stack(outputs), terms_all)

    def per_sample(totals, sample):
        inputs, mask, cotangent = sample
        usable = jnp.pad(mask == 1, ((0, 0), (SH, SH), (0, 0)))
        section_outs = []
        micro_terms = []
        for micro_no in range(MICRO):
            outputs, terms_all = run_micro(inputs[micro_no], usable[micro_no], cotangent[micro_no])
            section_outs.append(outputs)
            micro_terms.append(terms_all)
        total_merge, total_qkv, total_out, total_gain = totals
        for index in range(sections):
            stacked = [jnp.stack([micro_terms[micro_no][index][position] for micro_no in range(MICRO)]) for position in range(8)]
            total_merge = total_merge.at[index].add(rounded_sum(band_terms(stacked[0], stacked[1])))
            total_qkv = total_qkv.at[index].add(rounded_sum(band_terms(stacked[2], stacked[3])))
            total_out = total_out.at[index].add(rounded_sum(band_terms(stacked[4], stacked[5])))
            gain_parts = lax.optimization_barrier(jnp.sum((stacked[6] * stacked[7]).reshape(MICRO, N_BAND, -1, D), axis=(0, 2)))
            total_gain = total_gain.at[index].add(rounded_sum(gain_parts))
        return ((total_merge, total_qkv, total_out, total_gain), jnp.stack(section_outs, axis=1))
    initial = (jnp.zeros(merge_weight.shape, jnp.float32), jnp.zeros(qkv_weight.shape, jnp.float32), jnp.zeros(out_weight.shape, jnp.float32), jnp.zeros(norm_gain.shape, jnp.float32))
    totals, outputs = lax.scan(per_sample, initial, (fields, cell_mask, out_cotangent))
    section_out = jnp.swapaxes(outputs, 0, 1)
    return (section_out, totals[0], totals[1], totals[2], totals[3])
```

```python
import functools

import jax
import jax.numpy as jnp
from jax import lax
from jax.experimental import pallas as pl
from jax.experimental.pallas import tpu as pltpu
from jax.sharding import PartitionSpec as P

D = 512
HEADS = 8
NX = 4
NY = 4
NZ = 8
TOK = 128
HALF = 64
COLS = 5 * D
EPSILON = 1e-05
MASKED = -1e30
SWAP = (0, 2, 1, 3)
VMEM_LIMIT = 56 * 1024 * 1024
MESH = pl.DeviceIdType.MESH
BF = jnp.bfloat16
F32 = jnp.float32


def dot(left, right):
    return lax.dot_general(left, right, (((1,), (0,)), ((), ())), preferred_element_type=F32)


def dot_nt(left, right):
    return lax.dot_general(left, right, (((1,), (1,)), ((), ())), preferred_element_type=F32)


def dot_tn(left, right):
    return lax.dot_general(left, right, (((0,), (0,)), ((), ())), preferred_element_type=F32)


def rows(index, size):
    return pl.ds(pl.multiple_of(index * size, size), size)


class Links:
    def __init__(self, send, recv, local):
        self.send, self.recv, self.local = send, recv, local
        self.used = 0
        self.used_local = 0
        self.started = []

    def put(self, src, dst, device):
        copy = pltpu.make_async_remote_copy(
            src_ref=src,
            dst_ref=dst,
            send_sem=self.send.at[self.used],
            recv_sem=self.recv.at[self.used],
            device_id=device,
            device_id_type=MESH,
        )
        self.used += 1
        self.started.append(copy)
        copy.start()
        return copy

    def keep(self, src, dst):
        copy = pltpu.make_async_copy(src, dst, self.local.at[self.used_local])
        self.used_local += 1
        copy.start()
        return copy

    def drain(self):
        for copy in self.started:
            copy.wait_send()


def place():
    d = lax.axis_index("dp")
    s = lax.axis_index("segment")
    b = lax.axis_index("band")
    return d, s, b


def x_dev(d, step):
    return {"dp": lax.rem(d + step, NX)}


def y_dev(b, step):
    z, y = b // NY, lax.rem(b, NY)
    return {"band": z * NY + lax.rem(y + step, NY)}


def z_dev(b, step):
    z, y = b // NY, lax.rem(b, NY)
    return {"band": lax.rem(z + step, NZ) * NY + y}


def barrier(devices):
    sem = pltpu.get_barrier_semaphore()
    for device in devices:
        pl.semaphore_signal(sem, inc=1, device_id=device, device_id_type=MESH)
    pl.semaphore_wait(sem, len(devices))


def band_step(b, step):
    count = NY * NZ
    return lax.rem(b + step + count, count)


def gather_kernel(x_in, g_in, use_in, wm_in, wq_in, wo_in, gain_in,
                  x_out, g_out, use_out, wm, wq, wo, gain, send, recv, local):
    d, s, b = place()
    right, left = x_dev(d, 1), x_dev(d, NX - 1)
    core = {"segment": 1 - s}
    before, after = {"band": band_step(b, -1)}, {"band": band_step(b, 1)}
    barrier([right, left, core, before, after])
    link = Links(send, recv, local)
    shifted = [
        link.put(x_in.at[s, pl.ds(0, HALF)], x_out.at[pl.ds(HALF, HALF)], before),
        link.put(use_in, use_out.at[1], before),
        link.put(g_in.at[s, pl.ds(0, HALF)], g_out.at[pl.ds(HALF, HALF)], before),
    ]
    own = [
        link.keep(x_in.at[s, pl.ds(HALF, HALF)], x_out.at[pl.ds(0, HALF)]),
        link.keep(use_in, use_out.at[0]),
        link.keep(g_in.at[s, pl.ds(HALF, HALF)], g_out.at[pl.ds(0, HALF)]),
    ]
    parts = ((wm_in, wm, 2 * TOK), (wq_in, wq, TOK), (wo_in, wo, TOK))

    def full(buffer, owner, size):
        return buffer.at[s, rows(owner, size)]

    def half(buffer, owner, size, which):
        start = pl.multiple_of(owner * size + which * (size // 2), size // 2)
        return buffer.at[s, pl.ds(start, size // 2)]

    to_right, to_left, to_core = [], [], []
    for src, dst, size in parts:
        to_right.append(link.put(src.at[0], full(dst, d, size), right))
        to_left.append(link.put(src.at[0], full(dst, d, size), left))
    gain_right = link.put(gain_in, gain.at[s, d], right)
    gain_left = link.put(gain_in, gain.at[s, d], left)
    for src, dst, size in parts:
        to_core.append(link.put(src.at[0], full(dst, d, size), core))
        own.append(link.keep(src.at[0], full(dst, d, size)))
    to_core.append(link.put(gain_in, gain.at[s, d], core))
    own.append(link.keep(gain_in, gain.at[s, d]))
    from_left, from_right = lax.rem(d + NX - 1, NX), lax.rem(d + 1, NX)
    across = lax.rem(d + 2, NX)
    far = []
    for index, (src, dst, size) in enumerate(parts):
        to_right[index].wait_recv()
        one = link.put(half(dst, from_left, size, 0), half(dst, from_left, size, 0), right)
        to_core.append(link.put(full(dst, from_left, size), full(dst, from_left, size), core))
        to_left[index].wait_recv()
        two = link.put(half(dst, from_right, size, 1), half(dst, from_right, size, 1), left)
        to_core.append(link.put(full(dst, from_right, size), full(dst, from_right, size), core))
        far.append((one, two))
    gain_right.wait_recv()
    gain_far = link.put(gain.at[s, from_left], gain.at[s, from_left], right)
    to_core.append(link.put(gain.at[s, from_left], gain.at[s, from_left], core))
    gain_left.wait_recv()
    to_core.append(link.put(gain.at[s, from_right], gain.at[s, from_right], core))
    for index, (src, dst, size) in enumerate(parts):
        one, two = far[index]
        one.wait_recv()
        two.wait_recv()
        to_core.append(link.put(full(dst, across, size), full(dst, across, size), core))
    gain_far.wait_recv()
    to_core.append(link.put(gain.at[s, across], gain.at[s, across], core))
    for copy in shifted + to_core:
        copy.wait_recv()
    for copy in own:
        copy.wait()
    link.drain()


def compute_kernel(x_ref, cot_ref, use_ref, wm, wq, wo, gain, y_ref, grads, gain_grads,
                   normed_ref, hidden_ref, proj_ref, prob_ref, mix_ref, dproj_ref):
    b = lax.axis_index("band")
    last = b == lax.axis_size("band") - 1
    lane = lax.broadcasted_iota(jnp.int32, (8, TOK), 1)
    own_use = pltpu.roll(use_ref[0], HALF, 1)
    next_use = pltpu.roll(use_ref[1], HALF, 1)
    usable = jnp.where(lane < HALF, own_use, next_use)[0:1]
    query = lax.broadcasted_iota(jnp.int32, (TOK, TOK), 0)
    key = lax.broadcasted_iota(jnp.int32, (TOK, TOK), 1)
    same_lon = (query % 16 // 8) == (key % 16 // 8)
    same_lat = ((query // HALF) == (key // HALF)) | jnp.logical_not(last)
    open_key = jnp.broadcast_to(usable, (TOK, TOK)) > 0.5
    allowed = same_lon & same_lat & (open_key | (query == key))
    first = lax.broadcasted_iota(jnp.int32, (TOK, TOK), 1) < HALF
    zero = jnp.zeros((TOK, TOK), F32)
    head0 = jnp.where(first, zero + 1.0, zero).astype(BF)
    head1 = jnp.where(first, zero, zero + 1.0).astype(BF)

    def pair_cat(values):
        return jnp.concatenate([values * head0, values * head1], axis=0)

    def gain_row(sec):
        return jnp.concatenate([gain[sec, j][0:1] for j in range(4)], axis=1)

    def forward(sec, x):
        update = dot(x, wm[sec, 0:D]) + dot(x, wm[sec, D : 2 * D])
        average = jnp.mean(update, axis=-1, keepdims=True)
        centered = update - average
        spread = jnp.mean(centered * centered, axis=-1, keepdims=True)
        inverse = lax.rsqrt(spread + EPSILON)
        normed = centered * inverse
        normed_ref[sec] = normed
        hidden = (normed * gain_row(sec)).astype(BF)
        hidden_ref[sec] = hidden
        proj_ref[sec] = dot(hidden, wq[sec]).astype(BF)
        for i in range(HEADS // 2):
            cols = slice(TOK * i, TOK * (i + 1))
            q = proj_ref[sec, :, cols]
            k = proj_ref[sec, :, D + TOK * i : D + TOK * (i + 1)]
            v = proj_ref[sec, :, 2 * D + TOK * i : 2 * D + TOK * (i + 1)]
            scores = dot_nt(q, pair_cat(k)) * 0.125
            probs = []
            for h in range(2):
                one = jnp.where(allowed, scores[:, TOK * h : TOK * (h + 1)], MASKED)
                weights = jnp.exp(one - jnp.max(one, axis=-1, keepdims=True))
                probs.append(weights / jnp.sum(weights, axis=-1, keepdims=True))
            prob = jnp.concatenate(probs, axis=1).astype(BF)
            prob_ref[sec, i] = prob
            mix_ref[sec, :, cols] = dot(prob, pair_cat(v)).astype(BF)
        y = (update + dot(mix_ref[sec], wo[sec])).astype(BF)
        y_ref[sec] = y
        return y, inverse

    def backward(sec, x, g, inverse):
        gm = dot_nt(g, wo[sec]).astype(BF)
        for i in range(HEADS // 2):
            cols = slice(TOK * i, TOK * (i + 1))
            q = proj_ref[sec, :, cols]
            k = proj_ref[sec, :, D + TOK * i : D + TOK * (i + 1)]
            v = proj_ref[sec, :, 2 * D + TOK * i : 2 * D + TOK * (i + 1)]
            gm_pair = gm[:, cols]
            prob = prob_ref[sec, i]
            dprob = dot_nt(gm_pair, pair_cat(v))
            pieces = []
            for h in range(2):
                half = slice(TOK * h, TOK * (h + 1))
                p = prob[:, half].astype(F32)
                dp = dprob[:, half]
                pieces.append(p * (dp - jnp.sum(dp * p, axis=-1, keepdims=True)) * 0.125)
            dscore = jnp.concatenate(pieces, axis=1).astype(BF)
            dproj_ref[:, cols] = dot(dscore, pair_cat(k)).astype(BF)
            dk = dot_tn(dscore, q)
            dv = dot_tn(prob, gm_pair)
            dproj_ref[:, D + TOK * i : D + TOK * (i + 1)] = jnp.where(first, dk[:TOK], dk[TOK:]).astype(BF)
            dproj_ref[:, 2 * D + TOK * i : 2 * D + TOK * (i + 1)] = jnp.where(first, dv[:TOK], dv[TOK:]).astype(BF)
        dhidden = dot_nt(dproj_ref[...], wq[sec])
        normed = normed_ref[sec]
        dgain = jnp.sum(dhidden * normed, axis=0, keepdims=True)
        for j in range(4):
            gain_grads[sec, j] = jnp.broadcast_to(dgain[:, TOK * j : TOK * (j + 1)], (8, TOK))
        dnormed = dhidden * gain_row(sec)
        gu = (
            g.astype(F32)
            + inverse
            * (
                dnormed
                - jnp.mean(dnormed, axis=-1, keepdims=True)
                - normed * jnp.mean(dnormed * normed, axis=-1, keepdims=True)
            )
        ).astype(BF)
        for c in range(4):
            part = slice(TOK * c, TOK * (c + 1))
            swapped = slice(TOK * SWAP[c], TOK * (SWAP[c] + 1))
            grads[sec, swapped, 0:D] = dot_tn(x[:, part], gu).astype(BF)
            grads[sec, part, D : 4 * D] = dot_tn(hidden_ref[sec, :, part], dproj_ref[...]).astype(BF)
            grads[sec, part, 4 * D : 5 * D] = dot_tn(mix_ref[sec, :, part], g).astype(BF)
        return gu

    x0 = x_ref[...]
    y0, inverse0 = forward(0, x0)
    y1, inverse1 = forward(1, y0)
    cot = cot_ref[...]
    gu = backward(1, y0, cot, inverse1)
    chain = dot_nt(gu, wm[1, 0:D]).astype(BF).astype(F32)
    side = dot_nt(gu, wm[1, D : 2 * D]).astype(BF).astype(F32)
    backward(0, x0, (chain + side).astype(BF), inverse0)


def reduce_kernel(y_ref, grads, gain_grads, y_home, total, merge_other, gain_total,
                  core_in, x_one, x_two, x_sum, y_one, y_two, y_sum, z_in, z_all,
                  gain_core, gain_sum, gain_x, gain_y, gain_z, send, recv, local):
    d, s, b = place()
    z, y = b // NY, lax.rem(b, NY)
    other = 1 - s
    core = {"segment": other}
    nxt, prev = band_step(b, 1), band_step(b, -1)
    x_right, x_left = x_dev(d, 1), x_dev(d, NX - 1)
    y_right, y_left = y_dev(b, 1), y_dev(b, NY - 1)
    barrier(
        [core]
        + [x_dev(d, k) for k in range(1, NX)]
        + [y_dev(b, k) for k in range(1, NY)]
        + [z_dev(b, k) for k in range(1, NZ)]
        + [{"band": nxt}, {"band": prev}]
        + [{"band": nxt, "segment": other}, {"band": prev, "segment": other}]
    )
    link = Links(send, recv, local)
    lo, hi = pl.ds(0, HALF), pl.ds(HALF, HALF)

    order = [lax.rem(d + k, NX) for k in (2, 1, 3, 0)]
    core_copies = [
        link.put(grads.at[other, rows(j, TOK)], core_in.at[rows(j, TOK)], core) for j in order
    ]
    gain_core_copy = link.put(gain_grads.at[other], gain_core, core)
    home = [
        link.put(y_ref.at[s, hi], y_home.at[s, lo], {"band": nxt}),
        link.put(y_ref.at[other, lo], y_home.at[s, hi], core),
        link.put(y_ref.at[other, hi], y_home.at[s, lo], {"band": nxt, "segment": other}),
    ]
    stays = link.keep(y_ref.at[s, lo], y_home.at[s, hi])

    def add_rows(count, step, terms, store):
        def one(i, carry):
            at = pl.ds(pl.multiple_of(i * step, step), step)
            value = None
            for term in terms:
                loaded = term(at).astype(F32)
                value = loaded if value is None else value + loaded
            store(at, value.astype(BF))
            return carry

        lax.fori_loop(0, count // step, one, 0)

    def at_row(j, at_size):
        return lambda i: None

    def core_sum(which, j):
        core_copies[which].wait_recv()
        base = j * TOK

        def one(i, carry):
            at = pl.ds(pl.multiple_of(base + i * 16, 16), 16)
            grads[s, at] = (grads[s, at].astype(F32) + core_in[at].astype(F32)).astype(BF)
            return carry

        lax.fori_loop(0, TOK // 16, one, 0)

    def chunk_half(j, which):
        return grads.at[s, pl.ds(pl.multiple_of(j * TOK + which * HALF, HALF), HALF)]

    core_sum(0, order[0])
    one_right = link.put(chunk_half(order[0], 0), x_one.at[0], x_right)
    one_left = link.put(chunk_half(order[0], 1), x_one.at[1], x_left)
    gain_core_copy.wait_recv()
    gain_sum[...] = gain_grads[s] + gain_core[...]
    gain_x[0] = gain_sum[d]
    gain_copies = [
        link.put(gain_sum.at[lax.rem(d + k, NX)], gain_x.at[k], x_dev(d, k)) for k in range(1, NX)
    ]
    core_sum(1, order[1])
    one_right.wait_recv()

    def fold(j, offset, source):
        def one(i, carry):
            at = pl.ds(pl.multiple_of(j * TOK + offset + i * 16, 16), 16)
            src = pl.ds(pl.multiple_of(i * 16, 16), 16)
            grads[s, at] = (grads[s, at].astype(F32) + source[src].astype(F32)).astype(BF)
            return carry

        lax.fori_loop(0, HALF // 16, one, 0)

    fold(order[1], 0, x_one.at[0])
    two_right = link.put(grads.at[s, rows(order[1], TOK)], x_two.at[0], x_right)
    core_sum(2, order[2])
    one_left.wait_recv()
    fold(order[2], HALF, x_one.at[1])
    two_left = link.put(grads.at[s, rows(order[2], TOK)], x_two.at[1], x_left)
    core_sum(3, order[3])
    for copy in gain_copies:
        copy.wait_recv()
    gain_y[0] = gain_x[0] + gain_x[1] + gain_x[2] + gain_x[3]
    gain_copies = [link.put(gain_y.at[0], gain_y.at[k], y_dev(b, k)) for k in range(1, NY)]
    two_right.wait_recv()
    two_left.wait_recv()

    def x_add(i, carry):
        at = pl.ds(pl.multiple_of(i * 16, 16), 16)
        mine = pl.ds(pl.multiple_of(d * TOK + i * 16, 16), 16)
        x_sum[at] = (
            grads[s, mine].astype(F32) + x_two[0, at].astype(F32) + x_two[1, at].astype(F32)
        ).astype(BF)
        return carry

    lax.fori_loop(0, TOK // 16, x_add, 0)

    wide = COLS // NY

    def col(j):
        return pl.ds(pl.multiple_of(j * wide, 128), wide)

    yn = [lax.rem(y + k, NY) for k in range(NY)]
    if NY == 4:
        one_right = link.put(x_sum.at[lo, col(yn[2])], y_one.at[0], y_right)
        one_left = link.put(x_sum.at[hi, col(yn[2])], y_one.at[1], y_left)
        one_right.wait_recv()
        x_sum[lo, col(yn[1])] = (x_sum[lo, col(yn[1])].astype(F32) + y_one[0].astype(F32)).astype(BF)
        two_right = link.put(x_sum.at[:, col(yn[1])], y_two.at[0], y_right)
        one_left.wait_recv()
        x_sum[hi, col(yn[3])] = (x_sum[hi, col(yn[3])].astype(F32) + y_one[1].astype(F32)).astype(BF)
        two_left = link.put(x_sum.at[:, col(yn[3])], y_two.at[1], y_left)
    else:
        two_right = link.put(x_sum.at[:, col(yn[1])], y_two.at[0], y_right)
    for copy in gain_copies:
        copy.wait_recv()
    gain_z[0] = functools.reduce(lambda p, q: p + q, [gain_y[k] for k in range(NY)])
    gain_copies = [link.put(gain_z.at[0], gain_z.at[k], z_dev(b, k)) for k in range(1, NZ)]
    two_right.wait_recv()
    value = x_sum[:, col(y)].astype(F32) + y_two[0].astype(F32)
    if NY == 4:
        two_left.wait_recv()
        value = value + y_two[1].astype(F32)
    y_sum[...] = value.astype(BF)

    tall = TOK // NZ
    z_copies = [
        link.put(y_sum.at[rows(lax.rem(z + k, NZ), tall)], z_in.at[k], z_dev(b, k))
        for k in range(1, NZ)
    ]
    mine = rows(z, tall)
    value = y_sum[mine].astype(F32)
    for k in range(1, NZ):
        z_copies[k - 1].wait_recv()
        value = value + z_in[k].astype(F32)
    z_all[mine] = value.astype(BF)
    z_copies = [link.put(z_all.at[mine], z_all.at[mine], z_dev(b, k)) for k in range(1, NZ)]
    for copy in gain_copies:
        copy.wait_recv()
    gain_total[...] = functools.reduce(lambda p, q: p + q, [gain_z[k] for k in range(NZ)])
    for copy in z_copies:
        copy.wait_recv()

    to_right = link.put(z_all, total.at[:, col(y)], y_right)
    if NY == 4:
        to_left = link.put(z_all, total.at[:, col(y)], y_left)
    total[:, col(y)] = z_all[...]
    to_right.wait_recv()
    if NY == 4:
        far_right = link.put(total.at[lo, col(yn[3])], total.at[lo, col(yn[3])], y_right)
        to_left.wait_recv()
        far_left = link.put(total.at[hi, col(yn[1])], total.at[hi, col(yn[1])], y_left)
        far_right.wait_recv()
        far_left.wait_recv()
    merge_copy = link.put(total.at[:, pl.ds(0, D)], merge_other, x_dev(d, 2))
    merge_copy.wait_recv()
    for copy in home:
        copy.wait_recv()
    stays.wait()
    link.drain()


def vmem(count):
    return [pl.BlockSpec(memory_space=pltpu.VMEM)] * count


def anywhere(count):
    return [pl.BlockSpec(memory_space=pl.ANY)] * count


def shape(dims, dtype=BF):
    return jax.ShapeDtypeStruct(dims, dtype)


def sems(count, local):
    return [
        pltpu.SemaphoreType.DMA((count,)),
        pltpu.SemaphoreType.DMA((count,)),
        pltpu.SemaphoreType.DMA((local,)),
    ]


def params(collective):
    if collective is None:
        return pltpu.CompilerParams(vmem_limit_bytes=VMEM_LIMIT)
    return pltpu.CompilerParams(
        collective_id=collective, has_side_effects=True, vmem_limit_bytes=VMEM_LIMIT
    )


def body(fields, cell_mask, merge_weight, qkv_weight, out_weight, norm_gain, out_cotangent):
    d, s, b = place()
    x_in = fields.reshape(2, TOK, D)
    g_in = out_cotangent.reshape(2, TOK, D)
    mask = lax.dynamic_index_in_dim(cell_mask[0], s, 0, keepdims=False).reshape(1, TOK)
    use = jnp.broadcast_to((mask == 1).astype(F32), (8, TOK))
    gain = jnp.broadcast_to(norm_gain.astype(F32), (8, TOK))
    x, cot, use, wm, wq, wo, gains = pl.pallas_call(
        gather_kernel,
        out_shape=(
            shape((TOK, D)), shape((TOK, D)), shape((2, 8, TOK), F32),
            shape((2, 2 * D, D)), shape((2, D, 3 * D)), shape((2, D, D)),
            shape((2, 4, 8, TOK), F32),
        ),
        in_specs=anywhere(7),
        out_specs=vmem(7),
        scratch_shapes=sems(40, 8),
        compiler_params=params(0),
        name="gather",
    )(x_in, g_in, use, merge_weight, qkv_weight, out_weight, gain)
    y, grads, gain_grads = pl.pallas_call(
        compute_kernel,
        out_shape=(shape((2, TOK, D)), shape((2, D, COLS)), shape((2, 4, 8, TOK), F32)),
        in_specs=vmem(7),
        out_specs=vmem(3),
        scratch_shapes=[
            pltpu.VMEM((2, TOK, D), F32),
            pltpu.VMEM((2, TOK, D), BF),
            pltpu.VMEM((2, TOK, 3 * D), BF),
            pltpu.VMEM((2, HEADS // 2, TOK, 2 * TOK), BF),
            pltpu.VMEM((2, TOK, D), BF),
            pltpu.VMEM((TOK, 3 * D), BF),
        ],
        compiler_params=params(None),
        name="compute",
    )(x, cot, use, wm, wq, wo, gains)
    wide = COLS // NY
    home, total, merge_other, gain_total = pl.pallas_call(
        reduce_kernel,
        out_shape=(
            shape((2, TOK, D)), shape((TOK, COLS)), shape((TOK, D)), shape((8, TOK), F32),
        ),
        in_specs=vmem(3),
        out_specs=vmem(4),
        scratch_shapes=[
            pltpu.VMEM((D, COLS), BF),
            pltpu.VMEM((2, HALF, COLS), BF),
            pltpu.VMEM((2, TOK, COLS), BF),
            pltpu.VMEM((TOK, COLS), BF),
            pltpu.VMEM((2, HALF, wide), BF),
            pltpu.VMEM((2, TOK, wide), BF),
            pltpu.VMEM((TOK, wide), BF),
            pltpu.VMEM((NZ, TOK // NZ, wide), BF),
            pltpu.VMEM((TOK, wide), BF),
            pltpu.VMEM((4, 8, TOK), F32),
            pltpu.VMEM((4, 8, TOK), F32),
            pltpu.VMEM((4, 8, TOK), F32),
            pltpu.VMEM((NY, 8, TOK), F32),
            pltpu.VMEM((NZ, 8, TOK), F32),
        ] + sems(64, 2),
        compiler_params=params(1),
        name="reduce",
    )(y, grads, gain_grads)
    section_home = home.reshape(1, 1, 2, 8, 16, D)
    own_merge, other_merge = total[:, :D].astype(F32), merge_other.astype(F32)
    upper = d // 2 == 1
    merge_grad = jnp.where(
        upper,
        jnp.concatenate([other_merge, own_merge], axis=0),
        jnp.concatenate([own_merge, other_merge], axis=0),
    )[None]
    qkv_grad = total[:, D : 4 * D].astype(F32)[None]
    out_grad = total[:, 4 * D :].astype(F32)[None]
    return (section_home, merge_grad, qkv_grad, out_grad, gain_total[0:1])


def solution(mesh):
    return jax.shard_map(
        body,
        mesh=mesh,
        in_specs=(
            P("dp", None, "band", None, None),
            P("dp", None, "band", None),
            P("segment", "dp", None),
            P("segment", "dp", None),
            P("segment", "dp", None),
            P("segment", "dp"),
            P("dp", None, "band", None, None),
        ),
        out_specs=(
            P("segment", "dp", None, "band", None, None),
            P("segment", "dp", None),
            P("segment", "dp", None),
            P("segment", "dp", None),
            P("segment", "dp"),
        ),
        check_vma=False,
    )
```

```python
import jax
import jax.numpy as jnp
from jax import lax
from jax.experimental import pallas as pl
from jax.experimental.pallas import tpu as pltpu
from jax.sharding import PartitionSpec as P

D = 512
HEADS = 8
NX = 4
NY = 4
NZ = 8
TOK = 128
HALF = 64
WIDE = 3 * D
PART = WIDE // NY
TALL = TOK // NZ
EPSILON = 1e-05
MASKED = -1e30
VMEM_LIMIT = 58 * 1024 * 1024
MESH = pl.DeviceIdType.MESH
BF = jnp.bfloat16
F32 = jnp.float32


def dot(left, right):
    return lax.dot_general(left, right, (((1,), (0,)), ((), ())), preferred_element_type=F32)


def dot_nt(left, right):
    return lax.dot_general(left, right, (((1,), (1,)), ((), ())), preferred_element_type=F32)


def dot_tn(left, right):
    return lax.dot_general(left, right, (((0,), (0,)), ((), ())), preferred_element_type=F32)


def span(index, size, unit=None):
    return pl.ds(pl.multiple_of(index, unit or size), size)


class Hop:
    def __init__(self, net, src, dst, device):
        at = net.used
        net.used += 1
        net.hops.append(self)
        self.copy = pltpu.make_async_remote_copy(
            src_ref=src,
            dst_ref=dst,
            send_sem=net.send.at[at],
            recv_sem=net.recv.at[at],
            device_id=device,
            device_id_type=MESH,
        )
        self.start = self.copy.start
        self.landed = self.copy.wait_recv
        self.sent = self.copy.wait_send


class Net:
    def __init__(self, send, recv, local):
        self.send, self.recv, self.local = send, recv, local
        self.used = 0
        self.kept = 0
        self.hops = []

    def hop(self, src, dst, device):
        return Hop(self, src, dst, device)

    def keep(self, src, dst):
        copy = pltpu.make_async_copy(src, dst, self.local.at[self.kept])
        self.kept += 1
        return copy


def start(hops):
    for hop in hops:
        hop.start()


def landed(hops):
    for hop in hops:
        hop.landed()


def add_into(count, dst, terms):
    def one(i, carry):
        at = i * 16
        value = terms[0](at).astype(F32)
        for term in terms[1:]:
            value = value + term(at).astype(F32)
        dst(at, value.astype(BF))
        return carry

    lax.fori_loop(0, count // 16, one, 0)


class Ring:
    def __init__(self, net, buf, rect, me, right, left, one_in, two_in):
        self.buf, self.one_in, self.two_in = buf, one_in, two_in
        step = [lax.rem(me + k, 4) for k in range(4)]
        self.rects = [rect(j) for j in step]
        self.nr = self.rects[0][1]
        far, after, before = self.rects[2], self.rects[1], self.rects[3]
        half = self.nr // 2
        self.one = [
            net.hop(self.view(far, 0, half), one_in.at[0], right),
            net.hop(self.view(far, half, half), one_in.at[1], left),
        ]
        self.two = [
            net.hop(self.view(after, 0, self.nr), two_in.at[0], right),
            net.hop(self.view(before, 0, self.nr), two_in.at[1], left),
        ]

    def index(self, rect, offset, count):
        r0, nr, c0, nc = rect
        first = pl.ds(offset, count) if isinstance(r0, int) else span(r0 + offset, count, 16)
        second = pl.ds(0, nc) if isinstance(c0, int) else span(c0, nc, 128)
        return (first, second)

    def view(self, rect, offset, count):
        return self.buf.at[self.index(rect, offset, count)]

    def rows_of(self, rect, base):
        r0, nr, c0, nc = rect

        def at(i):
            second = pl.ds(0, nc) if isinstance(c0, int) else span(c0, nc, 128)
            return (span(r0 + base + i, 16), second)

        return at

    def fold(self, which):
        self.one[which].landed()
        half = self.nr // 2
        rect, base = (self.rects[1], 0) if which == 0 else (self.rects[3], half)
        at = self.rows_of(rect, base)
        source = self.one_in.at[which]

        def store(i, value):
            self.buf[at(i)] = value

        add_into(half, store, [lambda i: self.buf[at(i)], lambda i: source[span(i, 16)]])
        self.two[which].start()

    def finish(self, dst):
        landed(self.two)
        at = self.rows_of(self.rects[0], 0)

        def store(i, value):
            dst[span(i, 16)] = value

        add_into(
            self.nr,
            store,
            [
                lambda i: self.buf[at(i)],
                lambda i: self.two_in[0, span(i, 16)],
                lambda i: self.two_in[1, span(i, 16)],
            ],
        )


def x_dev(d, step):
    return {"dp": lax.rem(d + step, NX)}


def y_dev(b, step):
    z, y = b // NY, lax.rem(b, NY)
    return {"band": z * NY + lax.rem(y + step, NY)}


def z_dev(b, step):
    z, y = b // NY, lax.rem(b, NY)
    return {"band": lax.rem(z + step, NZ) * NY + y}


def barrier(devices):
    sem = pltpu.get_barrier_semaphore()
    for device in devices:
        pl.semaphore_signal(sem, inc=1, device_id=device, device_id_type=MESH)
    pl.semaphore_wait(sem, len(devices))


def kernel(x_in, g_in, use_in, wm_in, wq_in, wo_in, gain_in,
           y_home, total, gain_total,
           x_ref, cot_ref, use_ref, wm, wq, wo, gain,
           y_ref, normed_ref, hidden_ref, proj_ref, prob_ref, mix_ref, dproj_ref,
           grads, gain_grads, core_in,
           ax_one, ax_two, ay_one, ay_two, qy_one, qy_two, qx_one, qx_two, a_sum, q_sum,
           y_sum, z_in, z_all,
           gain_core, gain_sum, gain_x, gain_y, gain_z, send, recv, local):
    d = lax.axis_index("dp")
    s = lax.axis_index("segment")
    b = lax.axis_index("band")
    z, y = b // NY, lax.rem(b, NY)
    other = 1 - s
    bands = NY * NZ
    nxt, prev = lax.rem(b + 1, bands), lax.rem(b + bands - 1, bands)
    core = {"segment": other}
    x_right, x_left = x_dev(d, 1), x_dev(d, NX - 1)
    y_right, y_left = y_dev(b, 1), y_dev(b, NY - 1)
    net = Net(send, recv, local)
    lo, hi = pl.ds(0, HALF), pl.ds(HALF, HALF)
    xd = [lax.rem(d + k, NX) for k in range(NX)]
    yd = [lax.rem(y + k, NY) for k in range(NY)]

    barrier(
        [core]
        + [x_dev(d, k) for k in range(1, NX)]
        + [y_dev(b, k) for k in range(1, NY)]
        + [z_dev(b, k) for k in range(1, NZ)]
        + [{"band": nxt}, {"band": prev}]
        + [{"band": nxt, "segment": other}, {"band": prev, "segment": other}]
    )

    shift = [
        net.hop(x_in.at[s, lo], x_ref.at[hi], {"band": prev}),
        net.hop(use_in.at[s], use_ref.at[1], {"band": prev}),
        net.hop(g_in.at[s, lo], cot_ref.at[hi], {"band": prev}),
    ]
    own = [
        net.keep(x_in.at[s, hi], x_ref.at[lo]),
        net.keep(use_in.at[s], use_ref.at[0]),
        net.keep(g_in.at[s, hi], cot_ref.at[lo]),
    ]
    gain[s, d] = jnp.broadcast_to(gain_in[...].astype(F32), (8, TOK))
    gain_hops = [net.hop(gain.at[s, d], gain.at[s, d], x_dev(d, k)) for k in range(1, NX)]
    gain_core_hops = [net.hop(gain.at[s, xd[0]], gain.at[s, xd[0]], core)] + [
        net.hop(gain.at[s, xd[NX - k]], gain.at[s, xd[NX - k]], core) for k in range(1, NX)
    ]

    class Gather:
        def __init__(self, src, dst, size):
            wide = dst.shape[-1]
            cols = span(y * (wide // NY), wide // NY)
            half, quarter = size // 2, size // 4

            def block(owner, offset, count):
                return dst.at[s, span(owner * size + offset, count, count)]

            def strip(owner):
                return dst.at[s, span(owner * size + half, half), cols]

            top, bottom = pl.ds(0, half), pl.ds(half, half)
            self.strips = [net.hop(src.at[0, bottom, cols], strip(d), x_dev(d, k)) for k in range(1, NX)]
            self.right = net.hop(src.at[0, top], block(d, 0, half), x_right)
            self.left = net.hop(src.at[0, top], block(d, 0, half), x_left)
            self.mine = net.hop(src.at[0], block(d, 0, size), core)
            self.local = net.keep(src.at[0], block(d, 0, size))
            self.spread = [
                [net.hop(strip(xd[NX - k]), strip(xd[NX - k]), y_dev(b, m)) for m in range(1, NY)]
                for k in range(1, NX)
            ]
            self.far_right = net.hop(block(xd[3], 0, quarter), block(xd[3], 0, quarter), x_right)
            self.far_left = net.hop(block(xd[1], quarter, quarter), block(xd[1], quarter, quarter), x_left)
            self.across = [
                net.hop(block(xd[NX - k], 0, size), block(xd[NX - k], 0, size), core)
                for k in range(1, NX)
            ]

        def begin(self):
            start(self.strips + [self.right, self.left, self.mine])
            self.local.start()

        def relay(self):
            for k in (1, 3, 2):
                self.strips[k - 1].landed()
                start(self.spread[k - 1])
            self.right.landed()
            self.far_right.start()
            self.left.landed()
            self.far_left.start()

        def pass_on(self):
            for k in (1, 3):
                landed(self.spread[k - 1])
                self.across[k - 1].start()
            landed(self.spread[1])
            landed([self.far_right, self.far_left])
            self.across[1].start()

        def ready(self):
            landed([self.mine] + self.across)
            self.local.wait()

    merge = Gather(wm_in, wm, 2 * TOK)
    qkv = Gather(wq_in, wq, TOK)
    outw = Gather(wo_in, wo, TOK)

    mine = grads.at[s]
    theirs = grads.at[other]
    a_order = [xd[k] for k in (2, 1, 3, 0)]
    q_order = [yd[k] for k in (2, 1, 3, 0)]

    def a_rows(j):
        return (0, span(j * TOK, TOK))

    def q_cols(j):
        return (1, pl.ds(0, D), span(j * PART, PART, 128))

    swap_a = [net.hop(theirs.at[a_rows(j)], core_in.at[a_rows(j)], core) for j in a_order]
    swap_q = [net.hop(theirs.at[q_cols(j)], core_in.at[q_cols(j)], core) for j in q_order]
    gain_swap = net.hop(gain_grads.at[other], gain_core, core)
    ring_ax = Ring(net, mine.at[0], lambda j: (j * TOK, TOK, 0, WIDE), d, x_right, x_left, ax_one, ax_two)
    ring_qy = Ring(net, mine.at[1], lambda j: (0, D, j * PART, PART), y, y_right, y_left, qy_one, qy_two)
    ring_ay = Ring(net, a_sum, lambda j: (0, TOK, j * PART, PART), y, y_right, y_left, ay_one, ay_two)
    ring_qx = Ring(net, q_sum, lambda j: (j * TOK, TOK, 0, PART), d, x_right, x_left, qx_one, qx_two)
    gain_x_hops = [net.hop(gain_sum.at[xd[k]], gain_x.at[k], x_dev(d, k)) for k in range(1, NX)]
    gain_y_hops = [net.hop(gain_y.at[0], gain_y.at[k], y_dev(b, k)) for k in range(1, NY)]
    gain_z_hops = [net.hop(gain_z.at[0], gain_z.at[k], z_dev(b, k)) for k in range(1, NZ)]
    z_rows = span(z * TALL, TALL)
    both = pl.ds(0, 2)
    z_hops = [
        net.hop(
            y_sum.at[both, span(lax.rem(z + k, NZ) * TALL, TALL)], z_in.at[k], z_dev(b, k)
        )
        for k in range(1, NZ)
    ]
    z_back = [net.hop(z_all.at[both, z_rows], z_all.at[both, z_rows], z_dev(b, k)) for k in range(1, NZ)]

    def col(j):
        return span(j * PART, PART, 128)

    all_rows = pl.ds(0, TOK)
    last_right = net.hop(z_all, total.at[both, all_rows, col(y)], y_right)
    last_left = net.hop(z_all, total.at[both, all_rows, col(y)], y_left)
    end_right = net.hop(total.at[both, lo, col(yd[3])], total.at[both, lo, col(yd[3])], y_right)
    end_left = net.hop(total.at[both, hi, col(yd[1])], total.at[both, hi, col(yd[1])], y_left)
    home = [
        net.hop(y_ref.at[other, lo], y_home.at[s, hi], core),
        net.hop(y_ref.at[s, hi], y_home.at[s, lo], {"band": nxt}),
        net.hop(y_ref.at[other, hi], y_home.at[s, lo], {"band": nxt, "segment": other}),
    ]
    stays = net.keep(y_ref.at[s, lo], y_home.at[s, hi])

    def a_core(i):
        swap_a[i].landed()
        base = a_order[i] * TOK

        def at(r):
            return (0, span(base + r, 16))

        def store(r, value):
            mine[at(r)] = value

        add_into(TOK, store, [lambda r: mine[at(r)], lambda r: core_in[at(r)]])

    def q_core(i):
        swap_q[i].landed()
        cols = span(q_order[i] * PART, PART, 128)

        def at(r):
            return (1, span(r, 16), cols)

        def store(r, value):
            mine[at(r)] = value

        add_into(D, store, [lambda r: mine[at(r)], lambda r: core_in[at(r)]])

    def swap():
        for hop_a, hop_q in zip(swap_a, swap_q):
            hop_a.start()
            hop_q.start()
        gain_swap.start()

    def stage1():
        a_core(0)
        start(ring_ax.one)
        q_core(0)
        start(ring_qy.one)
        for i in (1, 2):
            a_core(i)
            q_core(i)
        gain_swap.landed()
        gain_sum[...] = gain_grads[s] + gain_core[...]
        gain_x[0] = gain_sum[d]
        start(gain_x_hops)

    def stage2():
        for which in (0, 1):
            ring_ax.fold(which)
            ring_qy.fold(which)
        a_core(3)
        q_core(3)
        landed(gain_x_hops)
        gain_y[0] = (gain_x[0] + gain_x[1]) + (gain_x[2] + gain_x[3])
        start(gain_y_hops)

    def stage3():
        ring_ax.finish(a_sum)
        start(ring_ay.one)
        ring_qy.finish(q_sum)
        start(ring_qx.one)
        landed(gain_y_hops)
        gain_z[0] = (gain_y[0] + gain_y[1]) + (gain_y[2] + gain_y[3])
        start(gain_z_hops)

    def masks():
        lane = lax.broadcasted_iota(jnp.int32, (16, TOK), 1)
        sub = lax.broadcasted_iota(jnp.int32, (16, TOK), 0)
        spread = (lane % 16 == sub).astype(F32).astype(BF)
        lane8 = lax.broadcasted_iota(jnp.int32, (8, TOK), 1) // 16
        sub8 = lax.broadcasted_iota(jnp.int32, (8, TOK), 0)
        here = dot((use_ref[0] == 1).astype(F32).astype(BF), spread)
        there = dot((use_ref[1] == 1).astype(F32).astype(BF), spread)
        usable = jnp.sum(
            jnp.where(lane8 + 4 == sub8, here, 0.0) + jnp.where(lane8 - 4 == sub8, there, 0.0),
            axis=0, keepdims=True,
        )
        query = lax.broadcasted_iota(jnp.int32, (TOK, TOK), 0)
        key = lax.broadcasted_iota(jnp.int32, (TOK, TOK), 1)
        same_lon = (query % 16 // 8) == (key % 16 // 8)
        same_lat = ((query // HALF) == (key // HALF)) | jnp.logical_not(b == bands - 1)
        open_key = jnp.broadcast_to(usable, (TOK, TOK)) > 0.5
        return same_lon & same_lat & (open_key | (query == key))

    first = lax.broadcasted_iota(jnp.int32, (TOK, TOK), 1) < HALF
    zero = jnp.zeros((TOK, TOK), F32)
    head0 = jnp.where(first, zero + 1.0, zero).astype(BF)
    head1 = jnp.where(first, zero, zero + 1.0).astype(BF)

    def pair_cat(values):
        return jnp.concatenate([values * head0, values * head1], axis=0)

    def gain_row(sec):
        return jnp.concatenate([gain[sec, j][0:1] for j in range(4)], axis=1)

    def tile(sec, which, i):
        return proj_ref[sec, :, which * D + TOK * i : which * D + TOK * (i + 1)]

    def forward_merge(sec, x):
        update = dot(x, wm[sec, 0:D]) + dot(x, wm[sec, D : 2 * D])
        average = jnp.mean(update, axis=-1, keepdims=True)
        centered = update - average
        spread = jnp.mean(centered * centered, axis=-1, keepdims=True)
        inverse = lax.rsqrt(spread + EPSILON)
        normed = centered * inverse
        normed_ref[sec] = normed
        hidden_ref[sec] = (normed * gain_row(sec)).astype(BF)
        return update, inverse

    def forward_attend(sec, allowed):
        proj_ref[sec] = dot(hidden_ref[sec], wq[sec]).astype(BF)
        for i in range(HEADS // 2):
            scores = dot_nt(tile(sec, 0, i), pair_cat(tile(sec, 1, i))) * 0.125
            probs = []
            for h in range(2):
                one = jnp.where(allowed, scores[:, TOK * h : TOK * (h + 1)], MASKED)
                weights = jnp.exp(one - jnp.max(one, axis=-1, keepdims=True))
                probs.append(weights / jnp.sum(weights, axis=-1, keepdims=True))
            prob = jnp.concatenate(probs, axis=1).astype(BF)
            prob_ref[sec, i] = prob
            mix_ref[sec, :, TOK * i : TOK * (i + 1)] = dot(prob, pair_cat(tile(sec, 2, i))).astype(BF)

    def forward_out(sec, update):
        result = (update + dot(mix_ref[sec], wo[sec])).astype(BF)
        y_ref[sec] = result
        return result

    def backward_attend(sec, g):
        gm = dot_nt(g, wo[sec]).astype(BF)
        for i in range(HEADS // 2):
            q, k, v = tile(sec, 0, i), tile(sec, 1, i), tile(sec, 2, i)
            gm_pair = gm[:, TOK * i : TOK * (i + 1)]
            prob = prob_ref[sec, i]
            dprob = dot_nt(gm_pair, pair_cat(v))
            pieces = []
            for h in range(2):
                half = slice(TOK * h, TOK * (h + 1))
                p = prob[:, half].astype(F32)
                dp = dprob[:, half]
                pieces.append(p * (dp - jnp.sum(dp * p, axis=-1, keepdims=True)) * 0.125)
            dscore = jnp.concatenate(pieces, axis=1).astype(BF)
            dk = dot_tn(dscore, q)
            dv = dot_tn(prob, gm_pair)
            dproj_ref[:, TOK * i : TOK * (i + 1)] = dot(dscore, pair_cat(k)).astype(BF)
            dproj_ref[:, D + TOK * i : D + TOK * (i + 1)] = jnp.where(first, dk[:TOK], dk[TOK:]).astype(BF)
            dproj_ref[:, 2 * D + TOK * i : 2 * D + TOK * (i + 1)] = jnp.where(first, dv[:TOK], dv[TOK:]).astype(BF)

    def backward_terms(sec, x, g, inverse):
        dhidden = dot_nt(dproj_ref[...], wq[sec])
        normed = normed_ref[sec]
        dgain = jnp.sum(dhidden * normed, axis=0, keepdims=True)
        for j in range(4):
            gain_grads[sec, j] = jnp.broadcast_to(dgain[:, TOK * j : TOK * (j + 1)], (8, TOK))
        dnormed = dhidden * gain_row(sec)
        gu = (
            g.astype(F32)
            + inverse
            * (
                dnormed
                - jnp.mean(dnormed, axis=-1, keepdims=True)
                - normed * jnp.mean(dnormed * normed, axis=-1, keepdims=True)
            )
        ).astype(BF)
        for c in range(4):
            part = slice(TOK * c, TOK * (c + 1))
            grads[sec, 1, part] = dot_tn(hidden_ref[sec, :, part], dproj_ref[...]).astype(BF)
            grads[sec, 0, part, 2 * D : 3 * D] = dot_tn(mix_ref[sec, :, part], g).astype(BF)
            term = dot_tn(x[:, part], gu).astype(BF)
            for j in (c // 2, c // 2 + 2):
                grads[sec, 0, TOK * j : TOK * (j + 1), D * (c % 2) : D * (c % 2 + 1)] = term
        return gu

    start(shift[:2])
    merge.begin()
    start(gain_hops + gain_core_hops[:1])
    for copy in own:
        copy.start()
    qkv.begin()
    outw.begin()
    shift[2].start()
    merge.relay()
    qkv.relay()
    for k in range(1, NX):
        gain_hops[k - 1].landed()
        gain_core_hops[k].start()
    merge.pass_on()
    landed(gain_core_hops)
    landed(shift)
    for copy in own:
        copy.wait()
    allowed = masks()
    x0 = x_ref[...]
    merge.ready()
    update0, inverse0 = forward_merge(0, x0)
    outw.relay()
    qkv.pass_on()
    qkv.ready()
    forward_attend(0, allowed)
    outw.pass_on()
    outw.ready()
    y0 = forward_out(0, update0)
    update1, inverse1 = forward_merge(1, y0)
    forward_attend(1, allowed)
    forward_out(1, update1)
    start(home)
    stays.start()
    cot = cot_ref[...]
    backward_attend(1, cot)
    gu1 = backward_terms(1, y0, cot, inverse1)

    @pl.when(s == 0)
    def _():
        swap()

    chain = dot_nt(gu1, wm[1, 0:D]).astype(BF).astype(F32)
    side = dot_nt(gu1, wm[1, D : 2 * D]).astype(BF).astype(F32)
    g0 = (chain + side).astype(BF)

    @pl.when(s == 1)
    def _():
        stage1()

    backward_attend(0, g0)

    @pl.when(s == 1)
    def _():
        stage2()

    backward_terms(0, x0, g0, inverse0)

    @pl.when(s == 1)
    def _():
        swap()
        stage3()

    @pl.when(s == 0)
    def _():
        stage1()
        stage2()
        stage3()

    for which in (0, 1):
        ring_ay.fold(which)
        ring_qx.fold(which)
    ring_ay.finish(y_sum.at[0])
    ring_qx.finish(y_sum.at[1])
    start(z_hops)
    value = y_sum[both, z_rows].astype(F32)
    for k in range(1, NZ):
        z_hops[k - 1].landed()
        value = value + z_in[k].astype(F32)
    z_all[both, z_rows] = value.astype(BF)
    start(z_back)
    landed(gain_z_hops)
    gain_value = gain_z[0]
    for k in range(1, NZ):
        gain_value = gain_value + gain_z[k]
    gain_total[...] = gain_value
    landed(z_back)
    start([last_right, last_left])
    total[both, all_rows, col(y)] = z_all[...]
    last_right.landed()
    end_right.start()
    last_left.landed()
    end_left.start()
    landed(home)
    stays.wait()
    landed([end_right, end_left])
    for hop in net.hops:
        hop.sent()


def vmem(count):
    return [pl.BlockSpec(memory_space=pltpu.VMEM)] * count


def anywhere(count):
    return [pl.BlockSpec(memory_space=pl.ANY)] * count


def shape(dims, dtype=BF):
    return jax.ShapeDtypeStruct(dims, dtype)


def body(fields, cell_mask, merge_weight, qkv_weight, out_weight, norm_gain, out_cotangent):
    x_in = fields.reshape(2, TOK, D)
    g_in = out_cotangent.reshape(2, TOK, D)
    use = cell_mask.reshape(2, 8, 16)
    home, total, gain_total = pl.pallas_call(
        kernel,
        out_shape=(shape((2, TOK, D)), shape((2, TOK, WIDE)), shape((8, TOK), F32)),
        in_specs=anywhere(6) + vmem(1),
        out_specs=vmem(3),
        scratch_shapes=[
            pltpu.VMEM((TOK, D), BF),
            pltpu.VMEM((TOK, D), BF),
            pltpu.VMEM((2, 8, 16), jnp.int32),
            pltpu.VMEM((2, 2 * D, D), BF),
            pltpu.VMEM((2, D, 3 * D), BF),
            pltpu.VMEM((2, D, D), BF),
            pltpu.VMEM((2, 4, 8, TOK), F32),
            pltpu.VMEM((2, TOK, D), BF),
            pltpu.VMEM((2, TOK, D), F32),
            pltpu.VMEM((2, TOK, D), BF),
            pltpu.VMEM((2, TOK, 3 * D), BF),
            pltpu.VMEM((2, HEADS // 2, TOK, 2 * TOK), BF),
            pltpu.VMEM((2, TOK, D), BF),
            pltpu.VMEM((TOK, 3 * D), BF),
            pltpu.VMEM((2, 2, D, WIDE), BF),
            pltpu.VMEM((2, 4, 8, TOK), F32),
            pltpu.VMEM((2, D, WIDE), BF),
            pltpu.VMEM((2, HALF, WIDE), BF),
            pltpu.VMEM((2, TOK, WIDE), BF),
            pltpu.VMEM((2, HALF, PART), BF),
            pltpu.VMEM((2, TOK, PART), BF),
            pltpu.VMEM((2, D // 2, PART), BF),
            pltpu.VMEM((2, D, PART), BF),
            pltpu.VMEM((2, HALF, PART), BF),
            pltpu.VMEM((2, TOK, PART), BF),
            pltpu.VMEM((TOK, WIDE), BF),
            pltpu.VMEM((D, PART), BF),
            pltpu.VMEM((2, TOK, PART), BF),
            pltpu.VMEM((NZ, 2, TALL, PART), BF),
            pltpu.VMEM((2, TOK, PART), BF),
            pltpu.VMEM((4, 8, TOK), F32),
            pltpu.VMEM((4, 8, TOK), F32),
            pltpu.VMEM((4, 8, TOK), F32),
            pltpu.VMEM((NY, 8, TOK), F32),
            pltpu.VMEM((NZ, 8, TOK), F32),
            pltpu.SemaphoreType.DMA((144,)),
            pltpu.SemaphoreType.DMA((144,)),
            pltpu.SemaphoreType.DMA((8,)),
        ],
        compiler_params=pltpu.CompilerParams(
            collective_id=0, has_side_effects=True, vmem_limit_bytes=VMEM_LIMIT
        ),
        name="step",
    )(x_in, g_in, use, merge_weight, qkv_weight, out_weight, norm_gain)
    section_home = home.reshape(1, 1, 2, 8, 16, D)
    merge_grad = jnp.concatenate([total[0, :, :D], total[0, :, D : 2 * D]], axis=0).astype(F32)[None]
    qkv_grad = total[1].astype(F32)[None]
    out_grad = total[0, :, 2 * D :].astype(F32)[None]
    return (section_home, merge_grad, qkv_grad, out_grad, gain_total[0:1])


def solution(mesh):
    return jax.shard_map(
        body,
        mesh=mesh,
        in_specs=(
            P("dp", None, "band", None, None),
            P("dp", None, "band", None),
            P("segment", "dp", None),
            P("segment", "dp", None),
            P("segment", "dp", None),
            P("segment", "dp"),
            P("dp", None, "band", None, None),
        ),
        out_specs=(
            P("segment", "dp", None, "band", None, None),
            P("segment", "dp", None),
            P("segment", "dp", None),
            P("segment", "dp", None),
            P("segment", "dp"),
        ),
        check_vma=False,
    )
```

```python
import jax
import jax.numpy as jnp
from jax import lax
from jax.experimental import pallas as pl
from jax.experimental.pallas import tpu as pltpu
from jax.sharding import PartitionSpec as P

D = 512
HEADS = 8
NX = 4
NY = 4
NZ = 8
TOK = 128
HALF = 64
WIDE = 3 * D
PART = WIDE // NY
TALL = TOK // NZ
EPSILON = 1e-05
MASKED = -1e30
VMEM_LIMIT = 58 * 1024 * 1024
MESH = pl.DeviceIdType.MESH
BF = jnp.bfloat16
F32 = jnp.float32


def dot(left, right):
    return lax.dot_general(left, right, (((1,), (0,)), ((), ())), preferred_element_type=F32)


def dot_nt(left, right):
    return lax.dot_general(left, right, (((1,), (1,)), ((), ())), preferred_element_type=F32)


def dot_tn(left, right):
    return lax.dot_general(left, right, (((0,), (0,)), ((), ())), preferred_element_type=F32)


def span(index, size, unit=None):
    return pl.ds(pl.multiple_of(index, unit or size), size)


class Hop:
    def __init__(self, net, src, dst, device):
        at = net.used
        net.used += 1
        net.hops.append(self)
        self.copy = pltpu.make_async_remote_copy(
            src_ref=src,
            dst_ref=dst,
            send_sem=net.send.at[at],
            recv_sem=net.recv.at[at],
            device_id=device,
            device_id_type=MESH,
        )
        self.start = self.copy.start
        self.landed = self.copy.wait_recv
        self.sent = self.copy.wait_send


class Net:
    def __init__(self, send, recv, local):
        self.send, self.recv, self.local = send, recv, local
        self.used = 0
        self.kept = 0
        self.hops = []

    def hop(self, src, dst, device):
        return Hop(self, src, dst, device)

    def keep(self, src, dst):
        copy = pltpu.make_async_copy(src, dst, self.local.at[self.kept])
        self.kept += 1
        return copy


def start(hops):
    for hop in hops:
        hop.start()


def landed(hops):
    for hop in hops:
        hop.landed()


def add_into(count, dst, terms):
    def one(i, carry):
        at = i * 16
        value = terms[0](at).astype(F32)
        for term in terms[1:]:
            value = value + term(at).astype(F32)
        dst(at, value.astype(BF))
        return carry

    lax.fori_loop(0, count // 16, one, 0)


class Ring:
    def __init__(self, net, buf, rect, me, right, left, one_in, two_in):
        self.buf, self.one_in, self.two_in = buf, one_in, two_in
        step = [lax.rem(me + k, 4) for k in range(4)]
        self.rects = [rect(j) for j in step]
        self.nr = self.rects[0][1]
        far, after, before = self.rects[2], self.rects[1], self.rects[3]
        half = self.nr // 2
        self.one = [
            net.hop(self.view(far, 0, half), one_in.at[0], right),
            net.hop(self.view(far, half, half), one_in.at[1], left),
        ]
        self.two = [
            net.hop(self.view(after, 0, self.nr), two_in.at[0], right),
            net.hop(self.view(before, 0, self.nr), two_in.at[1], left),
        ]

    def index(self, rect, offset, count):
        r0, nr, c0, nc = rect
        first = pl.ds(offset, count) if isinstance(r0, int) else span(r0 + offset, count, 16)
        second = pl.ds(0, nc) if isinstance(c0, int) else span(c0, nc, 128)
        return (first, second)

    def view(self, rect, offset, count):
        return self.buf.at[self.index(rect, offset, count)]

    def rows_of(self, rect, base):
        r0, nr, c0, nc = rect

        def at(i):
            second = pl.ds(0, nc) if isinstance(c0, int) else span(c0, nc, 128)
            return (span(r0 + base + i, 16), second)

        return at

    def fold(self, which):
        self.one[which].landed()
        half = self.nr // 2
        rect, base = (self.rects[1], 0) if which == 0 else (self.rects[3], half)
        at = self.rows_of(rect, base)
        source = self.one_in.at[which]

        def store(i, value):
            self.buf[at(i)] = value

        add_into(half, store, [lambda i: self.buf[at(i)], lambda i: source[span(i, 16)]])
        self.two[which].start()

    def finish(self, dst):
        landed(self.two)
        at = self.rows_of(self.rects[0], 0)

        def store(i, value):
            dst[span(i, 16)] = value

        add_into(
            self.nr,
            store,
            [
                lambda i: self.buf[at(i)],
                lambda i: self.two_in[0, span(i, 16)],
                lambda i: self.two_in[1, span(i, 16)],
            ],
        )


class Direct:
    def __init__(self, net, buf, rect, me, peer, came_in):
        self.buf, self.came_in = buf, came_in
        self.mine = rect(me)
        self.hops = [
            net.hop(buf.at[self.index(rect(lax.rem(me + k, 4)), 0, None)], came_in.at[k - 1], peer(k))
            for k in range(1, 4)
        ]

    def index(self, rect, offset, count):
        r0, nr, c0, nc = rect
        count = count or nr
        first = pl.ds(offset, count) if isinstance(r0, int) and isinstance(offset, int) else span(r0 + offset, count, 16)
        second = pl.ds(0, nc) if isinstance(c0, int) else span(c0, nc, 128)
        return (first, second)

    def begin(self):
        for k in (2, 1, 3):
            self.hops[k - 1].start()

    def finish(self, dst):
        landed(self.hops)

        def store(i, value):
            dst[span(i, 16)] = value

        def term(k):
            return lambda i: self.came_in[k, span(i, 16)]

        add_into(
            self.mine[1],
            store,
            [lambda i: self.buf[self.index(self.mine, i, 16)]] + [term(k) for k in range(3)],
        )


def x_dev(d, step):
    return {"dp": lax.rem(d + step, NX)}


def y_dev(b, step):
    z, y = b // NY, lax.rem(b, NY)
    return {"band": z * NY + lax.rem(y + step, NY)}


def z_dev(b, step):
    z, y = b // NY, lax.rem(b, NY)
    return {"band": lax.rem(z + step, NZ) * NY + y}


def barrier(devices):
    sem = pltpu.get_barrier_semaphore()
    for device in devices:
        pl.semaphore_signal(sem, inc=1, device_id=device, device_id_type=MESH)
    pl.semaphore_wait(sem, len(devices))


def kernel(x_in, g_in, use_in, wm_in, wq_in, wo_in, gain_in,
           y_home, total, gain_total,
           x_ref, cot_ref, use_ref, wm, wq, wo, gain,
           y_ref, normed_ref, hidden_ref, proj_ref, prob_ref, mix_ref, dproj_ref,
           grads, gain_grads, core_in,
           ax_one, ax_two, qy_one, qy_two, ay_in, qx_in, a_sum, q_sum,
           y_sum, z_in,
           gain_core, gain_sum, gain_x, gain_y, gain_z, send, recv, local):
    d = lax.axis_index("dp")
    s = lax.axis_index("segment")
    b = lax.axis_index("band")
    z, y = b // NY, lax.rem(b, NY)
    other = 1 - s
    bands = NY * NZ
    nxt, prev = lax.rem(b + 1, bands), lax.rem(b + bands - 1, bands)
    core = {"segment": other}
    x_right, x_left = x_dev(d, 1), x_dev(d, NX - 1)
    y_right, y_left = y_dev(b, 1), y_dev(b, NY - 1)
    net = Net(send, recv, local)
    lo, hi = pl.ds(0, HALF), pl.ds(HALF, HALF)
    xd = [lax.rem(d + k, NX) for k in range(NX)]
    yd = [lax.rem(y + k, NY) for k in range(NY)]

    barrier(
        [core]
        + [x_dev(d, k) for k in range(1, NX)]
        + [y_dev(b, k) for k in range(1, NY)]
        + [z_dev(b, k) for k in range(1, NZ)]
        + [{"band": nxt}, {"band": prev}]
        + [{"band": nxt, "segment": other}, {"band": prev, "segment": other}]
    )

    shift = [
        net.hop(x_in.at[s, lo], x_ref.at[hi], {"band": prev}),
        net.hop(use_in.at[s], use_ref.at[1], {"band": prev}),
        net.hop(g_in.at[s, lo], cot_ref.at[hi], {"band": prev}),
    ]
    own = [
        net.keep(x_in.at[s, hi], x_ref.at[lo]),
        net.keep(use_in.at[s], use_ref.at[0]),
        net.keep(g_in.at[s, hi], cot_ref.at[lo]),
    ]
    gain[s, d] = jnp.broadcast_to(gain_in[...].astype(F32), (8, TOK))
    gain_hops = [net.hop(gain.at[s, d], gain.at[s, d], x_dev(d, k)) for k in range(1, NX)]
    gain_core_hops = [net.hop(gain.at[s, xd[0]], gain.at[s, xd[0]], core)] + [
        net.hop(gain.at[s, xd[NX - k]], gain.at[s, xd[NX - k]], core) for k in range(1, NX)
    ]

    class Gather:
        def __init__(self, src, dst, size):
            wide = dst.shape[-1]
            cols = span(y * (wide // NY), wide // NY)
            half, quarter = size // 2, size // 4

            def block(owner, offset, count):
                return dst.at[s, span(owner * size + offset, count, count)]

            def strip(owner):
                return dst.at[s, span(owner * size + half, half), cols]

            top, bottom = pl.ds(0, half), pl.ds(half, half)
            self.strips = [net.hop(src.at[0, bottom, cols], strip(d), x_dev(d, k)) for k in range(1, NX)]
            self.right = net.hop(src.at[0, top], block(d, 0, half), x_right)
            self.left = net.hop(src.at[0, top], block(d, 0, half), x_left)
            self.mine = net.hop(src.at[0], block(d, 0, size), core)
            self.local = net.keep(src.at[0], block(d, 0, size))
            self.spread = [
                [net.hop(strip(xd[NX - k]), strip(xd[NX - k]), y_dev(b, m)) for m in range(1, NY)]
                for k in range(1, NX)
            ]
            self.far_right = net.hop(block(xd[3], 0, quarter), block(xd[3], 0, quarter), x_right)
            self.far_left = net.hop(block(xd[1], quarter, quarter), block(xd[1], quarter, quarter), x_left)
            self.across = [
                net.hop(block(xd[NX - k], 0, size), block(xd[NX - k], 0, size), core)
                for k in range(1, NX)
            ]

        def begin(self):
            start([self.right, self.left, self.mine])
            self.local.start()

        def relay_strips(self):
            for k in (1, 3, 2):
                self.strips[k - 1].landed()
                start(self.spread[k - 1])

        def relay(self):
            self.right.landed()
            self.far_right.start()
            self.left.landed()
            self.far_left.start()

        def pass_on(self):
            for k in (1, 3):
                landed(self.spread[k - 1])
                self.across[k - 1].start()
            landed(self.spread[1])
            landed([self.far_right, self.far_left])
            self.across[1].start()

        def ready(self):
            landed([self.mine] + self.across)
            self.local.wait()

    merge = Gather(wm_in, wm, 2 * TOK)
    qkv = Gather(wq_in, wq, TOK)
    outw = Gather(wo_in, wo, TOK)

    mine = grads.at[s]
    theirs = grads.at[other]
    a_order = [xd[k] for k in (2, 1, 3, 0)]
    q_order = [yd[k] for k in (2, 1, 3, 0)]

    def a_rows(j):
        return (0, span(j * TOK, TOK))

    def q_cols(j):
        return (1, pl.ds(0, D), span(j * PART, PART, 128))

    swap_a = [net.hop(theirs.at[a_rows(j)], core_in.at[a_rows(j)], core) for j in a_order]
    swap_q = [net.hop(theirs.at[q_cols(j)], core_in.at[q_cols(j)], core) for j in q_order]
    gain_swap = net.hop(gain_grads.at[other], gain_core, core)
    ring_ax = Ring(net, mine.at[0], lambda j: (j * TOK, TOK, 0, WIDE), d, x_right, x_left, ax_one, ax_two)
    ring_qy = Ring(net, mine.at[1], lambda j: (0, D, j * PART, PART), y, y_right, y_left, qy_one, qy_two)
    to_ay = Direct(net, a_sum, lambda j: (0, TOK, j * PART, PART), y, lambda k: y_dev(b, k), ay_in)
    to_qx = Direct(net, q_sum, lambda j: (j * TOK, TOK, 0, PART), d, lambda k: x_dev(d, k), qx_in)
    gain_x_hops = [net.hop(gain_sum.at[xd[k]], gain_x.at[k], x_dev(d, k)) for k in range(1, NX)]
    gain_y_hops = [net.hop(gain_y.at[0], gain_y.at[k], y_dev(b, k)) for k in range(1, NY)]
    gain_z_hops = [net.hop(gain_z.at[0], gain_z.at[k], z_dev(b, k)) for k in range(1, NZ)]
    z_rows = span(z * TALL, TALL)
    both = pl.ds(0, 2)
    z_hops = [
        net.hop(
            y_sum.at[both, span(lax.rem(z + k, NZ) * TALL, TALL)], z_in.at[k], z_dev(b, k)
        )
        for k in range(1, NZ)
    ]
    def piece(k):
        at = (both, span(lax.rem(z + NZ - k, NZ) * TALL, TALL), span(y * PART, PART, 128))
        return total.at[at]

    z_back = [net.hop(piece(0), piece(0), z_dev(b, k)) for k in range(1, NZ)]
    y_back = [[net.hop(piece(k), piece(k), y_dev(b, m)) for m in range(1, NY)] for k in range(NZ)]
    home = [
        net.hop(y_ref.at[other, lo], y_home.at[s, hi], core),
        net.hop(y_ref.at[s, hi], y_home.at[s, lo], {"band": nxt}),
        net.hop(y_ref.at[other, hi], y_home.at[s, lo], {"band": nxt, "segment": other}),
    ]
    stays = net.keep(y_ref.at[s, lo], y_home.at[s, hi])

    def a_core(i):
        swap_a[i].landed()
        base = a_order[i] * TOK

        def at(r):
            return (0, span(base + r, 16))

        def store(r, value):
            mine[at(r)] = value

        add_into(TOK, store, [lambda r: mine[at(r)], lambda r: core_in[at(r)]])

    def q_core(i):
        swap_q[i].landed()
        cols = span(q_order[i] * PART, PART, 128)

        def at(r):
            return (1, span(r, 16), cols)

        def store(r, value):
            mine[at(r)] = value

        add_into(D, store, [lambda r: mine[at(r)], lambda r: core_in[at(r)]])

    def swap():
        for hop_a, hop_q in zip(swap_a, swap_q):
            hop_a.start()
            hop_q.start()
        gain_swap.start()

    def stage1():
        a_core(0)
        start(ring_ax.one)
        q_core(0)
        start(ring_qy.one)
        for i in (1, 2):
            a_core(i)
            q_core(i)
        gain_swap.landed()
        gain_sum[...] = gain_grads[s] + gain_core[...]
        gain_x[0] = gain_sum[d]
        start(gain_x_hops)

    def stage2():
        for which in (0, 1):
            ring_ax.fold(which)
            ring_qy.fold(which)
        a_core(3)
        q_core(3)
        landed(gain_x_hops)
        gain_y[0] = (gain_x[0] + gain_x[1]) + (gain_x[2] + gain_x[3])
        start(gain_y_hops)

    def stage3():
        ring_ax.finish(a_sum)
        to_ay.begin()
        ring_qy.finish(q_sum)
        to_qx.begin()
        landed(gain_y_hops)
        gain_z[0] = (gain_y[0] + gain_y[1]) + (gain_y[2] + gain_y[3])
        start(gain_z_hops)

    def masks():
        lane = lax.broadcasted_iota(jnp.int32, (16, TOK), 1)
        sub = lax.broadcasted_iota(jnp.int32, (16, TOK), 0)
        spread = (lane % 16 == sub).astype(F32).astype(BF)
        lane8 = lax.broadcasted_iota(jnp.int32, (8, TOK), 1) // 16
        sub8 = lax.broadcasted_iota(jnp.int32, (8, TOK), 0)
        here = dot((use_ref[0] == 1).astype(F32).astype(BF), spread)
        there = dot((use_ref[1] == 1).astype(F32).astype(BF), spread)
        usable = jnp.sum(
            jnp.where(lane8 + 4 == sub8, here, 0.0) + jnp.where(lane8 - 4 == sub8, there, 0.0),
            axis=0, keepdims=True,
        )
        query = lax.broadcasted_iota(jnp.int32, (TOK, TOK), 0)
        key = lax.broadcasted_iota(jnp.int32, (TOK, TOK), 1)
        same_lon = (query % 16 // 8) == (key % 16 // 8)
        same_lat = ((query // HALF) == (key // HALF)) | jnp.logical_not(b == bands - 1)
        open_key = jnp.broadcast_to(usable, (TOK, TOK)) > 0.5
        return same_lon & same_lat & (open_key | (query == key))

    first = lax.broadcasted_iota(jnp.int32, (TOK, TOK), 1) < HALF
    zero = jnp.zeros((TOK, TOK), F32)
    head0 = jnp.where(first, zero + 1.0, zero).astype(BF)
    head1 = jnp.where(first, zero, zero + 1.0).astype(BF)

    def pair_cat(values):
        return jnp.concatenate([values * head0, values * head1], axis=0)

    def gain_row(sec):
        return jnp.concatenate([gain[sec, j][0:1] for j in range(4)], axis=1)

    def tile(sec, which, i):
        return proj_ref[sec, :, which * D + TOK * i : which * D + TOK * (i + 1)]

    def forward_merge(sec, x):
        update = dot(x, wm[sec, 0:D]) + dot(x, wm[sec, D : 2 * D])
        average = jnp.mean(update, axis=-1, keepdims=True)
        centered = update - average
        spread = jnp.mean(centered * centered, axis=-1, keepdims=True)
        inverse = lax.rsqrt(spread + EPSILON)
        normed = centered * inverse
        normed_ref[sec] = normed
        hidden_ref[sec] = (normed * gain_row(sec)).astype(BF)
        return update, inverse

    def forward_attend(sec, allowed):
        proj_ref[sec] = dot(hidden_ref[sec], wq[sec]).astype(BF)
        for i in range(HEADS // 2):
            scores = dot_nt(tile(sec, 0, i), pair_cat(tile(sec, 1, i))) * 0.125
            probs = []
            for h in range(2):
                one = jnp.where(allowed, scores[:, TOK * h : TOK * (h + 1)], MASKED)
                weights = jnp.exp(one - jnp.max(one, axis=-1, keepdims=True))
                probs.append(weights / jnp.sum(weights, axis=-1, keepdims=True))
            prob = jnp.concatenate(probs, axis=1).astype(BF)
            prob_ref[sec, i] = prob
            mix_ref[sec, :, TOK * i : TOK * (i + 1)] = dot(prob, pair_cat(tile(sec, 2, i))).astype(BF)

    def forward_out(sec, update):
        result = (update + dot(mix_ref[sec], wo[sec])).astype(BF)
        y_ref[sec] = result
        return result

    def backward_attend(sec, g):
        gm = dot_nt(g, wo[sec]).astype(BF)
        for i in range(HEADS // 2):
            q, k, v = tile(sec, 0, i), tile(sec, 1, i), tile(sec, 2, i)
            gm_pair = gm[:, TOK * i : TOK * (i + 1)]
            prob = prob_ref[sec, i]
            dprob = dot_nt(gm_pair, pair_cat(v))
            pieces = []
            for h in range(2):
                half = slice(TOK * h, TOK * (h + 1))
                p = prob[:, half].astype(F32)
                dp = dprob[:, half]
                pieces.append(p * (dp - jnp.sum(dp * p, axis=-1, keepdims=True)) * 0.125)
            dscore = jnp.concatenate(pieces, axis=1).astype(BF)
            dk = dot_tn(dscore, q)
            dv = dot_tn(prob, gm_pair)
            dproj_ref[:, TOK * i : TOK * (i + 1)] = dot(dscore, pair_cat(k)).astype(BF)
            dproj_ref[:, D + TOK * i : D + TOK * (i + 1)] = jnp.where(first, dk[:TOK], dk[TOK:]).astype(BF)
            dproj_ref[:, 2 * D + TOK * i : 2 * D + TOK * (i + 1)] = jnp.where(first, dv[:TOK], dv[TOK:]).astype(BF)

    def backward_terms(sec, x, g, inverse):
        dhidden = dot_nt(dproj_ref[...], wq[sec])
        normed = normed_ref[sec]
        dgain = jnp.sum(dhidden * normed, axis=0, keepdims=True)
        for j in range(4):
            gain_grads[sec, j] = jnp.broadcast_to(dgain[:, TOK * j : TOK * (j + 1)], (8, TOK))
        dnormed = dhidden * gain_row(sec)
        gu = (
            g.astype(F32)
            + inverse
            * (
                dnormed
                - jnp.mean(dnormed, axis=-1, keepdims=True)
                - normed * jnp.mean(dnormed * normed, axis=-1, keepdims=True)
            )
        ).astype(BF)
        for c in range(4):
            part = slice(TOK * c, TOK * (c + 1))
            grads[sec, 1, part] = dot_tn(hidden_ref[sec, :, part], dproj_ref[...]).astype(BF)
            grads[sec, 0, part, 2 * D : 3 * D] = dot_tn(mix_ref[sec, :, part], g).astype(BF)
            term = dot_tn(x[:, part], gu).astype(BF)
            for j in (c // 2, c // 2 + 2):
                grads[sec, 0, TOK * j : TOK * (j + 1), D * (c % 2) : D * (c % 2 + 1)] = term
        return gu

    for part in (merge, qkv, outw):
        start(part.strips)
    start(shift[:2])
    merge.begin()
    start(gain_hops + gain_core_hops[:1])
    for copy in own:
        copy.start()
    qkv.begin()
    outw.begin()
    shift[2].start()
    for part in (merge, qkv, outw):
        part.relay_strips()
    merge.relay()
    qkv.relay()
    for k in range(1, NX):
        gain_hops[k - 1].landed()
        gain_core_hops[k].start()
    merge.pass_on()
    landed(gain_core_hops)
    landed(shift)
    for copy in own:
        copy.wait()
    allowed = masks()
    x0 = x_ref[...]
    merge.ready()
    update0, inverse0 = forward_merge(0, x0)
    outw.relay()
    qkv.pass_on()
    qkv.ready()
    forward_attend(0, allowed)
    outw.pass_on()
    outw.ready()
    y0 = forward_out(0, update0)
    update1, inverse1 = forward_merge(1, y0)
    forward_attend(1, allowed)
    forward_out(1, update1)
    start(home)
    stays.start()
    cot = cot_ref[...]
    backward_attend(1, cot)
    gu1 = backward_terms(1, y0, cot, inverse1)

    @pl.when(s == 0)
    def _():
        swap()

    chain = dot_nt(gu1, wm[1, 0:D]).astype(BF).astype(F32)
    side = dot_nt(gu1, wm[1, D : 2 * D]).astype(BF).astype(F32)
    g0 = (chain + side).astype(BF)

    @pl.when(s == 1)
    def _():
        stage1()

    backward_attend(0, g0)

    backward_terms(0, x0, g0, inverse0)

    @pl.when(s == 1)
    def _():
        swap()
        stage2()
        stage3()

    @pl.when(s == 0)
    def _():
        stage1()
        stage2()
        stage3()

    to_ay.finish(y_sum.at[0])
    to_qx.finish(y_sum.at[1])
    start(z_hops)
    value = y_sum[both, z_rows].astype(F32)
    for k in range(1, NZ):
        z_hops[k - 1].landed()
        value = value + z_in[k].astype(F32)
    total[both, z_rows, span(y * PART, PART, 128)] = value.astype(BF)
    start(z_back)
    start(y_back[0])
    landed(gain_z_hops)
    gain_value = gain_z[0]
    for k in range(1, NZ):
        gain_value = gain_value + gain_z[k]
    gain_total[...] = gain_value
    for k in (1, 7, 2, 6, 3, 5, 4):
        if k < NZ:
            z_back[k - 1].landed()
            start(y_back[k])
    landed(home)
    stays.wait()
    for hops in y_back:
        landed(hops)
    for hop in net.hops:
        hop.sent()


def widen(home_in, total, gain_in, home, merge, qkv, out, gain):
    home[...] = home_in[...]
    merge[0:TOK] = total[0, :, 0:D].astype(F32)
    merge[TOK : 2 * TOK] = total[0, :, D : 2 * D].astype(F32)
    out[...] = total[0, :, 2 * D : 3 * D].astype(F32)
    qkv[...] = total[1].astype(F32)
    gain[...] = gain_in[0:1]


def vmem(count):
    return [pl.BlockSpec(memory_space=pltpu.VMEM)] * count


def anywhere(count):
    return [pl.BlockSpec(memory_space=pl.ANY)] * count


def shape(dims, dtype=BF):
    return jax.ShapeDtypeStruct(dims, dtype)


def body(fields, cell_mask, merge_weight, qkv_weight, out_weight, norm_gain, out_cotangent):
    x_in = fields.reshape(2, TOK, D)
    g_in = out_cotangent.reshape(2, TOK, D)
    use = cell_mask.reshape(2, 8, 16)
    home, total, gain_total = pl.pallas_call(
        kernel,
        out_shape=(shape((2, TOK, D)), shape((2, TOK, WIDE)), shape((8, TOK), F32)),
        in_specs=anywhere(6) + vmem(1),
        out_specs=vmem(3),
        scratch_shapes=[
            pltpu.VMEM((TOK, D), BF),
            pltpu.VMEM((TOK, D), BF),
            pltpu.VMEM((2, 8, 16), jnp.int32),
            pltpu.VMEM((2, 2 * D, D), BF),
            pltpu.VMEM((2, D, 3 * D), BF),
            pltpu.VMEM((2, D, D), BF),
            pltpu.VMEM((2, 4, 8, TOK), F32),
            pltpu.VMEM((2, TOK, D), BF),
            pltpu.VMEM((2, TOK, D), F32),
            pltpu.VMEM((2, TOK, D), BF),
            pltpu.VMEM((2, TOK, 3 * D), BF),
            pltpu.VMEM((2, HEADS // 2, TOK, 2 * TOK), BF),
            pltpu.VMEM((2, TOK, D), BF),
            pltpu.VMEM((TOK, 3 * D), BF),
            pltpu.VMEM((2, 2, D, WIDE), BF),
            pltpu.VMEM((2, 4, 8, TOK), F32),
            pltpu.VMEM((2, D, WIDE), BF),
            pltpu.VMEM((2, HALF, WIDE), BF),
            pltpu.VMEM((2, TOK, WIDE), BF),
            pltpu.VMEM((2, D // 2, PART), BF),
            pltpu.VMEM((2, D, PART), BF),
            pltpu.VMEM((3, TOK, PART), BF),
            pltpu.VMEM((3, TOK, PART), BF),
            pltpu.VMEM((TOK, WIDE), BF),
            pltpu.VMEM((D, PART), BF),
            pltpu.VMEM((2, TOK, PART), BF),
            pltpu.VMEM((NZ, 2, TALL, PART), BF),
            pltpu.VMEM((4, 8, TOK), F32),
            pltpu.VMEM((4, 8, TOK), F32),
            pltpu.VMEM((4, 8, TOK), F32),
            pltpu.VMEM((NY, 8, TOK), F32),
            pltpu.VMEM((NZ, 8, TOK), F32),
            pltpu.SemaphoreType.DMA((176,)),
            pltpu.SemaphoreType.DMA((176,)),
            pltpu.SemaphoreType.DMA((8,)),
        ],
        compiler_params=pltpu.CompilerParams(
            collective_id=0, has_side_effects=True, vmem_limit_bytes=VMEM_LIMIT
        ),
        name="step",
    )(x_in, g_in, use, merge_weight, qkv_weight, out_weight, norm_gain)
    home, merge_grad, qkv_grad, out_grad, gain_grad = pl.pallas_call(
        widen,
        out_shape=(
            shape((2, TOK, D)), shape((2 * TOK, D), F32), shape((TOK, 3 * D), F32),
            shape((TOK, D), F32), shape((1, TOK), F32),
        ),
        in_specs=vmem(3),
        out_specs=vmem(5),
        compiler_params=pltpu.CompilerParams(vmem_limit_bytes=16 * 1024 * 1024),
        name="widen",
    )(home, total, gain_total)
    section_home = home.reshape(1, 1, 2, 8, 16, D)
    return (section_home, merge_grad[None], qkv_grad[None], out_grad[None], gain_grad)


def solution(mesh):
    return jax.shard_map(
        body,
        mesh=mesh,
        in_specs=(
            P("dp", None, "band", None, None),
            P("dp", None, "band", None),
            P("segment", "dp", None),
            P("segment", "dp", None),
            P("segment", "dp", None),
            P("segment", "dp"),
            P("dp", None, "band", None, None),
        ),
        out_specs=(
            P("segment", "dp", None, "band", None, None),
            P("segment", "dp", None),
            P("segment", "dp", None),
            P("segment", "dp", None),
            P("segment", "dp"),
        ),
        check_vma=False,
    )
```

```python
import jax
import jax.numpy as jnp
from jax import lax
from jax.experimental import pallas as pl
from jax.experimental.pallas import tpu as pltpu
from jax.sharding import PartitionSpec as P

D = 512
HEADS = 8
NX = 4
NY = 4
NZ = 8
TOK = 128
HALF = 64
WIDE = 3 * D
PART = WIDE // NY
TALL = TOK // NZ
EPSILON = 1e-05
MASKED = -1e30
VMEM_LIMIT = 58 * 1024 * 1024
MESH = pl.DeviceIdType.MESH
BF = jnp.bfloat16
F32 = jnp.float32


def dot(left, right):
    return lax.dot_general(left, right, (((1,), (0,)), ((), ())), preferred_element_type=F32)


def dot_nt(left, right):
    return lax.dot_general(left, right, (((1,), (1,)), ((), ())), preferred_element_type=F32)


def dot_tn(left, right):
    return lax.dot_general(left, right, (((0,), (0,)), ((), ())), preferred_element_type=F32)


def span(index, size, unit=None):
    return pl.ds(pl.multiple_of(index, unit or size), size)


class Hop:
    def __init__(self, net, src, dst, device):
        at = net.used
        net.used += 1
        net.hops.append(self)
        self.copy = pltpu.make_async_remote_copy(
            src_ref=src,
            dst_ref=dst,
            send_sem=net.send.at[at],
            recv_sem=net.recv.at[at],
            device_id=device,
            device_id_type=MESH,
        )
        self.start = self.copy.start
        self.landed = self.copy.wait_recv
        self.sent = self.copy.wait_send


class Net:
    def __init__(self, send, recv, local):
        self.send, self.recv, self.local = send, recv, local
        self.used = 0
        self.kept = 0
        self.hops = []

    def hop(self, src, dst, device):
        return Hop(self, src, dst, device)

    def keep(self, src, dst):
        copy = pltpu.make_async_copy(src, dst, self.local.at[self.kept])
        self.kept += 1
        return copy


def start(hops):
    for hop in hops:
        hop.start()


def landed(hops):
    for hop in hops:
        hop.landed()


def add_into(count, step, dst, terms):
    def one(i, carry):
        at = i * step
        if len(terms) == 2:
            dst(at, terms[0](at) + terms[1](at))
        else:
            value = terms[0](at).astype(F32)
            for term in terms[1:]:
                value = value + term(at).astype(F32)
            dst(at, value.astype(BF))
        return carry

    lax.fori_loop(0, count // step, one, 0)


def block_rows(count, wide):
    return min(count, 49152 // wide // 16 * 16)


class Ring:
    def __init__(self, net, buf, rect, me, right, left, one_in, two_in):
        self.buf, self.one_in, self.two_in = buf, one_in, two_in
        step = [lax.rem(me + k, 4) for k in range(4)]
        self.rects = [rect(j) for j in step]
        self.nr, self.nc = self.rects[0][1], self.rects[0][3]
        far, after, before = self.rects[2], self.rects[1], self.rects[3]
        half = self.nr // 2
        top, bottom = pl.ds(0, half), pl.ds(half, half)
        self.one = [
            net.hop(self.view(far, 0, half), one_in.at[0], right),
            net.hop(self.view(far, half, half), one_in.at[1], left),
        ]
        self.plain = [
            net.hop(self.view(after, half, half), two_in.at[0, bottom], right),
            net.hop(self.view(before, 0, half), two_in.at[1, top], left),
        ]
        self.two = [
            net.hop(self.view(after, 0, half), two_in.at[0, top], right),
            net.hop(self.view(before, half, half), two_in.at[1, bottom], left),
        ]

    def at(self, rect, offset, count):
        r0, nr, c0, nc = rect
        first = pl.ds(offset, count) if isinstance(r0, int) and isinstance(offset, int) else span(r0 + offset, count, 16)
        second = pl.ds(0, nc) if isinstance(c0, int) else span(c0, nc, 128)
        return (first, second)

    def view(self, rect, offset, count):
        return self.buf.at[self.at(rect, offset, count)]

    def fold(self, which):
        self.one[which].landed()
        half = self.nr // 2
        rect, base = (self.rects[1], 0) if which == 0 else (self.rects[3], half)
        step = block_rows(half, self.nc)

        def store(i, value):
            self.buf[self.at(rect, base + i, step)] = value

        add_into(
            half,
            step,
            store,
            [lambda i: self.buf[self.at(rect, base + i, step)], lambda i: self.one_in[which, span(i, step, 16)]],
        )
        self.two[which].start()

    def finish(self, dst):
        landed(self.plain + self.two)
        step = block_rows(self.nr, self.nc)

        def store(i, value):
            dst[span(i, step, 16)] = value

        add_into(
            self.nr,
            step,
            store,
            [
                lambda i: self.buf[self.at(self.rects[0], i, step)],
                lambda i: self.two_in[0, span(i, step, 16)],
                lambda i: self.two_in[1, span(i, step, 16)],
            ],
        )


class Direct:
    def __init__(self, net, buf, rect, me, peer, came_in):
        self.buf, self.came_in = buf, came_in
        self.mine = rect(me)
        self.hops = [
            net.hop(buf.at[self.index(rect(lax.rem(me + k, 4)), 0, None)], came_in.at[k - 1], peer(k))
            for k in range(1, 4)
        ]

    def index(self, rect, offset, count):
        r0, nr, c0, nc = rect
        count = count or nr
        first = pl.ds(offset, count) if isinstance(r0, int) and isinstance(offset, int) else span(r0 + offset, count, 16)
        second = pl.ds(0, nc) if isinstance(c0, int) else span(c0, nc, 128)
        return (first, second)

    def begin(self):
        for k in (2, 1, 3):
            self.hops[k - 1].start()

    def finish(self, dst):
        landed(self.hops)
        step = block_rows(self.mine[1], self.mine[3])

        def store(i, value):
            dst[span(i, step, 16)] = value

        def term(k):
            return lambda i: self.came_in[k, span(i, step, 16)]

        add_into(
            self.mine[1],
            step,
            store,
            [lambda i: self.buf[self.index(self.mine, i, step)]] + [term(k) for k in range(3)],
        )


def x_dev(d, step):
    return {"dp": lax.rem(d + step, NX)}


def y_dev(b, step):
    z, y = b // NY, lax.rem(b, NY)
    return {"band": z * NY + lax.rem(y + step, NY)}


def z_dev(b, step):
    z, y = b // NY, lax.rem(b, NY)
    return {"band": lax.rem(z + step, NZ) * NY + y}


def z_near(b, step):
    z, y = b // NY, lax.rem(b, NY)
    return {"band": (z // 4 * 4 + lax.rem(lax.rem(z, 4) + step, 4)) * NY + y}


def barrier(devices):
    sem = pltpu.get_barrier_semaphore()
    for device in devices:
        pl.semaphore_signal(sem, inc=1, device_id=device, device_id_type=MESH)
    pl.semaphore_wait(sem, len(devices))


def kernel(x_in, g_in, use_in, wm_in, wq_in, wo_in, gain_in,
           y_home, total, gain_total,
           x_ref, cot_ref, use_ref, wm, wq, wo, gain,
           y_ref, normed_ref, hidden_ref, proj_ref, prob_ref, mix_ref, dproj_ref,
           grads, gain_grads, core_in,
           ax_one, ax_two, qy_one, qy_two, ay_in, qx_in, a_sum, q_sum,
           y_sum, z_in,
           gain_core, gain_sum, gain_x, gain_y, gain_z, send, recv, local):
    d = lax.axis_index("dp")
    s = lax.axis_index("segment")
    b = lax.axis_index("band")
    z, y = b // NY, lax.rem(b, NY)
    other = 1 - s
    bands = NY * NZ
    nxt, prev = lax.rem(b + 1, bands), lax.rem(b + bands - 1, bands)
    core = {"segment": other}
    x_right, x_left = x_dev(d, 1), x_dev(d, NX - 1)
    y_right, y_left = y_dev(b, 1), y_dev(b, NY - 1)
    net = Net(send, recv, local)
    lo, hi = pl.ds(0, HALF), pl.ds(HALF, HALF)
    xd = [lax.rem(d + k, NX) for k in range(NX)]
    yd = [lax.rem(y + k, NY) for k in range(NY)]

    barrier(
        [core]
        + [x_dev(d, k) for k in range(1, NX)]
        + [y_dev(b, k) for k in range(1, NY)]
        + [z_dev(b, k) for k in range(1, NZ)]
        + [{"band": nxt}, {"band": prev}]
        + [{"band": nxt, "segment": other}, {"band": prev, "segment": other}]
    )

    shift = [
        net.hop(x_in.at[s, lo], x_ref.at[hi], {"band": prev}),
        net.hop(use_in.at[s], use_ref.at[1], {"band": prev}),
        net.hop(g_in.at[s, lo], cot_ref.at[hi], {"band": prev}),
    ]
    own = [
        net.keep(x_in.at[s, hi], x_ref.at[lo]),
        net.keep(use_in.at[s], use_ref.at[0]),
        net.keep(g_in.at[s, hi], cot_ref.at[lo]),
    ]
    gain[s, d] = jnp.broadcast_to(gain_in[...].astype(F32), (8, TOK))
    gain_hops = [net.hop(gain.at[s, d], gain.at[s, d], x_dev(d, k)) for k in range(1, NX)]
    gain_core_hops = [net.hop(gain.at[s, xd[0]], gain.at[s, xd[0]], core)] + [
        net.hop(gain.at[s, xd[NX - k]], gain.at[s, xd[NX - k]], core) for k in range(1, NX)
    ]

    class Gather:
        def __init__(self, src, dst, size):
            wide = dst.shape[-1] // 4
            half, quarter, eighth = size // 2, size // 4, size // 8

            def block(owner, offset, count):
                return dst.at[s, span(owner * size + offset, count, count)]

            def y_strip(owner):
                return dst.at[s, span(owner * size + quarter, half, quarter), span(y * wide, wide)]

            def z_strip(owner):
                return dst.at[
                    s, span(owner * size + 3 * quarter, quarter), span(lax.rem(z, 4) * wide, wide)
                ]

            top = pl.ds(0, quarter)
            y_src = src.at[0, pl.ds(quarter, half), span(y * wide, wide)]
            z_src = src.at[0, pl.ds(3 * quarter, quarter), span(lax.rem(z, 4) * wide, wide)]
            self.y_strips = [net.hop(y_src, y_strip(d), x_dev(d, k)) for k in range(1, NX)]
            self.z_strips = [net.hop(z_src, z_strip(d), x_dev(d, k)) for k in range(1, NX)]
            self.right = net.hop(src.at[0, top], block(d, 0, quarter), x_right)
            self.left = net.hop(src.at[0, top], block(d, 0, quarter), x_left)
            self.mine = net.hop(src.at[0], block(d, 0, size), core)
            self.local = net.keep(src.at[0], block(d, 0, size))
            owners = [xd[NX - k] for k in range(1, NX)]
            self.y_spread = [
                [net.hop(y_strip(o), y_strip(o), y_dev(b, m)) for m in range(1, NY)] for o in owners
            ]
            self.z_spread = [
                [net.hop(z_strip(o), z_strip(o), z_near(b, m)) for m in range(1, 4)] for o in owners
            ]
            self.far_right = net.hop(block(xd[3], 0, eighth), block(xd[3], 0, eighth), x_right)
            self.far_left = net.hop(block(xd[1], eighth, eighth), block(xd[1], eighth, eighth), x_left)
            self.across = [net.hop(block(o, 0, size), block(o, 0, size), core) for o in owners]

        def begin_strips(self):
            for k in (2, 1, 3):
                self.y_strips[k - 1].start()
                self.z_strips[k - 1].start()

        def begin_blocks(self):
            start([self.right, self.left, self.mine])
            self.local.start()

        def relay_strips(self):
            for k in (1, 3, 2):
                self.y_strips[k - 1].landed()
                start(self.y_spread[k - 1])
                self.z_strips[k - 1].landed()
                start(self.z_spread[k - 1])

        def relay(self):
            self.right.landed()
            self.far_right.start()
            self.left.landed()
            self.far_left.start()

        def pass_on(self):
            for k in (1, 3, 2):
                landed(self.y_spread[k - 1])
                landed(self.z_spread[k - 1])
                if k == 2:
                    landed([self.far_right, self.far_left])
                self.across[k - 1].start()

        def ready(self):
            landed([self.mine] + self.across)
            self.local.wait()

    merge = Gather(wm_in, wm, 2 * TOK)
    qkv = Gather(wq_in, wq, TOK)
    outw = Gather(wo_in, wo, TOK)

    mine = grads.at[s]
    theirs = grads.at[other]
    a_order = [xd[k] for k in (2, 1, 3, 0)]
    q_order = [yd[k] for k in (2, 1, 3, 0)]

    def a_rows(j):
        return (0, span(j * TOK, TOK))

    def q_cols(j):
        return (1, pl.ds(0, D), span(j * PART, PART, 128))

    swap_a = [net.hop(theirs.at[a_rows(j)], core_in.at[a_rows(j)], core) for j in a_order]
    swap_q = [net.hop(theirs.at[q_cols(j)], core_in.at[q_cols(j)], core) for j in q_order]
    gain_swap = net.hop(gain_grads.at[other], gain_core, core)
    ring_ax = Ring(net, mine.at[0], lambda j: (j * TOK, TOK, 0, WIDE), d, x_right, x_left, ax_one, ax_two)
    ring_qy = Ring(net, mine.at[1], lambda j: (0, D, j * PART, PART), y, y_right, y_left, qy_one, qy_two)
    to_ay = Direct(net, a_sum, lambda j: (0, TOK, j * PART, PART), y, lambda k: y_dev(b, k), ay_in)
    to_qx = Direct(net, q_sum, lambda j: (j * TOK, TOK, 0, PART), d, lambda k: x_dev(d, k), qx_in)
    gain_x_hops = [net.hop(gain_sum.at[xd[k]], gain_x.at[k], x_dev(d, k)) for k in range(1, NX)]
    gain_y_hops = [net.hop(gain_y.at[0], gain_y.at[k], y_dev(b, k)) for k in range(1, NY)]
    gain_z_hops = [net.hop(gain_z.at[0], gain_z.at[k], z_dev(b, k)) for k in range(1, NZ)]
    z_rows = span(z * TALL, TALL)
    both = pl.ds(0, 2)
    z_hops = [
        net.hop(
            y_sum.at[both, span(lax.rem(z + k, NZ) * TALL, TALL)], z_in.at[k], z_dev(b, k)
        )
        for k in range(1, NZ)
    ]
    def piece(k):
        at = (both, span(lax.rem(z + NZ - k, NZ) * TALL, TALL), span(y * PART, PART, 128))
        return total.at[at]

    z_back = [net.hop(piece(0), piece(0), z_dev(b, k)) for k in range(1, NZ)]
    y_back = [[net.hop(piece(k), piece(k), y_dev(b, m)) for m in range(1, NY)] for k in range(NZ)]
    home = [
        net.hop(y_ref.at[other, lo], y_home.at[s, hi], core),
        net.hop(y_ref.at[s, hi], y_home.at[s, lo], {"band": nxt}),
        net.hop(y_ref.at[other, hi], y_home.at[s, lo], {"band": nxt, "segment": other}),
    ]
    stays = net.keep(y_ref.at[s, lo], y_home.at[s, hi])

    def core_sum(where, count, wide):
        step = block_rows(count, wide)

        def store(r, value):
            mine[where(r, step)] = value

        add_into(
            count, step, store, [lambda r: mine[where(r, step)], lambda r: core_in[where(r, step)]]
        )

    def a_core(i):
        swap_a[i].landed()
        core_sum(lambda r, step: (0, span(a_order[i] * TOK + r, step, 16)), TOK, WIDE)

    def q_core(i):
        swap_q[i].landed()
        core_sum(lambda r, step: (1, span(r, step, 16), span(q_order[i] * PART, PART, 128)), D, PART)

    def swap():
        for hop_a, hop_q in zip(swap_a, swap_q):
            hop_a.start()
            hop_q.start()
        gain_swap.start()

    def stage1():
        a_core(0)
        start(ring_ax.one)
        q_core(0)
        start(ring_qy.one)
        for i in (1, 2):
            a_core(i)
            ring_ax.plain[i - 1].start()
            q_core(i)
            ring_qy.plain[i - 1].start()
        gain_swap.landed()
        gain_sum[...] = gain_grads[s] + gain_core[...]
        gain_x[0] = gain_sum[d]
        start(gain_x_hops)

    def stage2():
        for which in (0, 1):
            ring_ax.fold(which)
            ring_qy.fold(which)
        a_core(3)
        q_core(3)
        landed(gain_x_hops)
        gain_y[0] = (gain_x[0] + gain_x[1]) + (gain_x[2] + gain_x[3])
        start(gain_y_hops)

    def stage3():
        ring_ax.finish(a_sum)
        to_ay.begin()
        ring_qy.finish(q_sum)
        to_qx.begin()
        landed(gain_y_hops)
        gain_z[0] = (gain_y[0] + gain_y[1]) + (gain_y[2] + gain_y[3])
        start(gain_z_hops)

    def masks():
        lane = lax.broadcasted_iota(jnp.int32, (16, TOK), 1)
        sub = lax.broadcasted_iota(jnp.int32, (16, TOK), 0)
        spread = (lane % 16 == sub).astype(F32).astype(BF)
        lane8 = lax.broadcasted_iota(jnp.int32, (8, TOK), 1) // 16
        sub8 = lax.broadcasted_iota(jnp.int32, (8, TOK), 0)
        here = dot((use_ref[0] == 1).astype(F32).astype(BF), spread)
        there = dot((use_ref[1] == 1).astype(F32).astype(BF), spread)
        usable = jnp.sum(
            jnp.where(lane8 + 4 == sub8, here, 0.0) + jnp.where(lane8 - 4 == sub8, there, 0.0),
            axis=0, keepdims=True,
        )
        query = lax.broadcasted_iota(jnp.int32, (TOK, TOK), 0)
        key = lax.broadcasted_iota(jnp.int32, (TOK, TOK), 1)
        same_lon = (query % 16 // 8) == (key % 16 // 8)
        same_lat = ((query // HALF) == (key // HALF)) | jnp.logical_not(b == bands - 1)
        open_key = jnp.broadcast_to(usable, (TOK, TOK)) > 0.5
        return same_lon & same_lat & (open_key | (query == key))

    first = lax.broadcasted_iota(jnp.int32, (TOK, TOK), 1) < HALF
    zero = jnp.zeros((TOK, TOK), F32)
    head0 = jnp.where(first, zero + 1.0, zero).astype(BF)
    head1 = jnp.where(first, zero, zero + 1.0).astype(BF)

    def pair_cat(values):
        return jnp.concatenate([values * head0, values * head1], axis=0)

    def gain_row(sec):
        return jnp.concatenate([gain[sec, j][0:1] for j in range(4)], axis=1)

    def tile(sec, which, i):
        return proj_ref[sec, :, which * D + TOK * i : which * D + TOK * (i + 1)]

    def forward_merge(sec, x):
        update = dot(x, wm[sec, 0:D]) + dot(x, wm[sec, D : 2 * D])
        average = jnp.mean(update, axis=-1, keepdims=True)
        centered = update - average
        spread = jnp.mean(centered * centered, axis=-1, keepdims=True)
        inverse = lax.rsqrt(spread + EPSILON)
        normed = centered * inverse
        normed_ref[sec] = normed
        hidden_ref[sec] = (normed * gain_row(sec)).astype(BF)
        return update, inverse

    def forward_attend(sec, allowed):
        proj_ref[sec] = dot(hidden_ref[sec], wq[sec]).astype(BF)
        for i in range(HEADS // 2):
            scores = dot_nt(tile(sec, 0, i), pair_cat(tile(sec, 1, i))) * 0.125
            probs = []
            for h in range(2):
                one = jnp.where(allowed, scores[:, TOK * h : TOK * (h + 1)], MASKED)
                weights = jnp.exp(one - jnp.max(one, axis=-1, keepdims=True))
                probs.append(weights / jnp.sum(weights, axis=-1, keepdims=True))
            prob = jnp.concatenate(probs, axis=1).astype(BF)
            prob_ref[sec, i] = prob
            mix_ref[sec, :, TOK * i : TOK * (i + 1)] = dot(prob, pair_cat(tile(sec, 2, i))).astype(BF)

    def forward_out(sec, update):
        result = (update + dot(mix_ref[sec], wo[sec])).astype(BF)
        y_ref[sec] = result
        return result

    def backward_attend(sec, g):
        gm = dot_nt(g, wo[sec]).astype(BF)
        for i in range(HEADS // 2):
            q, k, v = tile(sec, 0, i), tile(sec, 1, i), tile(sec, 2, i)
            gm_pair = gm[:, TOK * i : TOK * (i + 1)]
            prob = prob_ref[sec, i]
            dprob = dot_nt(gm_pair, pair_cat(v))
            pieces = []
            for h in range(2):
                half = slice(TOK * h, TOK * (h + 1))
                p = prob[:, half].astype(F32)
                dp = dprob[:, half]
                pieces.append(p * (dp - jnp.sum(dp * p, axis=-1, keepdims=True)) * 0.125)
            dscore = jnp.concatenate(pieces, axis=1).astype(BF)
            dk = dot_tn(dscore, q)
            dv = dot_tn(prob, gm_pair)
            dproj_ref[:, TOK * i : TOK * (i + 1)] = dot(dscore, pair_cat(k)).astype(BF)
            dproj_ref[:, D + TOK * i : D + TOK * (i + 1)] = jnp.where(first, dk[:TOK], dk[TOK:]).astype(BF)
            dproj_ref[:, 2 * D + TOK * i : 2 * D + TOK * (i + 1)] = jnp.where(first, dv[:TOK], dv[TOK:]).astype(BF)

    def backward_terms(sec, x, g, inverse):
        dhidden = dot_nt(dproj_ref[...], wq[sec])
        normed = normed_ref[sec]
        dgain = jnp.sum(dhidden * normed, axis=0, keepdims=True)
        for j in range(4):
            gain_grads[sec, j] = jnp.broadcast_to(dgain[:, TOK * j : TOK * (j + 1)], (8, TOK))
        dnormed = dhidden * gain_row(sec)
        gu = (
            g.astype(F32)
            + inverse
            * (
                dnormed
                - jnp.mean(dnormed, axis=-1, keepdims=True)
                - normed * jnp.mean(dnormed * normed, axis=-1, keepdims=True)
            )
        ).astype(BF)
        for c in range(4):
            part = slice(TOK * c, TOK * (c + 1))
            grads[sec, 1, part] = dot_tn(hidden_ref[sec, :, part], dproj_ref[...]).astype(BF)
            grads[sec, 0, part, 2 * D : 3 * D] = dot_tn(mix_ref[sec, :, part], g).astype(BF)
            term = dot_tn(x[:, part], gu).astype(BF)
            for j in (c // 2, c // 2 + 2):
                grads[sec, 0, TOK * j : TOK * (j + 1), D * (c % 2) : D * (c % 2 + 1)] = term
        return gu

    for part in (merge, qkv, outw):
        part.begin_strips()
    start(shift[:2] + gain_hops + gain_core_hops[:1])
    for part in (merge, qkv, outw):
        part.begin_blocks()
    for copy in own:
        copy.start()
    shift[2].start()
    for part in (merge, qkv, outw):
        part.relay_strips()
    merge.relay()
    qkv.relay()
    for k in range(1, NX):
        gain_hops[k - 1].landed()
        gain_core_hops[k].start()
    merge.pass_on()
    landed(gain_core_hops)
    landed(shift)
    for copy in own:
        copy.wait()
    allowed = masks()
    x0 = x_ref[...]
    merge.ready()
    update0, inverse0 = forward_merge(0, x0)
    outw.relay()
    qkv.pass_on()
    qkv.ready()
    forward_attend(0, allowed)
    outw.pass_on()
    outw.ready()
    y0 = forward_out(0, update0)
    update1, inverse1 = forward_merge(1, y0)
    forward_attend(1, allowed)
    forward_out(1, update1)
    start(home)
    stays.start()
    cot = cot_ref[...]
    backward_attend(1, cot)
    gu1 = backward_terms(1, y0, cot, inverse1)

    @pl.when(s == 0)
    def _():
        swap()

    chain = dot_nt(gu1, wm[1, 0:D]).astype(BF).astype(F32)
    side = dot_nt(gu1, wm[1, D : 2 * D]).astype(BF).astype(F32)
    g0 = (chain + side).astype(BF)

    @pl.when(s == 1)
    def _():
        stage1()

    backward_attend(0, g0)

    backward_terms(0, x0, g0, inverse0)

    @pl.when(s == 1)
    def _():
        swap()
        stage2()
        stage3()

    @pl.when(s == 0)
    def _():
        stage1()
        stage2()
        stage3()

    to_ay.finish(y_sum.at[0])
    to_qx.finish(y_sum.at[1])
    start(z_hops)
    value = y_sum[both, z_rows].astype(F32)
    for k in range(1, NZ):
        z_hops[k - 1].landed()
        value = value + z_in[k].astype(F32)
    total[both, z_rows, span(y * PART, PART, 128)] = value.astype(BF)
    start(z_back)
    start(y_back[0])
    landed(gain_z_hops)
    gain_value = gain_z[0]
    for k in range(1, NZ):
        gain_value = gain_value + gain_z[k]
    gain_total[...] = gain_value
    for k in (1, 7, 2, 6, 3, 5, 4):
        if k < NZ:
            z_back[k - 1].landed()
            start(y_back[k])
    landed(home)
    stays.wait()
    for hops in y_back:
        landed(hops)
    for hop in net.hops:
        hop.sent()


def widen(home_in, total_in, gain_in, home, merge, qkv, out, gain, total, sems):
    copies = [
        pltpu.make_async_copy(total_in, total, sems.at[0]),
        pltpu.make_async_copy(home_in, home, sems.at[1]),
    ]
    for copy in copies:
        copy.start()
    gain[...] = gain_in[0:1]
    copies[0].wait()
    merge[0:TOK] = total[0, :, 0:D].astype(F32)
    merge[TOK : 2 * TOK] = total[0, :, D : 2 * D].astype(F32)
    out[...] = total[0, :, 2 * D : 3 * D].astype(F32)
    qkv[...] = total[1].astype(F32)
    copies[1].wait()


def vmem(count):
    return [pl.BlockSpec(memory_space=pltpu.VMEM)] * count


def anywhere(count):
    return [pl.BlockSpec(memory_space=pl.ANY)] * count


def shape(dims, dtype=BF):
    return jax.ShapeDtypeStruct(dims, dtype)


def body(fields, cell_mask, merge_weight, qkv_weight, out_weight, norm_gain, out_cotangent):
    x_in = fields.reshape(2, TOK, D)
    g_in = out_cotangent.reshape(2, TOK, D)
    use = cell_mask.reshape(2, 8, 16)
    home, total, gain_total = pl.pallas_call(
        kernel,
        out_shape=(shape((2, TOK, D)), shape((2, TOK, WIDE)), shape((8, TOK), F32)),
        in_specs=anywhere(6) + vmem(1),
        out_specs=vmem(3),
        scratch_shapes=[
            pltpu.VMEM((TOK, D), BF),
            pltpu.VMEM((TOK, D), BF),
            pltpu.VMEM((2, 8, 16), jnp.int32),
            pltpu.VMEM((2, 2 * D, D), BF),
            pltpu.VMEM((2, D, 3 * D), BF),
            pltpu.VMEM((2, D, D), BF),
            pltpu.VMEM((2, 4, 8, TOK), F32),
            pltpu.VMEM((2, TOK, D), BF),
            pltpu.VMEM((2, TOK, D), F32),
            pltpu.VMEM((2, TOK, D), BF),
            pltpu.VMEM((2, TOK, 3 * D), BF),
            pltpu.VMEM((2, HEADS // 2, TOK, 2 * TOK), BF),
            pltpu.VMEM((2, TOK, D), BF),
            pltpu.VMEM((TOK, 3 * D), BF),
            pltpu.VMEM((2, 2, D, WIDE), BF),
            pltpu.VMEM((2, 4, 8, TOK), F32),
            pltpu.VMEM((2, D, WIDE), BF),
            pltpu.VMEM((2, HALF, WIDE), BF),
            pltpu.VMEM((2, TOK, WIDE), BF),
            pltpu.VMEM((2, D // 2, PART), BF),
            pltpu.VMEM((2, D, PART), BF),
            pltpu.VMEM((3, TOK, PART), BF),
            pltpu.VMEM((3, TOK, PART), BF),
            pltpu.VMEM((TOK, WIDE), BF),
            pltpu.VMEM((D, PART), BF),
            pltpu.VMEM((2, TOK, PART), BF),
            pltpu.VMEM((NZ, 2, TALL, PART), BF),
            pltpu.VMEM((4, 8, TOK), F32),
            pltpu.VMEM((4, 8, TOK), F32),
            pltpu.VMEM((4, 8, TOK), F32),
            pltpu.VMEM((NY, 8, TOK), F32),
            pltpu.VMEM((NZ, 8, TOK), F32),
            pltpu.SemaphoreType.DMA((224,)),
            pltpu.SemaphoreType.DMA((224,)),
            pltpu.SemaphoreType.DMA((8,)),
        ],
        compiler_params=pltpu.CompilerParams(
            collective_id=0, has_side_effects=True, vmem_limit_bytes=VMEM_LIMIT
        ),
        name="step",
    )(x_in, g_in, use, merge_weight, qkv_weight, out_weight, norm_gain)
    home, merge_grad, qkv_grad, out_grad, gain_grad = pl.pallas_call(
        widen,
        out_shape=(
            shape((2, TOK, D)), shape((2 * TOK, D), F32), shape((TOK, 3 * D), F32),
            shape((TOK, D), F32), shape((1, TOK), F32),
        ),
        in_specs=anywhere(2) + vmem(1),
        out_specs=vmem(5),
        scratch_shapes=[pltpu.VMEM((2, TOK, WIDE), BF), pltpu.SemaphoreType.DMA((2,))],
        compiler_params=pltpu.CompilerParams(vmem_limit_bytes=VMEM_LIMIT),
        name="widen",
    )(home, total, gain_total)
    section_home = home.reshape(1, 1, 2, 8, 16, D)
    return (section_home, merge_grad[None], qkv_grad[None], out_grad[None], gain_grad)


def solution(mesh):
    return jax.shard_map(
        body,
        mesh=mesh,
        in_specs=(
            P("dp", None, "band", None, None),
            P("dp", None, "band", None),
            P("segment", "dp", None),
            P("segment", "dp", None),
            P("segment", "dp", None),
            P("segment", "dp"),
            P("dp", None, "band", None, None),
        ),
        out_specs=(
            P("segment", "dp", None, "band", None, None),
            P("segment", "dp", None),
            P("segment", "dp", None),
            P("segment", "dp", None),
            P("segment", "dp"),
        ),
        check_vma=False,
    )
```

```python
import jax
import jax.numpy as jnp
from jax import lax
from jax.experimental import pallas as pl
from jax.experimental.pallas import tpu as pltpu
from jax.sharding import PartitionSpec as P

D = 512
HEADS = 8
NX = 4
NY = 4
NZ = 8
TOK = 128
HALF = 64
WIDE = 3 * D
PART = WIDE // NY
TALL = TOK // NZ
EPSILON = 1e-05
MASKED = -1e30
SENDS = 22
RECVS = 88
VMEM_LIMIT = 58 * 1024 * 1024
MESH = pl.DeviceIdType.MESH
BF = jnp.bfloat16
F32 = jnp.float32


def dot(left, right):
    return lax.dot_general(left, right, (((1,), (0,)), ((), ())), preferred_element_type=F32)


def dot_nt(left, right):
    return lax.dot_general(left, right, (((1,), (1,)), ((), ())), preferred_element_type=F32)


def dot_tn(left, right):
    return lax.dot_general(left, right, (((0,), (0,)), ((), ())), preferred_element_type=F32)


def span(index, size, unit=None):
    return pl.ds(pl.multiple_of(index, unit or size), size)


class Group:
    def __init__(self, sem, size_ref):
        self.sem, self.size_ref = sem, size_ref

    def wait(self):
        pltpu.make_async_copy(self.size_ref, self.size_ref, self.sem).wait()


class Hop:
    def __init__(self, net, src, dst, device, send, recv):
        if send is None:
            net.alone.append(self)
        self.copy = pltpu.make_async_remote_copy(
            src_ref=src,
            dst_ref=dst,
            send_sem=send.sem if send else net.send_sem(),
            recv_sem=recv.sem if recv else net.recv_sem(),
            device_id=device,
            device_id_type=MESH,
        )
        self.start = self.copy.start
        self.landed = self.copy.wait_recv
        self.sent = self.copy.wait_send


class Net:
    def __init__(self, send, recv, local):
        self.send, self.recv, self.local = send, recv, local
        self.sends = 0
        self.recvs = 0
        self.kept = 0
        self.alone = []
        self.groups = []

    def send_sem(self):
        self.sends += 1
        return self.send.at[self.sends - 1]

    def recv_sem(self):
        self.recvs += 1
        return self.recv.at[self.recvs - 1]

    def sending(self, size_ref):
        group = Group(self.send_sem(), size_ref)
        self.groups.append(group)
        return group

    def landing(self, size_ref):
        return Group(self.recv_sem(), size_ref)

    def hop(self, src, dst, device, send=None, recv=None):
        return Hop(self, src, dst, device, send, recv)

    def keep(self, src, dst):
        copy = pltpu.make_async_copy(src, dst, self.local.at[self.kept])
        self.kept += 1
        return copy

    def drain(self):
        for hop in self.alone:
            hop.sent()
        for group in self.groups:
            group.wait()


def start(hops):
    for hop in hops:
        hop.start()


def landed(hops):
    for hop in hops:
        hop.landed()


def add_into(count, step, dst, terms):
    def one(i, carry):
        at = i * step
        if len(terms) == 2:
            dst(at, terms[0](at) + terms[1](at))
        else:
            value = terms[0](at).astype(F32)
            for term in terms[1:]:
                value = value + term(at).astype(F32)
            dst(at, value.astype(BF))
        return carry

    lax.fori_loop(0, count // step, one, 0)


def block_rows(count, wide):
    return min(count, 49152 // wide // 16 * 16)


class Ring:
    def __init__(self, net, buf, rect, me, right, left, one_in, two_in, sent_ref):
        self.buf, self.one_in, self.two_in = buf, one_in, two_in
        step = [lax.rem(me + k, 4) for k in range(4)]
        self.rects = [rect(j) for j in step]
        self.nr, self.nc = self.rects[0][1], self.rects[0][3]
        far, after, before = self.rects[2], self.rects[1], self.rects[3]
        half = self.nr // 2
        top, bottom = pl.ds(0, half), pl.ds(half, half)
        out = net.sending(sent_ref)
        self.came = net.landing(two_in)
        self.one = [
            net.hop(self.view(far, 0, half), one_in.at[0], right, out),
            net.hop(self.view(far, half, half), one_in.at[1], left, out),
        ]
        self.plain = [
            net.hop(self.view(after, half, half), two_in.at[0, bottom], right, out, self.came),
            net.hop(self.view(before, 0, half), two_in.at[1, top], left, out, self.came),
        ]
        self.two = [
            net.hop(self.view(after, 0, half), two_in.at[0, top], right, out, self.came),
            net.hop(self.view(before, half, half), two_in.at[1, bottom], left, out, self.came),
        ]

    def at(self, rect, offset, count):
        r0, nr, c0, nc = rect
        first = pl.ds(offset, count) if isinstance(r0, int) and isinstance(offset, int) else span(r0 + offset, count, 16)
        second = pl.ds(0, nc) if isinstance(c0, int) else span(c0, nc, 128)
        return (first, second)

    def view(self, rect, offset, count):
        return self.buf.at[self.at(rect, offset, count)]

    def fold(self, which):
        self.one[which].landed()
        half = self.nr // 2
        rect, base = (self.rects[1], 0) if which == 0 else (self.rects[3], half)
        step = block_rows(half, self.nc)

        def store(i, value):
            self.buf[self.at(rect, base + i, step)] = value

        add_into(
            half,
            step,
            store,
            [lambda i: self.buf[self.at(rect, base + i, step)], lambda i: self.one_in[which, span(i, step, 16)]],
        )
        self.two[which].start()

    def finish(self, dst):
        self.came.wait()
        step = block_rows(self.nr, self.nc)

        def store(i, value):
            dst[span(i, step, 16)] = value

        add_into(
            self.nr,
            step,
            store,
            [
                lambda i: self.buf[self.at(self.rects[0], i, step)],
                lambda i: self.two_in[0, span(i, step, 16)],
                lambda i: self.two_in[1, span(i, step, 16)],
            ],
        )


class Direct:
    def __init__(self, net, buf, rect, me, peer, came_in):
        self.buf, self.came_in = buf, came_in
        self.mine = rect(me)
        out, self.came = net.sending(came_in), net.landing(came_in)
        self.hops = [
            net.hop(buf.at[self.index(rect(lax.rem(me + k, 4)), 0, None)], came_in.at[k - 1], peer(k), out, self.came)
            for k in range(1, 4)
        ]

    def index(self, rect, offset, count):
        r0, nr, c0, nc = rect
        count = count or nr
        first = pl.ds(offset, count) if isinstance(r0, int) and isinstance(offset, int) else span(r0 + offset, count, 16)
        second = pl.ds(0, nc) if isinstance(c0, int) else span(c0, nc, 128)
        return (first, second)

    def begin(self):
        for k in (2, 1, 3):
            self.hops[k - 1].start()

    def finish(self, dst):
        self.came.wait()
        step = block_rows(self.mine[1], self.mine[3])

        def store(i, value):
            dst[span(i, step, 16)] = value

        def term(k):
            return lambda i: self.came_in[k, span(i, step, 16)]

        add_into(
            self.mine[1],
            step,
            store,
            [lambda i: self.buf[self.index(self.mine, i, step)]] + [term(k) for k in range(3)],
        )


def x_dev(d, step):
    return {"dp": lax.rem(d + step, NX)}


def y_dev(b, step):
    z, y = b // NY, lax.rem(b, NY)
    return {"band": z * NY + lax.rem(y + step, NY)}


def z_dev(b, step):
    z, y = b // NY, lax.rem(b, NY)
    return {"band": lax.rem(z + step, NZ) * NY + y}


def z_near(b, step):
    z, y = b // NY, lax.rem(b, NY)
    return {"band": (z // 4 * 4 + lax.rem(lax.rem(z, 4) + step, 4)) * NY + y}


def barrier(devices):
    sem = pltpu.get_barrier_semaphore()
    for device in devices:
        pl.semaphore_signal(sem, inc=1, device_id=device, device_id_type=MESH)
    pl.semaphore_wait(sem, len(devices))


def kernel(x_in, g_in, use_in, wm_in, wq_in, wo_in, gain_in,
           y_home, total, gain_total,
           x_ref, cot_ref, use_ref, wm, wq, wo, gain,
           y_ref, normed_ref, hidden_ref, proj_ref, prob_ref, mix_ref, dproj_ref,
           grads, gain_grads, core_in,
           ax_one, ax_two, qy_one, qy_two, ay_in, qx_in, a_sum, q_sum,
           y_sum, z_in,
           gain_core, gain_sum, gain_x, gain_y, gain_z, send, recv, local):
    d = lax.axis_index("dp")
    s = lax.axis_index("segment")
    b = lax.axis_index("band")
    z, y = b // NY, lax.rem(b, NY)
    other = 1 - s
    bands = NY * NZ
    nxt, prev = lax.rem(b + 1, bands), lax.rem(b + bands - 1, bands)
    core = {"segment": other}
    x_right, x_left = x_dev(d, 1), x_dev(d, NX - 1)
    y_right, y_left = y_dev(b, 1), y_dev(b, NY - 1)
    net = Net(send, recv, local)
    lo, hi = pl.ds(0, HALF), pl.ds(HALF, HALF)
    xd = [lax.rem(d + k, NX) for k in range(NX)]
    yd = [lax.rem(y + k, NY) for k in range(NY)]

    barrier(
        [core]
        + [x_dev(d, k) for k in range(1, NX)]
        + [y_dev(b, k) for k in range(1, NY)]
        + [z_dev(b, k) for k in range(1, NZ)]
        + [{"band": nxt}, {"band": prev}]
        + [{"band": nxt, "segment": other}, {"band": prev, "segment": other}]
    )

    shift = [
        net.hop(x_in.at[s, lo], x_ref.at[hi], {"band": prev}),
        net.hop(use_in.at[s], use_ref.at[1], {"band": prev}),
        net.hop(g_in.at[s, lo], cot_ref.at[hi], {"band": prev}),
    ]
    own = [
        net.keep(x_in.at[s, hi], x_ref.at[lo]),
        net.keep(use_in.at[s], use_ref.at[0]),
        net.keep(g_in.at[s, hi], cot_ref.at[lo]),
    ]
    gain[s, d] = jnp.broadcast_to(gain_in[...].astype(F32), (8, TOK))
    seven = gain_z.at[pl.ds(0, 7)]
    gain_out, gain_in_all = net.sending(seven), net.landing(gain.at[0, pl.ds(0, 3)])
    gain_in_core = net.landing(gain.at[0])
    gain_hops = [
        net.hop(gain.at[s, d], gain.at[s, d], x_dev(d, k), gain_out, gain_in_all) for k in range(1, NX)
    ]
    gain_core_hops = [net.hop(gain.at[s, xd[0]], gain.at[s, xd[0]], core, gain_out, gain_in_core)] + [
        net.hop(gain.at[s, xd[NX - k]], gain.at[s, xd[NX - k]], core, gain_out, gain_in_core)
        for k in range(1, NX)
    ]

    class Gather:
        def __init__(self, src, dst, size, sent_ref):
            wide = dst.shape[-1] // 4
            half, quarter, eighth = size // 2, size // 4, size // 8

            def block(owner, offset, count):
                return dst.at[s, span(owner * size + offset, count, count)]

            def y_strip(owner):
                return dst.at[s, span(owner * size + quarter, half, quarter), span(y * wide, wide)]

            def z_strip(owner):
                return dst.at[
                    s, span(owner * size + 3 * quarter, quarter), span(lax.rem(z, 4) * wide, wide)
                ]

            top = pl.ds(0, quarter)
            y_src = src.at[0, pl.ds(quarter, half), span(y * wide, wide)]
            z_src = src.at[0, pl.ds(3 * quarter, quarter), span(lax.rem(z, 4) * wide, wide)]
            out = net.sending(sent_ref)
            self.y_strips = [net.hop(y_src, y_strip(d), x_dev(d, k), out) for k in range(1, NX)]
            self.z_strips = [net.hop(z_src, z_strip(d), x_dev(d, k), out) for k in range(1, NX)]
            self.right = net.hop(src.at[0, top], block(d, 0, quarter), x_right, out)
            self.left = net.hop(src.at[0, top], block(d, 0, quarter), x_left, out)
            self.from_core = net.landing(dst.at[0])
            self.mine = net.hop(src.at[0], block(d, 0, size), core, out, self.from_core)
            self.local = net.keep(src.at[0], block(d, 0, size))
            owners = [xd[NX - k] for k in range(1, NX)]
            others = pl.ds(0, 3 * wide)
            self.y_came = [net.landing(dst.at[0, pl.ds(0, half), others]) for o in owners]
            self.z_came = [net.landing(dst.at[0, pl.ds(0, quarter), others]) for o in owners]
            self.y_spread = [
                [net.hop(y_strip(o), y_strip(o), y_dev(b, m), out, came) for m in range(1, NY)]
                for o, came in zip(owners, self.y_came)
            ]
            self.z_spread = [
                [net.hop(z_strip(o), z_strip(o), z_near(b, m), out, came) for m in range(1, 4)]
                for o, came in zip(owners, self.z_came)
            ]
            self.far_right = net.hop(block(xd[3], 0, eighth), block(xd[3], 0, eighth), x_right, out)
            self.far_left = net.hop(block(xd[1], eighth, eighth), block(xd[1], eighth, eighth), x_left, out)
            self.across = [
                net.hop(block(o, 0, size), block(o, 0, size), core, out, self.from_core)
                for o in owners
            ]

        def begin_strips(self):
            for k in (2, 1, 3):
                self.y_strips[k - 1].start()
                self.z_strips[k - 1].start()

        def begin_blocks(self):
            start([self.right, self.left, self.mine])
            self.local.start()

        def relay_strips(self):
            for k in (1, 3, 2):
                self.y_strips[k - 1].landed()
                start(self.y_spread[k - 1])
                self.z_strips[k - 1].landed()
                start(self.z_spread[k - 1])

        def relay(self):
            self.right.landed()
            self.far_right.start()
            self.left.landed()
            self.far_left.start()

        def pass_on(self):
            for k in (1, 3, 2):
                self.y_came[k - 1].wait()
                self.z_came[k - 1].wait()
                if k == 2:
                    landed([self.far_right, self.far_left])
                self.across[k - 1].start()

        def ready(self):
            self.from_core.wait()
            self.local.wait()

    merge = Gather(wm_in, wm, 2 * TOK, grads.at[:, :, pl.ds(0, 448), pl.ds(0, D)])
    qkv = Gather(wq_in, wq, TOK, grads.at[0, :, pl.ds(0, 448)])
    outw = Gather(wo_in, wo, TOK, grads.at[0, :, pl.ds(0, 448), pl.ds(0, D)])

    mine = grads.at[s]
    theirs = grads.at[other]
    a_order = [xd[k] for k in (2, 1, 3, 0)]
    q_order = [yd[k] for k in (2, 1, 3, 0)]

    def a_rows(j):
        return (0, span(j * TOK, TOK))

    def q_cols(j):
        return (1, pl.ds(0, D), span(j * PART, PART, 128))

    out = net.sending(core_in)
    swap_a = [net.hop(theirs.at[a_rows(j)], core_in.at[a_rows(j)], core, out) for j in a_order]
    swap_q = [net.hop(theirs.at[q_cols(j)], core_in.at[q_cols(j)], core, out) for j in q_order]
    gain_swap = net.hop(gain_grads.at[other], gain_core, core)
    ring_ax = Ring(net, mine.at[0], lambda j: (j * TOK, TOK, 0, WIDE), d, x_right, x_left, ax_one, ax_two,
                   core_in.at[0, pl.ds(0, 3 * TOK)])
    ring_qy = Ring(net, mine.at[1], lambda j: (0, D, j * PART, PART), y, y_right, y_left, qy_one, qy_two,
                   core_in.at[0, :, pl.ds(0, 3 * PART)])
    to_ay = Direct(net, a_sum, lambda j: (0, TOK, j * PART, PART), y, lambda k: y_dev(b, k), ay_in)
    to_qx = Direct(net, q_sum, lambda j: (j * TOK, TOK, 0, PART), d, lambda k: x_dev(d, k), qx_in)
    three = gain_x.at[pl.ds(0, 3)]
    out, gain_x_in = net.sending(three), net.landing(three)
    gain_x_hops = [
        net.hop(gain_sum.at[xd[k]], gain_x.at[k], x_dev(d, k), out, gain_x_in) for k in range(1, NX)
    ]
    out, gain_y_in = net.sending(three), net.landing(three)
    gain_y_hops = [
        net.hop(gain_y.at[0], gain_y.at[k], y_dev(b, k), out, gain_y_in) for k in range(1, NY)
    ]
    out, gain_z_in = net.sending(seven), net.landing(seven)
    gain_z_hops = [
        net.hop(gain_z.at[0], gain_z.at[k], z_dev(b, k), out, gain_z_in) for k in range(1, NZ)
    ]
    z_rows = span(z * TALL, TALL)
    both = pl.ds(0, 2)
    seven_pieces = z_in.at[pl.ds(0, 7)]
    out, z_came = net.sending(seven_pieces), net.landing(seven_pieces)
    z_hops = [
        net.hop(
            y_sum.at[both, span(lax.rem(z + k, NZ) * TALL, TALL)], z_in.at[k], z_dev(b, k), out, z_came
        )
        for k in range(1, NZ)
    ]
    def piece(k):
        at = (both, span(lax.rem(z + NZ - k, NZ) * TALL, TALL), span(y * PART, PART, 128))
        return total.at[at]

    out = net.sending(seven_pieces)
    z_back = [net.hop(piece(0), piece(0), z_dev(b, k), out) for k in range(1, NZ)]
    three_parts = total.at[both, pl.ds(0, TOK), pl.ds(0, 3 * PART)]
    out, y_came = net.sending(three_parts), net.landing(three_parts)
    y_back = [
        [net.hop(piece(k), piece(k), y_dev(b, m), out, y_came) for m in range(1, NY)]
        for k in range(NZ)
    ]
    home = [
        net.hop(y_ref.at[other, lo], y_home.at[s, hi], core),
        net.hop(y_ref.at[s, hi], y_home.at[s, lo], {"band": nxt}),
        net.hop(y_ref.at[other, hi], y_home.at[s, lo], {"band": nxt, "segment": other}),
    ]
    stays = net.keep(y_ref.at[s, lo], y_home.at[s, hi])

    def core_sum(where, count, wide):
        step = block_rows(count, wide)

        def store(r, value):
            mine[where(r, step)] = value

        add_into(
            count, step, store, [lambda r: mine[where(r, step)], lambda r: core_in[where(r, step)]]
        )

    def a_core(i):
        swap_a[i].landed()
        core_sum(lambda r, step: (0, span(a_order[i] * TOK + r, step, 16)), TOK, WIDE)

    def q_core(i):
        swap_q[i].landed()
        core_sum(lambda r, step: (1, span(r, step, 16), span(q_order[i] * PART, PART, 128)), D, PART)

    def swap():
        for hop_a, hop_q in zip(swap_a, swap_q):
            hop_a.start()
            hop_q.start()
        gain_swap.start()

    def stage1():
        a_core(0)
        start(ring_ax.one)
        q_core(0)
        start(ring_qy.one)
        for i in (1, 2):
            a_core(i)
            ring_ax.plain[i - 1].start()
            q_core(i)
            ring_qy.plain[i - 1].start()
        gain_swap.landed()
        gain_sum[...] = gain_grads[s] + gain_core[...]
        gain_x[0] = gain_sum[d]
        start(gain_x_hops)

    def stage2():
        for which in (0, 1):
            ring_ax.fold(which)
            ring_qy.fold(which)
        a_core(3)
        q_core(3)
        gain_x_in.wait()
        gain_y[0] = (gain_x[0] + gain_x[1]) + (gain_x[2] + gain_x[3])
        start(gain_y_hops)

    def stage3():
        ring_ax.finish(a_sum)
        to_ay.begin()
        ring_qy.finish(q_sum)
        to_qx.begin()
        gain_y_in.wait()
        gain_z[0] = (gain_y[0] + gain_y[1]) + (gain_y[2] + gain_y[3])
        start(gain_z_hops)

    def masks():
        lane = lax.broadcasted_iota(jnp.int32, (16, TOK), 1)
        sub = lax.broadcasted_iota(jnp.int32, (16, TOK), 0)
        spread = (lane % 16 == sub).astype(F32).astype(BF)
        lane8 = lax.broadcasted_iota(jnp.int32, (8, TOK), 1) // 16
        sub8 = lax.broadcasted_iota(jnp.int32, (8, TOK), 0)
        here = dot((use_ref[0] == 1).astype(F32).astype(BF), spread)
        there = dot((use_ref[1] == 1).astype(F32).astype(BF), spread)
        usable = jnp.sum(
            jnp.where(lane8 + 4 == sub8, here, 0.0) + jnp.where(lane8 - 4 == sub8, there, 0.0),
            axis=0, keepdims=True,
        )
        query = lax.broadcasted_iota(jnp.int32, (TOK, TOK), 0)
        key = lax.broadcasted_iota(jnp.int32, (TOK, TOK), 1)
        same_lon = (query % 16 // 8) == (key % 16 // 8)
        same_lat = ((query // HALF) == (key // HALF)) | jnp.logical_not(b == bands - 1)
        open_key = jnp.broadcast_to(usable, (TOK, TOK)) > 0.5
        return same_lon & same_lat & (open_key | (query == key))

    first = lax.broadcasted_iota(jnp.int32, (TOK, TOK), 1) < HALF
    zero = jnp.zeros((TOK, TOK), F32)
    head0 = jnp.where(first, zero + 1.0, zero).astype(BF)
    head1 = jnp.where(first, zero, zero + 1.0).astype(BF)

    def pair_cat(values):
        return jnp.concatenate([values * head0, values * head1], axis=0)

    def gain_row(sec):
        return jnp.concatenate([gain[sec, j][0:1] for j in range(4)], axis=1)

    def tile(sec, which, i):
        return proj_ref[sec, :, which * D + TOK * i : which * D + TOK * (i + 1)]

    def forward_merge(sec, x):
        update = dot(x, wm[sec, 0:D]) + dot(x, wm[sec, D : 2 * D])
        average = jnp.mean(update, axis=-1, keepdims=True)
        centered = update - average
        spread = jnp.mean(centered * centered, axis=-1, keepdims=True)
        inverse = lax.rsqrt(spread + EPSILON)
        normed = centered * inverse
        normed_ref[sec] = normed
        hidden_ref[sec] = (normed * gain_row(sec)).astype(BF)
        return update, inverse

    def forward_attend(sec, allowed):
        proj_ref[sec] = dot(hidden_ref[sec], wq[sec]).astype(BF)
        for i in range(HEADS // 2):
            scores = dot_nt(tile(sec, 0, i), pair_cat(tile(sec, 1, i))) * 0.125
            probs = []
            for h in range(2):
                one = jnp.where(allowed, scores[:, TOK * h : TOK * (h + 1)], MASKED)
                weights = jnp.exp(one - jnp.max(one, axis=-1, keepdims=True))
                probs.append(weights / jnp.sum(weights, axis=-1, keepdims=True))
            prob = jnp.concatenate(probs, axis=1).astype(BF)
            prob_ref[sec, i] = prob
            mix_ref[sec, :, TOK * i : TOK * (i + 1)] = dot(prob, pair_cat(tile(sec, 2, i))).astype(BF)

    def forward_out(sec, update):
        result = (update + dot(mix_ref[sec], wo[sec])).astype(BF)
        y_ref[sec] = result
        return result

    def backward_attend(sec, g):
        gm = dot_nt(g, wo[sec]).astype(BF)
        for i in range(HEADS // 2):
            q, k, v = tile(sec, 0, i), tile(sec, 1, i), tile(sec, 2, i)
            gm_pair = gm[:, TOK * i : TOK * (i + 1)]
            prob = prob_ref[sec, i]
            dprob = dot_nt(gm_pair, pair_cat(v))
            pieces = []
            for h in range(2):
                half = slice(TOK * h, TOK * (h + 1))
                p = prob[:, half].astype(F32)
                dp = dprob[:, half]
                pieces.append(p * (dp - jnp.sum(dp * p, axis=-1, keepdims=True)) * 0.125)
            dscore = jnp.concatenate(pieces, axis=1).astype(BF)
            dk = dot_tn(dscore, q)
            dv = dot_tn(prob, gm_pair)
            dproj_ref[:, TOK * i : TOK * (i + 1)] = dot(dscore, pair_cat(k)).astype(BF)
            dproj_ref[:, D + TOK * i : D + TOK * (i + 1)] = jnp.where(first, dk[:TOK], dk[TOK:]).astype(BF)
            dproj_ref[:, 2 * D + TOK * i : 2 * D + TOK * (i + 1)] = jnp.where(first, dv[:TOK], dv[TOK:]).astype(BF)

    def backward_terms(sec, x, g, inverse):
        dhidden = dot_nt(dproj_ref[...], wq[sec])
        normed = normed_ref[sec]
        dgain = jnp.sum(dhidden * normed, axis=0, keepdims=True)
        for j in range(4):
            gain_grads[sec, j] = jnp.broadcast_to(dgain[:, TOK * j : TOK * (j + 1)], (8, TOK))
        dnormed = dhidden * gain_row(sec)
        gu = (
            g.astype(F32)
            + inverse
            * (
                dnormed
                - jnp.mean(dnormed, axis=-1, keepdims=True)
                - normed * jnp.mean(dnormed * normed, axis=-1, keepdims=True)
            )
        ).astype(BF)
        for c in range(4):
            part = slice(TOK * c, TOK * (c + 1))
            grads[sec, 1, part] = dot_tn(hidden_ref[sec, :, part], dproj_ref[...]).astype(BF)
            grads[sec, 0, part, 2 * D : 3 * D] = dot_tn(mix_ref[sec, :, part], g).astype(BF)
            term = dot_tn(x[:, part], gu).astype(BF)
            for j in (c // 2, c // 2 + 2):
                grads[sec, 0, TOK * j : TOK * (j + 1), D * (c % 2) : D * (c % 2 + 1)] = term
        return gu

    for part in (merge, qkv, outw):
        part.begin_strips()
    start(shift[:2] + gain_hops + gain_core_hops[:1])
    for part in (merge, qkv, outw):
        part.begin_blocks()
    for copy in own:
        copy.start()
    shift[2].start()
    for part in (merge, qkv, outw):
        part.relay_strips()
    merge.relay()
    qkv.relay()
    gain_in_all.wait()
    start(gain_core_hops[1:])
    merge.pass_on()
    gain_in_core.wait()
    landed(shift)
    for copy in own:
        copy.wait()
    allowed = masks()
    x0 = x_ref[...]
    merge.ready()
    update0, inverse0 = forward_merge(0, x0)
    outw.relay()
    qkv.pass_on()
    qkv.ready()
    forward_attend(0, allowed)
    outw.pass_on()
    outw.ready()
    y0 = forward_out(0, update0)
    update1, inverse1 = forward_merge(1, y0)
    forward_attend(1, allowed)
    forward_out(1, update1)
    start(home)
    stays.start()
    cot = cot_ref[...]
    backward_attend(1, cot)
    gu1 = backward_terms(1, y0, cot, inverse1)

    @pl.when(s == 0)
    def _():
        swap()

    chain = dot_nt(gu1, wm[1, 0:D]).astype(BF).astype(F32)
    side = dot_nt(gu1, wm[1, D : 2 * D]).astype(BF).astype(F32)
    g0 = (chain + side).astype(BF)

    @pl.when(s == 1)
    def _():
        stage1()

    backward_attend(0, g0)

    backward_terms(0, x0, g0, inverse0)

    @pl.when(s == 1)
    def _():
        swap()
        stage2()
        stage3()

    @pl.when(s == 0)
    def _():
        stage1()
        stage2()
        stage3()

    to_ay.finish(y_sum.at[0])
    to_qx.finish(y_sum.at[1])
    start(z_hops)
    value = y_sum[both, z_rows].astype(F32)
    z_came.wait()
    for k in range(1, NZ):
        value = value + z_in[k].astype(F32)
    total[both, z_rows, span(y * PART, PART, 128)] = value.astype(BF)
    start(z_back)
    start(y_back[0])
    gain_z_in.wait()
    gain_value = gain_z[0]
    for k in range(1, NZ):
        gain_value = gain_value + gain_z[k]
    gain_total[...] = gain_value
    for k in (1, 7, 2, 6, 3, 5, 4):
        if k < NZ:
            z_back[k - 1].landed()
            start(y_back[k])
    landed(home)
    stays.wait()
    y_came.wait()
    net.drain()


def widen(home_in, total, gain_in, home, merge, qkv, out, gain):
    home[...] = home_in[...]
    merge[0] = total[0, :, 0:D].astype(F32)
    merge[1] = total[0, :, D : 2 * D].astype(F32)
    out[...] = total[0, :, 2 * D : 3 * D].astype(F32)
    qkv[...] = total[1].astype(F32)
    gain[...] = gain_in[0:1]


def vmem(count):
    return [pl.BlockSpec(memory_space=pltpu.VMEM)] * count


def anywhere(count):
    return [pl.BlockSpec(memory_space=pl.ANY)] * count


def shape(dims, dtype=BF):
    return jax.ShapeDtypeStruct(dims, dtype)


def body(fields, cell_mask, merge_weight, qkv_weight, out_weight, norm_gain, out_cotangent):
    x_in = fields.reshape(2, TOK, D)
    g_in = out_cotangent.reshape(2, TOK, D)
    use = cell_mask.reshape(2, 8, 16)
    home, total, gain_total = pl.pallas_call(
        kernel,
        out_shape=(shape((2, TOK, D)), shape((2, TOK, WIDE)), shape((8, TOK), F32)),
        in_specs=anywhere(6) + vmem(1),
        out_specs=vmem(3),
        scratch_shapes=[
            pltpu.VMEM((TOK, D), BF),
            pltpu.VMEM((TOK, D), BF),
            pltpu.VMEM((2, 8, 16), jnp.int32),
            pltpu.VMEM((2, 2 * D, D), BF),
            pltpu.VMEM((2, D, 3 * D), BF),
            pltpu.VMEM((2, D, D), BF),
            pltpu.VMEM((2, 4, 8, TOK), F32),
            pltpu.VMEM((2, TOK, D), BF),
            pltpu.VMEM((2, TOK, D), F32),
            pltpu.VMEM((2, TOK, D), BF),
            pltpu.VMEM((2, TOK, 3 * D), BF),
            pltpu.VMEM((2, HEADS // 2, TOK, 2 * TOK), BF),
            pltpu.VMEM((2, TOK, D), BF),
            pltpu.VMEM((TOK, 3 * D), BF),
            pltpu.VMEM((2, 2, D, WIDE), BF),
            pltpu.VMEM((2, 4, 8, TOK), F32),
            pltpu.VMEM((2, D, WIDE), BF),
            pltpu.VMEM((2, HALF, WIDE), BF),
            pltpu.VMEM((2, TOK, WIDE), BF),
            pltpu.VMEM((2, D // 2, PART), BF),
            pltpu.VMEM((2, D, PART), BF),
            pltpu.VMEM((3, TOK, PART), BF),
            pltpu.VMEM((3, TOK, PART), BF),
            pltpu.VMEM((TOK, WIDE), BF),
            pltpu.VMEM((D, PART), BF),
            pltpu.VMEM((2, TOK, PART), BF),
            pltpu.VMEM((NZ, 2, TALL, PART), BF),
            pltpu.VMEM((4, 8, TOK), F32),
            pltpu.VMEM((4, 8, TOK), F32),
            pltpu.VMEM((4, 8, TOK), F32),
            pltpu.VMEM((NY, 8, TOK), F32),
            pltpu.VMEM((NZ, 8, TOK), F32),
            pltpu.SemaphoreType.DMA((SENDS,)),
            pltpu.SemaphoreType.DMA((RECVS,)),
            pltpu.SemaphoreType.DMA((7,)),
        ],
        compiler_params=pltpu.CompilerParams(
            collective_id=0, has_side_effects=True, vmem_limit_bytes=VMEM_LIMIT
        ),
        name="step",
    )(x_in, g_in, use, merge_weight, qkv_weight, out_weight, norm_gain)
    home, merge_grad, qkv_grad, out_grad, gain_grad = pl.pallas_call(
        widen,
        grid=(2,),
        out_shape=(
            shape((2, TOK, D)), shape((2, TOK, D), F32), shape((TOK, 3 * D), F32),
            shape((TOK, D), F32), shape((1, TOK), F32),
        ),
        in_specs=[
            pl.BlockSpec((2, 64, D), lambda i: (0, i, 0)),
            pl.BlockSpec((2, 64, WIDE), lambda i: (0, i, 0)),
            pl.BlockSpec((8, TOK), lambda i: (0, 0)),
        ],
        out_specs=[
            pl.BlockSpec((2, 64, D), lambda i: (0, i, 0)),
            pl.BlockSpec((2, 64, D), lambda i: (0, i, 0)),
            pl.BlockSpec((64, 3 * D), lambda i: (i, 0)),
            pl.BlockSpec((64, D), lambda i: (i, 0)),
            pl.BlockSpec((1, TOK), lambda i: (0, 0)),
        ],
        compiler_params=pltpu.CompilerParams(vmem_limit_bytes=VMEM_LIMIT),
        name="widen",
    )(home, total, gain_total)
    merge_grad = merge_grad.reshape(2 * TOK, D)
    section_home = home.reshape(1, 1, 2, 8, 16, D)
    return (section_home, merge_grad[None], qkv_grad[None], out_grad[None], gain_grad)


def solution(mesh):
    return jax.shard_map(
        body,
        mesh=mesh,
        in_specs=(
            P("dp", None, "band", None, None),
            P("dp", None, "band", None),
            P("segment", "dp", None),
            P("segment", "dp", None),
            P("segment", "dp", None),
            P("segment", "dp"),
            P("dp", None, "band", None, None),
        ),
        out_specs=(
            P("segment", "dp", None, "band", None, None),
            P("segment", "dp", None),
            P("segment", "dp", None),
            P("segment", "dp", None),
            P("segment", "dp"),
        ),
        check_vma=False,
    )
```

```python
import jax
import jax.numpy as jnp
from jax import lax
from jax.experimental import pallas as pl
from jax.experimental.pallas import tpu as pltpu
from jax.sharding import PartitionSpec as P

D = 512
HEADS = 8
NX = 4
NY = 4
NZ = 8
TOK = 128
HALF = 64
WIDE = 3 * D
PART = WIDE // NY
TALL = TOK // NZ
EPSILON = 1e-05
MASKED = -1e30
SENDS = 22
RECVS = 88
VMEM_LIMIT = 58 * 1024 * 1024
MESH = pl.DeviceIdType.MESH
BF = jnp.bfloat16
F32 = jnp.float32


def dot(left, right):
    return lax.dot_general(left, right, (((1,), (0,)), ((), ())), preferred_element_type=F32)


def dot_nt(left, right):
    return lax.dot_general(left, right, (((1,), (1,)), ((), ())), preferred_element_type=F32)


def dot_tn(left, right):
    return lax.dot_general(left, right, (((0,), (0,)), ((), ())), preferred_element_type=F32)


def span(index, size, unit=None):
    return pl.ds(pl.multiple_of(index, unit or size), size)


class Group:
    def __init__(self, sem, size_ref):
        self.sem, self.size_ref = sem, size_ref

    def wait(self):
        pltpu.make_async_copy(self.size_ref, self.size_ref, self.sem).wait()


class Hop:
    def __init__(self, net, src, dst, device, send, recv):
        if send is None:
            net.alone.append(self)
        self.copy = pltpu.make_async_remote_copy(
            src_ref=src,
            dst_ref=dst,
            send_sem=send.sem if send else net.send_sem(),
            recv_sem=recv.sem if recv else net.recv_sem(),
            device_id=device,
            device_id_type=MESH,
        )
        self.start = self.copy.start
        self.landed = self.copy.wait_recv
        self.sent = self.copy.wait_send


class Net:
    def __init__(self, send, recv, local):
        self.send, self.recv, self.local = send, recv, local
        self.sends = 0
        self.recvs = 0
        self.kept = 0
        self.alone = []
        self.groups = []

    def send_sem(self):
        self.sends += 1
        return self.send.at[self.sends - 1]

    def recv_sem(self):
        self.recvs += 1
        return self.recv.at[self.recvs - 1]

    def sending(self, size_ref):
        group = Group(self.send_sem(), size_ref)
        self.groups.append(group)
        return group

    def landing(self, size_ref):
        return Group(self.recv_sem(), size_ref)

    def hop(self, src, dst, device, send=None, recv=None):
        return Hop(self, src, dst, device, send, recv)

    def keep(self, src, dst):
        copy = pltpu.make_async_copy(src, dst, self.local.at[self.kept])
        self.kept += 1
        return copy

    def drain(self):
        for hop in self.alone:
            hop.sent()
        for group in self.groups:
            group.wait()


def start(hops):
    for hop in hops:
        hop.start()


def landed(hops):
    for hop in hops:
        hop.landed()


def add_into(count, step, dst, terms):
    def one(i, carry):
        at = i * step
        if len(terms) == 2:
            dst(at, terms[0](at) + terms[1](at))
        else:
            value = terms[0](at).astype(F32)
            for term in terms[1:]:
                value = value + term(at).astype(F32)
            dst(at, value.astype(BF))
        return carry

    lax.fori_loop(0, count // step, one, 0)


def block_rows(count, wide):
    return min(count, 49152 // wide // 16 * 16)


class Ring:
    def __init__(self, net, buf, rect, me, right, left, one_in, two_in, sent_ref):
        self.buf, self.one_in, self.two_in = buf, one_in, two_in
        step = [lax.rem(me + k, 4) for k in range(4)]
        self.rects = [rect(j) for j in step]
        self.nr, self.nc = self.rects[0][1], self.rects[0][3]
        far, after, before = self.rects[2], self.rects[1], self.rects[3]
        half = self.nr // 2
        top, bottom = pl.ds(0, half), pl.ds(half, half)
        out = net.sending(sent_ref)
        self.came = net.landing(two_in)
        self.one = [
            net.hop(self.view(far, 0, half), one_in.at[0], right, out),
            net.hop(self.view(far, half, half), one_in.at[1], left, out),
        ]
        self.plain = [
            net.hop(self.view(after, half, half), two_in.at[0, bottom], right, out, self.came),
            net.hop(self.view(before, 0, half), two_in.at[1, top], left, out, self.came),
        ]
        self.two = [
            net.hop(self.view(after, 0, half), two_in.at[0, top], right, out, self.came),
            net.hop(self.view(before, half, half), two_in.at[1, bottom], left, out, self.came),
        ]

    def at(self, rect, offset, count):
        r0, nr, c0, nc = rect
        first = pl.ds(offset, count) if isinstance(r0, int) and isinstance(offset, int) else span(r0 + offset, count, 16)
        second = pl.ds(0, nc) if isinstance(c0, int) else span(c0, nc, 128)
        return (first, second)

    def view(self, rect, offset, count):
        return self.buf.at[self.at(rect, offset, count)]

    def fold(self, which):
        self.one[which].landed()
        half = self.nr // 2
        rect, base = (self.rects[1], 0) if which == 0 else (self.rects[3], half)
        step = block_rows(half, self.nc)

        def store(i, value):
            self.buf[self.at(rect, base + i, step)] = value

        add_into(
            half,
            step,
            store,
            [lambda i: self.buf[self.at(rect, base + i, step)], lambda i: self.one_in[which, span(i, step, 16)]],
        )
        self.two[which].start()

    def finish(self, dst):
        self.came.wait()
        step = block_rows(self.nr, self.nc)

        def store(i, value):
            dst[span(i, step, 16)] = value

        add_into(
            self.nr,
            step,
            store,
            [
                lambda i: self.buf[self.at(self.rects[0], i, step)],
                lambda i: self.two_in[0, span(i, step, 16)],
                lambda i: self.two_in[1, span(i, step, 16)],
            ],
        )


class Direct:
    def __init__(self, net, buf, rect, me, peer, came_in):
        self.buf, self.came_in = buf, came_in
        self.mine = rect(me)
        out, self.came = net.sending(came_in), net.landing(came_in)
        self.hops = [
            net.hop(buf.at[self.index(rect(lax.rem(me + k, 4)), 0, None)], came_in.at[k - 1], peer(k), out, self.came)
            for k in range(1, 4)
        ]

    def index(self, rect, offset, count):
        r0, nr, c0, nc = rect
        count = count or nr
        first = pl.ds(offset, count) if isinstance(r0, int) and isinstance(offset, int) else span(r0 + offset, count, 16)
        second = pl.ds(0, nc) if isinstance(c0, int) else span(c0, nc, 128)
        return (first, second)

    def begin(self):
        for k in (2, 1, 3):
            self.hops[k - 1].start()

    def finish(self, dst):
        self.came.wait()
        step = block_rows(self.mine[1], self.mine[3])

        def store(i, value):
            dst[span(i, step, 16)] = value

        def term(k):
            return lambda i: self.came_in[k, span(i, step, 16)]

        add_into(
            self.mine[1],
            step,
            store,
            [lambda i: self.buf[self.index(self.mine, i, step)]] + [term(k) for k in range(3)],
        )


def x_dev(d, step):
    return {"dp": lax.rem(d + step, NX)}


def y_dev(b, step):
    z, y = b // NY, lax.rem(b, NY)
    return {"band": z * NY + lax.rem(y + step, NY)}


def z_dev(b, step):
    z, y = b // NY, lax.rem(b, NY)
    return {"band": lax.rem(z + step, NZ) * NY + y}


def z_near(b, step):
    z, y = b // NY, lax.rem(b, NY)
    return {"band": (z // 4 * 4 + lax.rem(lax.rem(z, 4) + step, 4)) * NY + y}


def barrier(devices):
    sem = pltpu.get_barrier_semaphore()
    for device in devices:
        pl.semaphore_signal(sem, inc=1, device_id=device, device_id_type=MESH)
    pl.semaphore_wait(sem, len(devices))


def kernel(x_in, g_in, use_in, wm_in, wq_in, wo_in, gain_in,
           y_home, total, gain_total,
           x_ref, cot_ref, use_ref, wm, wq, wo, gain,
           y_ref, normed_ref, hidden_ref, proj_ref, prob_ref, mix_ref, dproj_ref,
           grads, gain_grads, core_in,
           ax_one, ax_two, qy_one, qy_two, ay_in, qx_in, a_sum, q_sum,
           y_sum, z_in,
           gain_core, gain_sum, gain_x, gain_y, gain_z, send, recv, local):
    d = lax.axis_index("dp")
    s = lax.axis_index("segment")
    b = lax.axis_index("band")
    z, y = b // NY, lax.rem(b, NY)
    other = 1 - s
    bands = NY * NZ
    nxt, prev = lax.rem(b + 1, bands), lax.rem(b + bands - 1, bands)
    core = {"segment": other}
    x_right, x_left = x_dev(d, 1), x_dev(d, NX - 1)
    y_right, y_left = y_dev(b, 1), y_dev(b, NY - 1)
    net = Net(send, recv, local)
    lo, hi = pl.ds(0, HALF), pl.ds(HALF, HALF)
    xd = [lax.rem(d + k, NX) for k in range(NX)]
    yd = [lax.rem(y + k, NY) for k in range(NY)]

    barrier(
        [core]
        + [x_dev(d, k) for k in range(1, NX)]
        + [y_dev(b, k) for k in range(1, NY)]
        + [z_dev(b, k) for k in range(1, NZ)]
        + [{"band": nxt}, {"band": prev}]
        + [{"band": nxt, "segment": other}, {"band": prev, "segment": other}]
    )

    shift = [
        net.hop(x_in.at[s, lo], x_ref.at[hi], {"band": prev}),
        net.hop(use_in.at[s], use_ref.at[1], {"band": prev}),
        net.hop(g_in.at[s, lo], cot_ref.at[hi], {"band": prev}),
    ]
    own = [
        net.keep(x_in.at[s, hi], x_ref.at[lo]),
        net.keep(use_in.at[s], use_ref.at[0]),
        net.keep(g_in.at[s, hi], cot_ref.at[lo]),
    ]
    gain[s, d] = jnp.broadcast_to(gain_in[...].astype(F32), (8, TOK))
    seven = gain_z.at[pl.ds(0, 7)]
    gain_out, gain_in_all = net.sending(seven), net.landing(gain.at[0, pl.ds(0, 3)])
    gain_in_core = net.landing(gain.at[0])
    gain_hops = [
        net.hop(gain.at[s, d], gain.at[s, d], x_dev(d, k), gain_out, gain_in_all) for k in range(1, NX)
    ]
    gain_core_hops = [net.hop(gain.at[s, xd[0]], gain.at[s, xd[0]], core, gain_out, gain_in_core)] + [
        net.hop(gain.at[s, xd[NX - k]], gain.at[s, xd[NX - k]], core, gain_out, gain_in_core)
        for k in range(1, NX)
    ]

    class Gather:
        def __init__(self, src, dst, size, sent_ref):
            wide = dst.shape[-1] // 4
            half, quarter, eighth = size // 2, size // 4, size // 8

            def block(owner, offset, count):
                return dst.at[s, span(owner * size + offset, count, count)]

            def y_strip(owner):
                return dst.at[s, span(owner * size + quarter, half, quarter), span(y * wide, wide)]

            def z_strip(owner):
                return dst.at[
                    s, span(owner * size + 3 * quarter, quarter), span(lax.rem(z, 4) * wide, wide)
                ]

            top = pl.ds(0, quarter)
            y_src = src.at[0, pl.ds(quarter, half), span(y * wide, wide)]
            z_src = src.at[0, pl.ds(3 * quarter, quarter), span(lax.rem(z, 4) * wide, wide)]
            out = net.sending(sent_ref)
            self.y_strips = [net.hop(y_src, y_strip(d), x_dev(d, k), out) for k in range(1, NX)]
            self.z_strips = [net.hop(z_src, z_strip(d), x_dev(d, k), out) for k in range(1, NX)]
            self.right = net.hop(src.at[0, top], block(d, 0, quarter), x_right, out)
            self.left = net.hop(src.at[0, top], block(d, 0, quarter), x_left, out)
            self.from_core = net.landing(dst.at[0])
            self.mine = net.hop(src.at[0], block(d, 0, size), core, out, self.from_core)
            self.local = net.keep(src.at[0], block(d, 0, size))
            owners = [xd[NX - k] for k in range(1, NX)]
            others = pl.ds(0, 3 * wide)
            self.y_came = [net.landing(dst.at[0, pl.ds(0, half), others]) for o in owners]
            self.z_came = [net.landing(dst.at[0, pl.ds(0, quarter), others]) for o in owners]
            self.y_spread = [
                [net.hop(y_strip(o), y_strip(o), y_dev(b, m), out, came) for m in range(1, NY)]
                for o, came in zip(owners, self.y_came)
            ]
            self.z_spread = [
                [net.hop(z_strip(o), z_strip(o), z_near(b, m), out, came) for m in range(1, 4)]
                for o, came in zip(owners, self.z_came)
            ]
            self.far_right = net.hop(block(xd[3], 0, eighth), block(xd[3], 0, eighth), x_right, out)
            self.far_left = net.hop(block(xd[1], eighth, eighth), block(xd[1], eighth, eighth), x_left, out)
            self.across = [
                net.hop(block(o, 0, size), block(o, 0, size), core, out, self.from_core)
                for o in owners
            ]

        def begin_strips(self):
            for k in (2, 1, 3):
                self.y_strips[k - 1].start()
                self.z_strips[k - 1].start()

        def begin_blocks(self):
            start([self.right, self.left, self.mine])
            self.local.start()

        def relay_strips(self):
            for k in (1, 3, 2):
                self.y_strips[k - 1].landed()
                start(self.y_spread[k - 1])
                self.z_strips[k - 1].landed()
                start(self.z_spread[k - 1])

        def relay(self):
            self.right.landed()
            self.far_right.start()
            self.left.landed()
            self.far_left.start()

        def pass_on(self):
            for k in (1, 3, 2):
                self.y_came[k - 1].wait()
                self.z_came[k - 1].wait()
                if k == 2:
                    landed([self.far_right, self.far_left])
                self.across[k - 1].start()

        def ready(self):
            self.from_core.wait()
            self.local.wait()

    merge = Gather(wm_in, wm, 2 * TOK, grads.at[:, :, pl.ds(0, 448), pl.ds(0, D)])
    qkv = Gather(wq_in, wq, TOK, grads.at[0, :, pl.ds(0, 448)])
    outw = Gather(wo_in, wo, TOK, grads.at[0, :, pl.ds(0, 448), pl.ds(0, D)])

    mine = grads.at[s]
    theirs = grads.at[other]
    a_order = [xd[k] for k in (2, 1, 3, 0)]
    q_order = [yd[k] for k in (2, 1, 3, 0)]

    def a_rows(j):
        return (0, span(j * TOK, TOK))

    def q_cols(j):
        return (1, pl.ds(0, D), span(j * PART, PART, 128))

    out = net.sending(core_in)
    swap_a = [net.hop(theirs.at[a_rows(j)], core_in.at[a_rows(j)], core, out) for j in a_order]
    swap_q = [net.hop(theirs.at[q_cols(j)], core_in.at[q_cols(j)], core, out) for j in q_order]
    gain_swap = net.hop(gain_grads.at[other], gain_core, core)
    ring_ax = Ring(net, mine.at[0], lambda j: (j * TOK, TOK, 0, WIDE), d, x_right, x_left, ax_one, ax_two,
                   core_in.at[0, pl.ds(0, 3 * TOK)])
    ring_qy = Ring(net, mine.at[1], lambda j: (0, D, j * PART, PART), y, y_right, y_left, qy_one, qy_two,
                   core_in.at[0, :, pl.ds(0, 3 * PART)])
    to_ay = Direct(net, a_sum, lambda j: (0, TOK, j * PART, PART), y, lambda k: y_dev(b, k), ay_in)
    to_qx = Direct(net, q_sum, lambda j: (j * TOK, TOK, 0, PART), d, lambda k: x_dev(d, k), qx_in)
    three = gain_x.at[pl.ds(0, 3)]
    out, gain_x_in = net.sending(three), net.landing(three)
    gain_x_hops = [
        net.hop(gain_sum.at[xd[k]], gain_x.at[k], x_dev(d, k), out, gain_x_in) for k in range(1, NX)
    ]
    out, gain_y_in = net.sending(three), net.landing(three)
    gain_y_hops = [
        net.hop(gain_y.at[0], gain_y.at[k], y_dev(b, k), out, gain_y_in) for k in range(1, NY)
    ]
    out, gain_z_in = net.sending(seven), net.landing(seven)
    gain_z_hops = [
        net.hop(gain_z.at[0], gain_z.at[k], z_dev(b, k), out, gain_z_in) for k in range(1, NZ)
    ]
    z_rows = span(z * TALL, TALL)
    both = pl.ds(0, 2)
    seven_pieces = z_in.at[pl.ds(0, 7)]
    out, z_came = net.sending(seven_pieces), net.landing(seven_pieces)
    z_hops = [
        [
            net.hop(
                y_sum.at[which, span(lax.rem(z + k, NZ) * TALL, TALL)], z_in.at[k, which],
                z_dev(b, k), out, z_came,
            )
            for k in (4, 3, 5, 2, 6, 1, 7)[-(NZ - 1):]
        ]
        for which in (0, 1)
    ]
    def piece(k):
        at = (both, span(lax.rem(z + NZ - k, NZ) * TALL, TALL), span(y * PART, PART, 128))
        return total.at[at]

    out = net.sending(seven_pieces)
    z_back = [net.hop(piece(0), piece(0), z_dev(b, k), out) for k in range(1, NZ)]
    three_parts = total.at[both, pl.ds(0, TOK), pl.ds(0, 3 * PART)]
    out, y_came = net.sending(three_parts), net.landing(three_parts)
    y_back = [
        [net.hop(piece(k), piece(k), y_dev(b, m), out, y_came) for m in range(1, NY)]
        for k in range(NZ)
    ]
    home = [
        net.hop(y_ref.at[other, lo], y_home.at[s, hi], core),
        net.hop(y_ref.at[s, hi], y_home.at[s, lo], {"band": nxt}),
        net.hop(y_ref.at[other, hi], y_home.at[s, lo], {"band": nxt, "segment": other}),
    ]
    stays = net.keep(y_ref.at[s, lo], y_home.at[s, hi])

    def core_sum(where, count, wide):
        step = block_rows(count, wide)

        def store(r, value):
            mine[where(r, step)] = value

        add_into(
            count, step, store, [lambda r: mine[where(r, step)], lambda r: core_in[where(r, step)]]
        )

    def a_core(i):
        swap_a[i].landed()
        core_sum(lambda r, step: (0, span(a_order[i] * TOK + r, step, 16)), TOK, WIDE)

    def q_core(i):
        swap_q[i].landed()
        core_sum(lambda r, step: (1, span(r, step, 16), span(q_order[i] * PART, PART, 128)), D, PART)

    def swap():
        for hop_a, hop_q in zip(swap_a, swap_q):
            hop_a.start()
            hop_q.start()
        gain_swap.start()

    def stage1():
        a_core(0)
        start(ring_ax.one)
        q_core(0)
        start(ring_qy.one)
        for i in (1, 2):
            a_core(i)
            ring_ax.plain[i - 1].start()
            q_core(i)
            ring_qy.plain[i - 1].start()
        gain_swap.landed()
        gain_sum[...] = gain_grads[s] + gain_core[...]
        gain_x[0] = gain_sum[d]
        start(gain_x_hops)

    def stage2():
        for which in (0, 1):
            ring_ax.fold(which)
            ring_qy.fold(which)
        a_core(3)
        q_core(3)
        gain_x_in.wait()
        gain_y[0] = (gain_x[0] + gain_x[1]) + (gain_x[2] + gain_x[3])
        start(gain_y_hops)

    def stage3():
        ring_ax.finish(a_sum)
        to_ay.begin()
        ring_qy.finish(q_sum)
        to_qx.begin()
        gain_y_in.wait()
        gain_z[0] = (gain_y[0] + gain_y[1]) + (gain_y[2] + gain_y[3])
        start(gain_z_hops)

    def masks():
        lane = lax.broadcasted_iota(jnp.int32, (16, TOK), 1)
        sub = lax.broadcasted_iota(jnp.int32, (16, TOK), 0)
        spread = (lane % 16 == sub).astype(F32).astype(BF)
        lane8 = lax.broadcasted_iota(jnp.int32, (8, TOK), 1) // 16
        sub8 = lax.broadcasted_iota(jnp.int32, (8, TOK), 0)
        here = dot((use_ref[0] == 1).astype(F32).astype(BF), spread)
        there = dot((use_ref[1] == 1).astype(F32).astype(BF), spread)
        usable = jnp.sum(
            jnp.where(lane8 + 4 == sub8, here, 0.0) + jnp.where(lane8 - 4 == sub8, there, 0.0),
            axis=0, keepdims=True,
        )
        query = lax.broadcasted_iota(jnp.int32, (TOK, TOK), 0)
        key = lax.broadcasted_iota(jnp.int32, (TOK, TOK), 1)
        same_lon = (query % 16 // 8) == (key % 16 // 8)
        same_lat = ((query // HALF) == (key // HALF)) | jnp.logical_not(b == bands - 1)
        open_key = jnp.broadcast_to(usable, (TOK, TOK)) > 0.5
        return same_lon & same_lat & (open_key | (query == key))

    first = lax.broadcasted_iota(jnp.int32, (TOK, TOK), 1) < HALF
    zero = jnp.zeros((TOK, TOK), F32)
    head0 = jnp.where(first, zero + 1.0, zero).astype(BF)
    head1 = jnp.where(first, zero, zero + 1.0).astype(BF)

    def pair_cat(values):
        return jnp.concatenate([values * head0, values * head1], axis=0)

    def gain_row(sec):
        return jnp.concatenate([gain[sec, j][0:1] for j in range(4)], axis=1)

    def tile(sec, which, i):
        return proj_ref[sec, :, which * D + TOK * i : which * D + TOK * (i + 1)]

    def forward_merge(sec, x):
        update = dot(x, wm[sec, 0:D]) + dot(x, wm[sec, D : 2 * D])
        average = jnp.mean(update, axis=-1, keepdims=True)
        centered = update - average
        spread = jnp.mean(centered * centered, axis=-1, keepdims=True)
        inverse = lax.rsqrt(spread + EPSILON)
        normed = centered * inverse
        normed_ref[sec] = normed
        hidden_ref[sec] = (normed * gain_row(sec)).astype(BF)
        return update, inverse

    def forward_attend(sec, allowed):
        proj_ref[sec] = dot(hidden_ref[sec], wq[sec]).astype(BF)
        for i in range(HEADS // 2):
            scores = dot_nt(tile(sec, 0, i), pair_cat(tile(sec, 1, i))) * 0.125
            probs = []
            for h in range(2):
                one = jnp.where(allowed, scores[:, TOK * h : TOK * (h + 1)], MASKED)
                weights = jnp.exp(one - jnp.max(one, axis=-1, keepdims=True))
                probs.append(weights / jnp.sum(weights, axis=-1, keepdims=True))
            prob = jnp.concatenate(probs, axis=1).astype(BF)
            prob_ref[sec, i] = prob
            mix_ref[sec, :, TOK * i : TOK * (i + 1)] = dot(prob, pair_cat(tile(sec, 2, i))).astype(BF)

    def forward_out(sec, update):
        result = (update + dot(mix_ref[sec], wo[sec])).astype(BF)
        y_ref[sec] = result
        return result

    def backward_attend(sec, g):
        gm = dot_nt(g, wo[sec]).astype(BF)
        for i in range(HEADS // 2):
            q, k, v = tile(sec, 0, i), tile(sec, 1, i), tile(sec, 2, i)
            gm_pair = gm[:, TOK * i : TOK * (i + 1)]
            prob = prob_ref[sec, i]
            dprob = dot_nt(gm_pair, pair_cat(v))
            pieces = []
            for h in range(2):
                half = slice(TOK * h, TOK * (h + 1))
                p = prob[:, half].astype(F32)
                dp = dprob[:, half]
                pieces.append(p * (dp - jnp.sum(dp * p, axis=-1, keepdims=True)) * 0.125)
            dscore = jnp.concatenate(pieces, axis=1).astype(BF)
            dk = dot_tn(dscore, q)
            dv = dot_tn(prob, gm_pair)
            dproj_ref[:, TOK * i : TOK * (i + 1)] = dot(dscore, pair_cat(k)).astype(BF)
            dproj_ref[:, D + TOK * i : D + TOK * (i + 1)] = jnp.where(first, dk[:TOK], dk[TOK:]).astype(BF)
            dproj_ref[:, 2 * D + TOK * i : 2 * D + TOK * (i + 1)] = jnp.where(first, dv[:TOK], dv[TOK:]).astype(BF)

    def backward_terms(sec, x, g, inverse):
        dhidden = dot_nt(dproj_ref[...], wq[sec])
        normed = normed_ref[sec]
        dgain = jnp.sum(dhidden * normed, axis=0, keepdims=True)
        for j in range(4):
            gain_grads[sec, j] = jnp.broadcast_to(dgain[:, TOK * j : TOK * (j + 1)], (8, TOK))
        dnormed = dhidden * gain_row(sec)
        gu = (
            g.astype(F32)
            + inverse
            * (
                dnormed
                - jnp.mean(dnormed, axis=-1, keepdims=True)
                - normed * jnp.mean(dnormed * normed, axis=-1, keepdims=True)
            )
        ).astype(BF)
        for c in range(4):
            part = slice(TOK * c, TOK * (c + 1))
            grads[sec, 1, part] = dot_tn(hidden_ref[sec, :, part], dproj_ref[...]).astype(BF)
            grads[sec, 0, part, 2 * D : 3 * D] = dot_tn(mix_ref[sec, :, part], g).astype(BF)
            term = dot_tn(x[:, part], gu).astype(BF)
            for j in (c // 2, c // 2 + 2):
                grads[sec, 0, TOK * j : TOK * (j + 1), D * (c % 2) : D * (c % 2 + 1)] = term
        return gu

    for part in (merge, qkv, outw):
        part.begin_strips()
    start(shift[:2] + gain_hops + gain_core_hops[:1])
    for part in (merge, qkv, outw):
        part.begin_blocks()
    for copy in own:
        copy.start()
    shift[2].start()
    for part in (merge, qkv, outw):
        part.relay_strips()
    for part in (merge, qkv, outw):
        part.relay()
    gain_in_all.wait()
    start(gain_core_hops[1:])
    merge.pass_on()
    qkv.pass_on()
    gain_in_core.wait()
    landed(shift)
    for copy in own:
        copy.wait()
    allowed = masks()
    x0 = x_ref[...]
    merge.ready()
    update0, inverse0 = forward_merge(0, x0)
    outw.pass_on()
    qkv.ready()
    forward_attend(0, allowed)
    outw.ready()
    y0 = forward_out(0, update0)
    update1, inverse1 = forward_merge(1, y0)
    forward_attend(1, allowed)
    forward_out(1, update1)
    start(home)
    stays.start()
    cot = cot_ref[...]
    backward_attend(1, cot)
    gu1 = backward_terms(1, y0, cot, inverse1)

    @pl.when(s == 0)
    def _():
        swap()

    chain = dot_nt(gu1, wm[1, 0:D]).astype(BF).astype(F32)
    side = dot_nt(gu1, wm[1, D : 2 * D]).astype(BF).astype(F32)
    g0 = (chain + side).astype(BF)

    backward_attend(0, g0)

    @pl.when(s == 1)
    def _():
        stage1()

    backward_terms(0, x0, g0, inverse0)

    @pl.when(s == 1)
    def _():
        swap()
        stage2()
        stage3()

    @pl.when(s == 0)
    def _():
        stage1()
        stage2()
        stage3()

    to_ay.finish(y_sum.at[0])
    start(z_hops[0])
    to_qx.finish(y_sum.at[1])
    start(z_hops[1])
    value = y_sum[both, z_rows].astype(F32)
    z_came.wait()
    for k in range(1, NZ):
        value = value + z_in[k].astype(F32)
    total[both, z_rows, span(y * PART, PART, 128)] = value.astype(BF)
    start(z_back)
    start(y_back[0])
    gain_z_in.wait()
    gain_value = gain_z[0]
    for k in range(1, NZ):
        gain_value = gain_value + gain_z[k]
    gain_total[...] = gain_value
    for k in (1, 7, 2, 6, 3, 5, 4):
        if k < NZ:
            z_back[k - 1].landed()
            start(y_back[k])
    landed(home)
    stays.wait()
    y_came.wait()
    net.drain()


def widen(home_in, total, gain_in, home, merge, qkv, out, gain):
    home[...] = home_in[...]
    merge[0] = total[0, :, 0:D].astype(F32)
    merge[1] = total[0, :, D : 2 * D].astype(F32)
    out[...] = total[0, :, 2 * D : 3 * D].astype(F32)
    qkv[...] = total[1].astype(F32)
    gain[...] = gain_in[0:1]


def vmem(count):
    return [pl.BlockSpec(memory_space=pltpu.VMEM)] * count


def anywhere(count):
    return [pl.BlockSpec(memory_space=pl.ANY)] * count


def shape(dims, dtype=BF):
    return jax.ShapeDtypeStruct(dims, dtype)


def body(fields, cell_mask, merge_weight, qkv_weight, out_weight, norm_gain, out_cotangent):
    x_in = fields.reshape(2, TOK, D)
    g_in = out_cotangent.reshape(2, TOK, D)
    use = cell_mask.reshape(2, 8, 16)
    home, total, gain_total = pl.pallas_call(
        kernel,
        out_shape=(shape((2, TOK, D)), shape((2, TOK, WIDE)), shape((8, TOK), F32)),
        in_specs=anywhere(6) + vmem(1),
        out_specs=vmem(3),
        scratch_shapes=[
            pltpu.VMEM((TOK, D), BF),
            pltpu.VMEM((TOK, D), BF),
            pltpu.VMEM((2, 8, 16), jnp.int32),
            pltpu.VMEM((2, 2 * D, D), BF),
            pltpu.VMEM((2, D, 3 * D), BF),
            pltpu.VMEM((2, D, D), BF),
            pltpu.VMEM((2, 4, 8, TOK), F32),
            pltpu.VMEM((2, TOK, D), BF),
            pltpu.VMEM((2, TOK, D), F32),
            pltpu.VMEM((2, TOK, D), BF),
            pltpu.VMEM((2, TOK, 3 * D), BF),
            pltpu.VMEM((2, HEADS // 2, TOK, 2 * TOK), BF),
            pltpu.VMEM((2, TOK, D), BF),
            pltpu.VMEM((TOK, 3 * D), BF),
            pltpu.VMEM((2, 2, D, WIDE), BF),
            pltpu.VMEM((2, 4, 8, TOK), F32),
            pltpu.VMEM((2, D, WIDE), BF),
            pltpu.VMEM((2, HALF, WIDE), BF),
            pltpu.VMEM((2, TOK, WIDE), BF),
            pltpu.VMEM((2, D // 2, PART), BF),
            pltpu.VMEM((2, D, PART), BF),
            pltpu.VMEM((3, TOK, PART), BF),
            pltpu.VMEM((3, TOK, PART), BF),
            pltpu.VMEM((TOK, WIDE), BF),
            pltpu.VMEM((D, PART), BF),
            pltpu.VMEM((2, TOK, PART), BF),
            pltpu.VMEM((NZ, 2, TALL, PART), BF),
            pltpu.VMEM((4, 8, TOK), F32),
            pltpu.VMEM((4, 8, TOK), F32),
            pltpu.VMEM((4, 8, TOK), F32),
            pltpu.VMEM((NY, 8, TOK), F32),
            pltpu.VMEM((NZ, 8, TOK), F32),
            pltpu.SemaphoreType.DMA((SENDS,)),
            pltpu.SemaphoreType.DMA((RECVS,)),
            pltpu.SemaphoreType.DMA((7,)),
        ],
        compiler_params=pltpu.CompilerParams(
            collective_id=0, has_side_effects=True, vmem_limit_bytes=VMEM_LIMIT
        ),
        name="step",
    )(x_in, g_in, use, merge_weight, qkv_weight, out_weight, norm_gain)
    home, merge_grad, qkv_grad, out_grad, gain_grad = pl.pallas_call(
        widen,
        grid=(2,),
        out_shape=(
            shape((2, TOK, D)), shape((2, TOK, D), F32), shape((TOK, 3 * D), F32),
            shape((TOK, D), F32), shape((1, TOK), F32),
        ),
        in_specs=[
            pl.BlockSpec((2, 64, D), lambda i: (0, i, 0)),
            pl.BlockSpec((2, 64, WIDE), lambda i: (0, i, 0)),
            pl.BlockSpec((8, TOK), lambda i: (0, 0)),
        ],
        out_specs=[
            pl.BlockSpec((2, 64, D), lambda i: (0, i, 0)),
            pl.BlockSpec((2, 64, D), lambda i: (0, i, 0)),
            pl.BlockSpec((64, 3 * D), lambda i: (i, 0)),
            pl.BlockSpec((64, D), lambda i: (i, 0)),
            pl.BlockSpec((1, TOK), lambda i: (0, 0)),
        ],
        compiler_params=pltpu.CompilerParams(vmem_limit_bytes=VMEM_LIMIT),
        name="widen",
    )(home, total, gain_total)
    merge_grad = merge_grad.reshape(2 * TOK, D)
    section_home = home.reshape(1, 1, 2, 8, 16, D)
    return (section_home, merge_grad[None], qkv_grad[None], out_grad[None], gain_grad)


def solution(mesh):
    return jax.shard_map(
        body,
        mesh=mesh,
        in_specs=(
            P("dp", None, "band", None, None),
            P("dp", None, "band", None),
            P("segment", "dp", None),
            P("segment", "dp", None),
            P("segment", "dp", None),
            P("segment", "dp"),
            P("dp", None, "band", None, None),
        ),
        out_specs=(
            P("segment", "dp", None, "band", None, None),
            P("segment", "dp", None),
            P("segment", "dp", None),
            P("segment", "dp", None),
            P("segment", "dp"),
        ),
        check_vma=False,
    )
```

```python
import jax
import jax.numpy as jnp
from jax import lax
from jax.experimental import pallas as pl
from jax.experimental.pallas import tpu as pltpu
from jax.sharding import PartitionSpec as P

D = 512
HEADS = 8
NX = 4
NY = 4
NZ = 8
TOK = 128
HALF = 64
WIDE = 3 * D
PART = WIDE // NY
TALL = TOK // NZ
EPSILON = 1e-05
MASKED = -1e30
SENDS = 22
RECVS = 88
VMEM_LIMIT = 58 * 1024 * 1024
MESH = pl.DeviceIdType.MESH
BF = jnp.bfloat16
F32 = jnp.float32


def dot(left, right):
    return lax.dot_general(left, right, (((1,), (0,)), ((), ())), preferred_element_type=F32)


def dot_nt(left, right):
    return lax.dot_general(left, right, (((1,), (1,)), ((), ())), preferred_element_type=F32)


def dot_tn(left, right):
    return lax.dot_general(left, right, (((0,), (0,)), ((), ())), preferred_element_type=F32)


def span(index, size, unit=None):
    return pl.ds(pl.multiple_of(index, unit or size), size)


class Group:
    def __init__(self, sem, size_ref):
        self.sem, self.size_ref = sem, size_ref

    def wait(self):
        pltpu.make_async_copy(self.size_ref, self.size_ref, self.sem).wait()


class Hop:
    def __init__(self, net, src, dst, device, send, recv):
        if send is None:
            net.alone.append(self)
        self.copy = pltpu.make_async_remote_copy(
            src_ref=src,
            dst_ref=dst,
            send_sem=send.sem if send else net.send_sem(),
            recv_sem=recv.sem if recv else net.recv_sem(),
            device_id=device,
            device_id_type=MESH,
        )
        self.start = self.copy.start
        self.landed = self.copy.wait_recv
        self.sent = self.copy.wait_send


class Net:
    def __init__(self, send, recv, local):
        self.send, self.recv, self.local = send, recv, local
        self.sends = 0
        self.recvs = 0
        self.kept = 0
        self.alone = []
        self.groups = []

    def send_sem(self):
        self.sends += 1
        return self.send.at[self.sends - 1]

    def recv_sem(self):
        self.recvs += 1
        return self.recv.at[self.recvs - 1]

    def sending(self, size_ref):
        group = Group(self.send_sem(), size_ref)
        self.groups.append(group)
        return group

    def landing(self, size_ref):
        return Group(self.recv_sem(), size_ref)

    def hop(self, src, dst, device, send=None, recv=None):
        return Hop(self, src, dst, device, send, recv)

    def keep(self, src, dst):
        copy = pltpu.make_async_copy(src, dst, self.local.at[self.kept])
        self.kept += 1
        return copy

    def drain(self):
        for hop in self.alone:
            hop.sent()
        for group in self.groups:
            group.wait()


def start(hops):
    for hop in hops:
        hop.start()


def landed(hops):
    for hop in hops:
        hop.landed()


def add_into(count, step, dst, terms):
    def one(i, carry):
        at = i * step
        if len(terms) == 2:
            dst(at, terms[0](at) + terms[1](at))
        else:
            value = terms[0](at).astype(F32)
            for term in terms[1:]:
                value = value + term(at).astype(F32)
            dst(at, value.astype(BF))
        return carry

    lax.fori_loop(0, count // step, one, 0)


def block_rows(count, wide):
    return min(count, 49152 // wide // 16 * 16)


class Ring:
    def __init__(self, net, buf, rect, me, right, left, one_in, two_in, sent_ref):
        self.buf, self.one_in, self.two_in = buf, one_in, two_in
        step = [lax.rem(me + k, 4) for k in range(4)]
        self.rects = [rect(j) for j in step]
        self.nr, self.nc = self.rects[0][1], self.rects[0][3]
        far, after, before = self.rects[2], self.rects[1], self.rects[3]
        half = self.nr // 2
        top, bottom = pl.ds(0, half), pl.ds(half, half)
        out = net.sending(sent_ref)
        self.came = net.landing(two_in)
        self.one = [
            net.hop(self.view(far, 0, half), one_in.at[0], right, out),
            net.hop(self.view(far, half, half), one_in.at[1], left, out),
        ]
        self.plain = [
            net.hop(self.view(after, half, half), two_in.at[0, bottom], right, out, self.came),
            net.hop(self.view(before, 0, half), two_in.at[1, top], left, out, self.came),
        ]
        self.two = [
            net.hop(self.view(after, 0, half), two_in.at[0, top], right, out, self.came),
            net.hop(self.view(before, half, half), two_in.at[1, bottom], left, out, self.came),
        ]

    def at(self, rect, offset, count):
        r0, nr, c0, nc = rect
        first = pl.ds(offset, count) if isinstance(r0, int) and isinstance(offset, int) else span(r0 + offset, count, 16)
        second = pl.ds(0, nc) if isinstance(c0, int) else span(c0, nc, 128)
        return (first, second)

    def view(self, rect, offset, count):
        return self.buf.at[self.at(rect, offset, count)]

    def fold(self, which):
        self.one[which].landed()
        half = self.nr // 2
        rect, base = (self.rects[1], 0) if which == 0 else (self.rects[3], half)
        step = block_rows(half, self.nc)

        def store(i, value):
            self.buf[self.at(rect, base + i, step)] = value

        add_into(
            half,
            step,
            store,
            [lambda i: self.buf[self.at(rect, base + i, step)], lambda i: self.one_in[which, span(i, step, 16)]],
        )
        self.two[which].start()

    def finish(self, dst):
        self.came.wait()
        step = block_rows(self.nr, self.nc)

        def store(i, value):
            dst[span(i, step, 16)] = value

        add_into(
            self.nr,
            step,
            store,
            [
                lambda i: self.buf[self.at(self.rects[0], i, step)],
                lambda i: self.two_in[0, span(i, step, 16)],
                lambda i: self.two_in[1, span(i, step, 16)],
            ],
        )


class Direct:
    def __init__(self, net, buf, rect, me, peer, came_in):
        self.buf, self.came_in = buf, came_in
        self.mine = rect(me)
        out, self.came = net.sending(came_in), net.landing(came_in)
        self.hops = [
            net.hop(buf.at[self.index(rect(lax.rem(me + k, 4)), 0, None)], came_in.at[k - 1], peer(k), out, self.came)
            for k in range(1, 4)
        ]

    def index(self, rect, offset, count):
        r0, nr, c0, nc = rect
        count = count or nr
        first = pl.ds(offset, count) if isinstance(r0, int) and isinstance(offset, int) else span(r0 + offset, count, 16)
        second = pl.ds(0, nc) if isinstance(c0, int) else span(c0, nc, 128)
        return (first, second)

    def begin(self):
        for k in (2, 1, 3):
            self.hops[k - 1].start()

    def finish(self, dst):
        self.came.wait()
        step = block_rows(self.mine[1], self.mine[3])

        def store(i, value):
            dst[span(i, step, 16)] = value

        def term(k):
            return lambda i: self.came_in[k, span(i, step, 16)]

        add_into(
            self.mine[1],
            step,
            store,
            [lambda i: self.buf[self.index(self.mine, i, step)]] + [term(k) for k in range(3)],
        )


def x_dev(d, step):
    return {"dp": lax.rem(d + step, NX)}


def y_dev(b, step):
    z, y = b // NY, lax.rem(b, NY)
    return {"band": z * NY + lax.rem(y + step, NY)}


def z_dev(b, step):
    z, y = b // NY, lax.rem(b, NY)
    return {"band": lax.rem(z + step, NZ) * NY + y}


def z_near(b, step):
    z, y = b // NY, lax.rem(b, NY)
    return {"band": (z // 4 * 4 + lax.rem(lax.rem(z, 4) + step, 4)) * NY + y}


def barrier(devices):
    sem = pltpu.get_barrier_semaphore()
    for device in devices:
        pl.semaphore_signal(sem, inc=1, device_id=device, device_id_type=MESH)
    pl.semaphore_wait(sem, len(devices))


def kernel(x_in, g_in, use_in, wm_in, wq_in, wo_in, gain_in,
           y_home, total, gain_total,
           x_ref, cot_ref, use_ref, wm, wq, wo, gain,
           y_ref, normed_ref, hidden_ref, proj_ref, prob_ref, mix_ref, dproj_ref,
           grads, gain_grads, core_in,
           ax_one, ax_two, qy_one, qy_two, ay_in, qx_in, a_sum, q_sum,
           y_sum, z_in,
           gain_core, gain_sum, gain_x, gain_y, gain_z, send, recv, local):
    d = lax.axis_index("dp")
    s = lax.axis_index("segment")
    b = lax.axis_index("band")
    z, y = b // NY, lax.rem(b, NY)
    other = 1 - s
    bands = NY * NZ
    nxt, prev = lax.rem(b + 1, bands), lax.rem(b + bands - 1, bands)
    core = {"segment": other}
    x_right, x_left = x_dev(d, 1), x_dev(d, NX - 1)
    y_right, y_left = y_dev(b, 1), y_dev(b, NY - 1)
    net = Net(send, recv, local)
    lo, hi = pl.ds(0, HALF), pl.ds(HALF, HALF)
    xd = [lax.rem(d + k, NX) for k in range(NX)]
    yd = [lax.rem(y + k, NY) for k in range(NY)]

    barrier(
        [core]
        + [x_dev(d, k) for k in range(1, NX)]
        + [y_dev(b, k) for k in range(1, NY)]
        + [z_dev(b, k) for k in range(1, NZ)]
        + [{"band": nxt}, {"band": prev}]
        + [{"band": nxt, "segment": other}, {"band": prev, "segment": other}]
    )

    shift = [
        net.hop(x_in.at[s, lo], x_ref.at[hi], {"band": prev}),
        net.hop(use_in.at[s], use_ref.at[1], {"band": prev}),
        net.hop(g_in.at[s, lo], cot_ref.at[hi], {"band": prev}),
    ]
    own = [
        net.keep(x_in.at[s, hi], x_ref.at[lo]),
        net.keep(use_in.at[s], use_ref.at[0]),
        net.keep(g_in.at[s, hi], cot_ref.at[lo]),
    ]
    gain[s, d] = jnp.broadcast_to(gain_in[...].astype(F32), (8, TOK))
    seven = gain_z.at[pl.ds(0, 7)]
    gain_out, gain_in_all = net.sending(seven), net.landing(gain.at[0, pl.ds(0, 3)])
    gain_in_core = net.landing(gain.at[0])
    gain_hops = [
        net.hop(gain.at[s, d], gain.at[s, d], x_dev(d, k), gain_out, gain_in_all) for k in range(1, NX)
    ]
    gain_core_hops = [net.hop(gain.at[s, xd[0]], gain.at[s, xd[0]], core, gain_out, gain_in_core)] + [
        net.hop(gain.at[s, xd[NX - k]], gain.at[s, xd[NX - k]], core, gain_out, gain_in_core)
        for k in range(1, NX)
    ]

    class Gather:
        def __init__(self, src, dst, size, sent_ref):
            wide = dst.shape[-1] // 4
            half, quarter, eighth = size // 2, size // 4, size // 8

            def block(owner, offset, count):
                return dst.at[s, span(owner * size + offset, count, count)]

            def y_strip(owner):
                return dst.at[s, span(owner * size + quarter, half, quarter), span(y * wide, wide)]

            def z_strip(owner):
                return dst.at[
                    s, span(owner * size + 3 * quarter, quarter), span(lax.rem(z, 4) * wide, wide)
                ]

            top = pl.ds(0, quarter)
            y_src = src.at[0, pl.ds(quarter, half), span(y * wide, wide)]
            z_src = src.at[0, pl.ds(3 * quarter, quarter), span(lax.rem(z, 4) * wide, wide)]
            out = net.sending(sent_ref)
            self.y_strips = [net.hop(y_src, y_strip(d), x_dev(d, k), out) for k in range(1, NX)]
            self.z_strips = [net.hop(z_src, z_strip(d), x_dev(d, k), out) for k in range(1, NX)]
            self.right = net.hop(src.at[0, top], block(d, 0, quarter), x_right, out)
            self.left = net.hop(src.at[0, top], block(d, 0, quarter), x_left, out)
            self.from_core = net.landing(dst.at[0])
            self.mine = net.hop(src.at[0], block(d, 0, size), core, out, self.from_core)
            self.local = net.keep(src.at[0], block(d, 0, size))
            owners = [xd[NX - k] for k in range(1, NX)]
            others = pl.ds(0, 3 * wide)
            self.y_came = [net.landing(dst.at[0, pl.ds(0, half), others]) for o in owners]
            self.z_came = [net.landing(dst.at[0, pl.ds(0, quarter), others]) for o in owners]
            self.y_spread = [
                [net.hop(y_strip(o), y_strip(o), y_dev(b, m), out, came) for m in range(1, NY)]
                for o, came in zip(owners, self.y_came)
            ]
            self.z_spread = [
                [net.hop(z_strip(o), z_strip(o), z_near(b, m), out, came) for m in range(1, 4)]
                for o, came in zip(owners, self.z_came)
            ]
            self.far_right = net.hop(block(xd[3], 0, eighth), block(xd[3], 0, eighth), x_right, out)
            self.far_left = net.hop(block(xd[1], eighth, eighth), block(xd[1], eighth, eighth), x_left, out)
            self.across = [
                net.hop(block(o, 0, size), block(o, 0, size), core, out, self.from_core)
                for o in owners
            ]

        def begin_strips(self):
            for k in (2, 1, 3):
                self.y_strips[k - 1].start()
                self.z_strips[k - 1].start()

        def begin_blocks(self):
            start([self.right, self.left, self.mine])
            self.local.start()

        def relay_strips(self):
            for k in (1, 3, 2):
                self.y_strips[k - 1].landed()
                start(self.y_spread[k - 1])
                self.z_strips[k - 1].landed()
                start(self.z_spread[k - 1])

        def relay(self):
            self.right.landed()
            self.far_right.start()
            self.left.landed()
            self.far_left.start()

        def pass_on(self):
            for k in (1, 3, 2):
                self.y_came[k - 1].wait()
                self.z_came[k - 1].wait()
                if k == 2:
                    landed([self.far_right, self.far_left])
                self.across[k - 1].start()

        def ready(self):
            self.from_core.wait()
            self.local.wait()

    merge = Gather(wm_in, wm, 2 * TOK, grads.at[:, :, pl.ds(0, 448), pl.ds(0, D)])
    qkv = Gather(wq_in, wq, TOK, grads.at[0, :, pl.ds(0, 448)])
    outw = Gather(wo_in, wo, TOK, grads.at[0, :, pl.ds(0, 448), pl.ds(0, D)])

    mine = grads.at[s]
    theirs = grads.at[other]
    a_order = [xd[k] for k in (2, 1, 3, 0)]
    q_order = [yd[k] for k in (2, 1, 3, 0)]

    def a_rows(j):
        return (0, span(j * TOK, TOK))

    def q_cols(j):
        return (1, pl.ds(0, D), span(j * PART, PART, 128))

    out = net.sending(core_in)
    swap_a = [net.hop(theirs.at[a_rows(j)], core_in.at[a_rows(j)], core, out) for j in a_order]
    swap_q = [net.hop(theirs.at[q_cols(j)], core_in.at[q_cols(j)], core, out) for j in q_order]
    gain_swap = net.hop(gain_grads.at[other], gain_core, core)
    ring_ax = Ring(net, mine.at[0], lambda j: (j * TOK, TOK, 0, WIDE), d, x_right, x_left, ax_one, ax_two,
                   core_in.at[0, pl.ds(0, 3 * TOK)])
    ring_qy = Ring(net, mine.at[1], lambda j: (0, D, j * PART, PART), y, y_right, y_left, qy_one, qy_two,
                   core_in.at[0, :, pl.ds(0, 3 * PART)])
    to_ay = Direct(net, a_sum, lambda j: (0, TOK, j * PART, PART), y, lambda k: y_dev(b, k), ay_in)
    to_qx = Direct(net, q_sum, lambda j: (j * TOK, TOK, 0, PART), d, lambda k: x_dev(d, k), qx_in)
    three = gain_x.at[pl.ds(0, 3)]
    out, gain_x_in = net.sending(three), net.landing(three)
    gain_x_hops = [
        net.hop(gain_sum.at[xd[k]], gain_x.at[k], x_dev(d, k), out, gain_x_in) for k in range(1, NX)
    ]
    out, gain_y_in = net.sending(three), net.landing(three)
    gain_y_hops = [
        net.hop(gain_y.at[0], gain_y.at[k], y_dev(b, k), out, gain_y_in) for k in range(1, NY)
    ]
    out, gain_z_in = net.sending(seven), net.landing(seven)
    gain_z_hops = [
        net.hop(gain_z.at[0], gain_z.at[k], z_dev(b, k), out, gain_z_in) for k in range(1, NZ)
    ]
    z_rows = span(z * TALL, TALL)
    both = pl.ds(0, 2)
    seven_pieces = z_in.at[pl.ds(0, 7)]
    out, z_came = net.sending(seven_pieces), net.landing(seven_pieces)
    z_hops = [
        [
            net.hop(
                y_sum.at[which, span(lax.rem(z + k, NZ) * TALL, TALL)], z_in.at[k, which],
                z_dev(b, k), out, z_came,
            )
            for k in (4, 3, 5, 2, 6, 1, 7)[-(NZ - 1):]
        ]
        for which in (0, 1)
    ]
    def piece(k):
        at = (both, span(lax.rem(z + NZ - k, NZ) * TALL, TALL), span(y * PART, PART, 128))
        return total.at[at]

    out = net.sending(seven_pieces)
    z_back = [net.hop(piece(0), piece(0), z_dev(b, k), out) for k in range(1, NZ)]
    three_parts = total.at[both, pl.ds(0, TOK), pl.ds(0, 3 * PART)]
    out, y_came = net.sending(three_parts), net.landing(three_parts)
    y_back = [
        [net.hop(piece(k), piece(k), y_dev(b, m), out, y_came) for m in range(1, NY)]
        for k in range(NZ)
    ]
    home = [
        net.hop(y_ref.at[other, lo], y_home.at[s, hi], core),
        net.hop(y_ref.at[s, hi], y_home.at[s, lo], {"band": nxt}),
        net.hop(y_ref.at[other, hi], y_home.at[s, lo], {"band": nxt, "segment": other}),
    ]
    stays = net.keep(y_ref.at[s, lo], y_home.at[s, hi])

    def core_sum(where, count, wide):
        step = block_rows(count, wide)

        def store(r, value):
            mine[where(r, step)] = value

        add_into(
            count, step, store, [lambda r: mine[where(r, step)], lambda r: core_in[where(r, step)]]
        )

    def a_core(i):
        swap_a[i].landed()
        core_sum(lambda r, step: (0, span(a_order[i] * TOK + r, step, 16)), TOK, WIDE)

    def q_core(i):
        swap_q[i].landed()
        core_sum(lambda r, step: (1, span(r, step, 16), span(q_order[i] * PART, PART, 128)), D, PART)

    def swap():
        for hop_a, hop_q in zip(swap_a, swap_q):
            hop_a.start()
            hop_q.start()
        gain_swap.start()

    def stage1():
        a_core(0)
        start(ring_ax.one)
        q_core(0)
        start(ring_qy.one)
        for i in (1, 2):
            a_core(i)
            ring_ax.plain[i - 1].start()
            q_core(i)
            ring_qy.plain[i - 1].start()
        gain_swap.landed()
        gain_sum[...] = gain_grads[s] + gain_core[...]
        gain_x[0] = gain_sum[d]
        start(gain_x_hops)

    def stage2():
        for which in (0, 1):
            ring_ax.fold(which)
            ring_qy.fold(which)
        a_core(3)
        q_core(3)
        gain_x_in.wait()
        gain_y[0] = (gain_x[0] + gain_x[1]) + (gain_x[2] + gain_x[3])
        start(gain_y_hops)

    def stage3():
        ring_ax.finish(a_sum)
        to_ay.begin()
        ring_qy.finish(q_sum)
        to_qx.begin()
        gain_y_in.wait()
        gain_z[0] = (gain_y[0] + gain_y[1]) + (gain_y[2] + gain_y[3])
        start(gain_z_hops)

    def masks():
        lane = lax.broadcasted_iota(jnp.int32, (16, TOK), 1)
        sub = lax.broadcasted_iota(jnp.int32, (16, TOK), 0)
        spread = (lane % 16 == sub).astype(F32).astype(BF)
        lane8 = lax.broadcasted_iota(jnp.int32, (8, TOK), 1) // 16
        sub8 = lax.broadcasted_iota(jnp.int32, (8, TOK), 0)
        here = dot((use_ref[0] == 1).astype(F32).astype(BF), spread)
        there = dot((use_ref[1] == 1).astype(F32).astype(BF), spread)
        usable = jnp.sum(
            jnp.where(lane8 + 4 == sub8, here, 0.0) + jnp.where(lane8 - 4 == sub8, there, 0.0),
            axis=0, keepdims=True,
        )
        query = lax.broadcasted_iota(jnp.int32, (TOK, TOK), 0)
        key = lax.broadcasted_iota(jnp.int32, (TOK, TOK), 1)
        same_lon = (query % 16 // 8) == (key % 16 // 8)
        same_lat = ((query // HALF) == (key // HALF)) | jnp.logical_not(b == bands - 1)
        open_key = jnp.broadcast_to(usable, (TOK, TOK)) > 0.5
        return same_lon & same_lat & (open_key | (query == key))

    first = lax.broadcasted_iota(jnp.int32, (TOK, TOK), 1) < HALF
    zero = jnp.zeros((TOK, TOK), F32)
    head0 = jnp.where(first, zero + 1.0, zero).astype(BF)
    head1 = jnp.where(first, zero, zero + 1.0).astype(BF)

    def pair_cat(values):
        return jnp.concatenate([values * head0, values * head1], axis=0)

    def gain_row(sec):
        return jnp.concatenate([gain[sec, j][0:1] for j in range(4)], axis=1)

    def tile(sec, which, i):
        return proj_ref[sec, :, which * D + TOK * i : which * D + TOK * (i + 1)]

    def forward_merge(sec, x):
        update = dot(x, wm[sec, 0:D]) + dot(x, wm[sec, D : 2 * D])
        average = jnp.mean(update, axis=-1, keepdims=True)
        centered = update - average
        spread = jnp.mean(centered * centered, axis=-1, keepdims=True)
        inverse = lax.rsqrt(spread + EPSILON)
        normed = centered * inverse
        normed_ref[sec] = normed
        hidden_ref[sec] = (normed * gain_row(sec)).astype(BF)
        return update, inverse

    def forward_attend(sec, allowed):
        proj_ref[sec] = dot(hidden_ref[sec], wq[sec]).astype(BF)
        for i in range(HEADS // 2):
            scores = dot_nt(tile(sec, 0, i), pair_cat(tile(sec, 1, i))) * 0.125
            probs = []
            for h in range(2):
                one = jnp.where(allowed, scores[:, TOK * h : TOK * (h + 1)], MASKED)
                weights = jnp.exp(one - jnp.max(one, axis=-1, keepdims=True))
                probs.append(weights / jnp.sum(weights, axis=-1, keepdims=True))
            prob = jnp.concatenate(probs, axis=1).astype(BF)
            prob_ref[sec, i] = prob
            mix_ref[sec, :, TOK * i : TOK * (i + 1)] = dot(prob, pair_cat(tile(sec, 2, i))).astype(BF)

    def forward_out(sec, update):
        result = (update + dot(mix_ref[sec], wo[sec])).astype(BF)
        y_ref[sec] = result
        return result

    def backward_attend(sec, g):
        gm = dot_nt(g, wo[sec]).astype(BF)
        for i in range(HEADS // 2):
            q, k, v = tile(sec, 0, i), tile(sec, 1, i), tile(sec, 2, i)
            gm_pair = gm[:, TOK * i : TOK * (i + 1)]
            prob = prob_ref[sec, i]
            dprob = dot_nt(gm_pair, pair_cat(v))
            pieces = []
            for h in range(2):
                half = slice(TOK * h, TOK * (h + 1))
                p = prob[:, half].astype(F32)
                dp = dprob[:, half]
                pieces.append(p * (dp - jnp.sum(dp * p, axis=-1, keepdims=True)) * 0.125)
            dscore = jnp.concatenate(pieces, axis=1).astype(BF)
            dk = dot_tn(dscore, q)
            dv = dot_tn(prob, gm_pair)
            dproj_ref[:, TOK * i : TOK * (i + 1)] = dot(dscore, pair_cat(k)).astype(BF)
            dproj_ref[:, D + TOK * i : D + TOK * (i + 1)] = jnp.where(first, dk[:TOK], dk[TOK:]).astype(BF)
            dproj_ref[:, 2 * D + TOK * i : 2 * D + TOK * (i + 1)] = jnp.where(first, dv[:TOK], dv[TOK:]).astype(BF)

    def backward_terms(sec, x, g, inverse):
        dhidden = dot_nt(dproj_ref[...], wq[sec])
        normed = normed_ref[sec]
        dgain = jnp.sum(dhidden * normed, axis=0, keepdims=True)
        for j in range(4):
            gain_grads[sec, j] = jnp.broadcast_to(dgain[:, TOK * j : TOK * (j + 1)], (8, TOK))
        dnormed = dhidden * gain_row(sec)
        gu = (
            g.astype(F32)
            + inverse
            * (
                dnormed
                - jnp.mean(dnormed, axis=-1, keepdims=True)
                - normed * jnp.mean(dnormed * normed, axis=-1, keepdims=True)
            )
        ).astype(BF)
        for c in range(4):
            part = slice(TOK * c, TOK * (c + 1))
            grads[sec, 1, part] = dot_tn(hidden_ref[sec, :, part], dproj_ref[...]).astype(BF)
            grads[sec, 0, part, 2 * D : 3 * D] = dot_tn(mix_ref[sec, :, part], g).astype(BF)
            term = dot_tn(x[:, part], gu).astype(BF)
            for j in (c // 2, c // 2 + 2):
                grads[sec, 0, TOK * j : TOK * (j + 1), D * (c % 2) : D * (c % 2 + 1)] = term
        return gu

    for part in (merge, qkv, outw):
        part.begin_strips()
    start(shift[:2] + gain_hops + gain_core_hops[:1])
    for part in (merge, qkv, outw):
        part.begin_blocks()
    for copy in own:
        copy.start()
    shift[2].start()
    for part in (merge, qkv, outw):
        part.relay_strips()
    for part in (merge, qkv, outw):
        part.relay()
    gain_in_all.wait()
    start(gain_core_hops[1:])
    merge.pass_on()
    qkv.pass_on()
    gain_in_core.wait()
    landed(shift)
    for copy in own:
        copy.wait()
    allowed = masks()
    x0 = x_ref[...]
    merge.ready()
    update0, inverse0 = forward_merge(0, x0)
    outw.pass_on()
    qkv.ready()
    forward_attend(0, allowed)
    outw.ready()
    y0 = forward_out(0, update0)
    update1, inverse1 = forward_merge(1, y0)
    forward_attend(1, allowed)
    forward_out(1, update1)
    start(home)
    stays.start()
    cot = cot_ref[...]
    backward_attend(1, cot)
    gu1 = backward_terms(1, y0, cot, inverse1)

    @pl.when(s == 0)
    def _():
        swap()

    chain = dot_nt(gu1, wm[1, 0:D]).astype(BF).astype(F32)
    side = dot_nt(gu1, wm[1, D : 2 * D]).astype(BF).astype(F32)
    g0 = (chain + side).astype(BF)

    backward_attend(0, g0)
    backward_terms(0, x0, g0, inverse0)

    @pl.when(s == 1)
    def _():
        swap()
        stage1()
        stage2()
        stage3()

    @pl.when(s == 0)
    def _():
        stage1()
        stage2()
        stage3()

    to_ay.finish(y_sum.at[0])
    start(z_hops[0])
    to_qx.finish(y_sum.at[1])
    start(z_hops[1])
    value = y_sum[both, z_rows].astype(F32)
    z_came.wait()
    for k in range(1, NZ):
        value = value + z_in[k].astype(F32)
    total[both, z_rows, span(y * PART, PART, 128)] = value.astype(BF)
    start(z_back)
    start(y_back[0])
    gain_z_in.wait()
    gain_value = gain_z[0]
    for k in range(1, NZ):
        gain_value = gain_value + gain_z[k]
    gain_total[...] = gain_value
    for k in (1, 7, 2, 6, 3, 5, 4):
        if k < NZ:
            z_back[k - 1].landed()
            start(y_back[k])
    landed(home)
    stays.wait()
    y_came.wait()
    net.drain()


def widen(home_in, total, gain_in, home, merge, qkv, out, gain):
    home[...] = home_in[...]
    merge[0] = total[0, :, 0:D].astype(F32)
    merge[1] = total[0, :, D : 2 * D].astype(F32)
    out[...] = total[0, :, 2 * D : 3 * D].astype(F32)
    qkv[...] = total[1].astype(F32)
    gain[...] = gain_in[0:1]


def vmem(count):
    return [pl.BlockSpec(memory_space=pltpu.VMEM)] * count


def anywhere(count):
    return [pl.BlockSpec(memory_space=pl.ANY)] * count


def shape(dims, dtype=BF):
    return jax.ShapeDtypeStruct(dims, dtype)


def body(fields, cell_mask, merge_weight, qkv_weight, out_weight, norm_gain, out_cotangent):
    x_in = fields.reshape(2, TOK, D)
    g_in = out_cotangent.reshape(2, TOK, D)
    use = cell_mask.reshape(2, 8, 16)
    home, total, gain_total = pl.pallas_call(
        kernel,
        out_shape=(shape((2, TOK, D)), shape((2, TOK, WIDE)), shape((8, TOK), F32)),
        in_specs=anywhere(6) + vmem(1),
        out_specs=vmem(3),
        scratch_shapes=[
            pltpu.VMEM((TOK, D), BF),
            pltpu.VMEM((TOK, D), BF),
            pltpu.VMEM((2, 8, 16), jnp.int32),
            pltpu.VMEM((2, 2 * D, D), BF),
            pltpu.VMEM((2, D, 3 * D), BF),
            pltpu.VMEM((2, D, D), BF),
            pltpu.VMEM((2, 4, 8, TOK), F32),
            pltpu.VMEM((2, TOK, D), BF),
            pltpu.VMEM((2, TOK, D), F32),
            pltpu.VMEM((2, TOK, D), BF),
            pltpu.VMEM((2, TOK, 3 * D), BF),
            pltpu.VMEM((2, HEADS // 2, TOK, 2 * TOK), BF),
            pltpu.VMEM((2, TOK, D), BF),
            pltpu.VMEM((TOK, 3 * D), BF),
            pltpu.VMEM((2, 2, D, WIDE), BF),
            pltpu.VMEM((2, 4, 8, TOK), F32),
            pltpu.VMEM((2, D, WIDE), BF),
            pltpu.VMEM((2, HALF, WIDE), BF),
            pltpu.VMEM((2, TOK, WIDE), BF),
            pltpu.VMEM((2, D // 2, PART), BF),
            pltpu.VMEM((2, D, PART), BF),
            pltpu.VMEM((3, TOK, PART), BF),
            pltpu.VMEM((3, TOK, PART), BF),
            pltpu.VMEM((TOK, WIDE), BF),
            pltpu.VMEM((D, PART), BF),
            pltpu.VMEM((2, TOK, PART), BF),
            pltpu.VMEM((NZ, 2, TALL, PART), BF),
            pltpu.VMEM((4, 8, TOK), F32),
            pltpu.VMEM((4, 8, TOK), F32),
            pltpu.VMEM((4, 8, TOK), F32),
            pltpu.VMEM((NY, 8, TOK), F32),
            pltpu.VMEM((NZ, 8, TOK), F32),
            pltpu.SemaphoreType.DMA((SENDS,)),
            pltpu.SemaphoreType.DMA((RECVS,)),
            pltpu.SemaphoreType.DMA((7,)),
        ],
        compiler_params=pltpu.CompilerParams(
            collective_id=0, has_side_effects=True, vmem_limit_bytes=VMEM_LIMIT
        ),
        name="step",
    )(x_in, g_in, use, merge_weight, qkv_weight, out_weight, norm_gain)
    home, merge_grad, qkv_grad, out_grad, gain_grad = pl.pallas_call(
        widen,
        grid=(2,),
        out_shape=(
            shape((2, TOK, D)), shape((2, TOK, D), F32), shape((TOK, 3 * D), F32),
            shape((TOK, D), F32), shape((1, TOK), F32),
        ),
        in_specs=[
            pl.BlockSpec((2, 64, D), lambda i: (0, i, 0)),
            pl.BlockSpec((2, 64, WIDE), lambda i: (0, i, 0)),
            pl.BlockSpec((8, TOK), lambda i: (0, 0)),
        ],
        out_specs=[
            pl.BlockSpec((2, 64, D), lambda i: (0, i, 0)),
            pl.BlockSpec((2, 64, D), lambda i: (0, i, 0)),
            pl.BlockSpec((64, 3 * D), lambda i: (i, 0)),
            pl.BlockSpec((64, D), lambda i: (i, 0)),
            pl.BlockSpec((1, TOK), lambda i: (0, 0)),
        ],
        compiler_params=pltpu.CompilerParams(vmem_limit_bytes=VMEM_LIMIT),
        name="widen",
    )(home, total, gain_total)
    merge_grad = merge_grad.reshape(2 * TOK, D)
    section_home = home.reshape(1, 1, 2, 8, 16, D)
    return (section_home, merge_grad[None], qkv_grad[None], out_grad[None], gain_grad)


def solution(mesh):
    return jax.shard_map(
        body,
        mesh=mesh,
        in_specs=(
            P("dp", None, "band", None, None),
            P("dp", None, "band", None),
            P("segment", "dp", None),
            P("segment", "dp", None),
            P("segment", "dp", None),
            P("segment", "dp"),
            P("dp", None, "band", None, None),
        ),
        out_specs=(
            P("segment", "dp", None, "band", None, None),
            P("segment", "dp", None),
            P("segment", "dp", None),
            P("segment", "dp", None),
            P("segment", "dp"),
        ),
        check_vma=False,
    )
```

```python
import jax
import jax.numpy as jnp
from jax import lax
from jax.experimental import pallas as pl
from jax.experimental.pallas import tpu as pltpu
from jax.sharding import PartitionSpec as P

D = 512
HEADS = 8
NX = 4
NY = 4
NZ = 8
TOK = 128
HALF = 64
WIDE = 3 * D
PART = WIDE // NY
TALL = TOK // NZ
EPSILON = 1e-05
MASKED = -1e30
SENDS = 22
RECVS = 88
VMEM_LIMIT = 58 * 1024 * 1024
MESH = pl.DeviceIdType.MESH
BF = jnp.bfloat16
F32 = jnp.float32


def dot(left, right):
    return lax.dot_general(left, right, (((1,), (0,)), ((), ())), preferred_element_type=F32)


def dot_nt(left, right):
    return lax.dot_general(left, right, (((1,), (1,)), ((), ())), preferred_element_type=F32)


def dot_tn(left, right):
    return lax.dot_general(left, right, (((0,), (0,)), ((), ())), preferred_element_type=F32)


def span(index, size, unit=None):
    return pl.ds(pl.multiple_of(index, unit or size), size)


class Group:
    def __init__(self, sem, size_ref):
        self.sem, self.size_ref = sem, size_ref

    def wait(self):
        pltpu.make_async_copy(self.size_ref, self.size_ref, self.sem).wait()


class Hop:
    def __init__(self, net, src, dst, device, send, recv):
        if send is None:
            net.alone.append(self)
        self.copy = pltpu.make_async_remote_copy(
            src_ref=src,
            dst_ref=dst,
            send_sem=send.sem if send else net.send_sem(),
            recv_sem=recv.sem if recv else net.recv_sem(),
            device_id=device,
            device_id_type=MESH,
        )
        self.start = self.copy.start
        self.landed = self.copy.wait_recv
        self.sent = self.copy.wait_send


class Net:
    def __init__(self, send, recv, local):
        self.send, self.recv, self.local = send, recv, local
        self.sends = 0
        self.recvs = 0
        self.kept = 0
        self.alone = []
        self.groups = []

    def send_sem(self):
        self.sends += 1
        return self.send.at[self.sends - 1]

    def recv_sem(self):
        self.recvs += 1
        return self.recv.at[self.recvs - 1]

    def sending(self, size_ref):
        group = Group(self.send_sem(), size_ref)
        self.groups.append(group)
        return group

    def landing(self, size_ref):
        return Group(self.recv_sem(), size_ref)

    def hop(self, src, dst, device, send=None, recv=None):
        return Hop(self, src, dst, device, send, recv)

    def keep(self, src, dst):
        copy = pltpu.make_async_copy(src, dst, self.local.at[self.kept])
        self.kept += 1
        return copy

    def drain(self):
        for hop in self.alone:
            hop.sent()
        for group in self.groups:
            group.wait()


def start(hops):
    for hop in hops:
        hop.start()


def landed(hops):
    for hop in hops:
        hop.landed()


def add_into(count, step, dst, terms):
    def one(i, carry):
        at = i * step
        if len(terms) == 2:
            dst(at, terms[0](at) + terms[1](at))
        else:
            value = terms[0](at).astype(F32)
            for term in terms[1:]:
                value = value + term(at).astype(F32)
            dst(at, value.astype(BF))
        return carry

    lax.fori_loop(0, count // step, one, 0)


def block_rows(count, wide):
    return min(count, 49152 // wide // 16 * 16)


class Ring:
    def __init__(self, net, buf, rect, me, right, left, one_in, two_in, sent_ref):
        self.buf, self.one_in, self.two_in = buf, one_in, two_in
        step = [lax.rem(me + k, 4) for k in range(4)]
        self.rects = [rect(j) for j in step]
        self.nr, self.nc = self.rects[0][1], self.rects[0][3]
        far, after, before = self.rects[2], self.rects[1], self.rects[3]
        half = self.nr // 2
        top, bottom = pl.ds(0, half), pl.ds(half, half)
        out = net.sending(sent_ref)
        self.came = net.landing(two_in)
        self.one = [
            net.hop(self.view(far, 0, half), one_in.at[0], right, out),
            net.hop(self.view(far, half, half), one_in.at[1], left, out),
        ]
        self.plain = [
            net.hop(self.view(after, half, half), two_in.at[0, bottom], right, out, self.came),
            net.hop(self.view(before, 0, half), two_in.at[1, top], left, out, self.came),
        ]
        self.two = [
            net.hop(self.view(after, 0, half), two_in.at[0, top], right, out, self.came),
            net.hop(self.view(before, half, half), two_in.at[1, bottom], left, out, self.came),
        ]

    def at(self, rect, offset, count):
        r0, nr, c0, nc = rect
        first = pl.ds(offset, count) if isinstance(r0, int) and isinstance(offset, int) else span(r0 + offset, count, 16)
        second = pl.ds(0, nc) if isinstance(c0, int) else span(c0, nc, 128)
        return (first, second)

    def view(self, rect, offset, count):
        return self.buf.at[self.at(rect, offset, count)]

    def fold(self, which):
        self.one[which].landed()
        half = self.nr // 2
        rect, base = (self.rects[1], 0) if which == 0 else (self.rects[3], half)
        step = block_rows(half, self.nc)

        def store(i, value):
            self.buf[self.at(rect, base + i, step)] = value

        add_into(
            half,
            step,
            store,
            [lambda i: self.buf[self.at(rect, base + i, step)], lambda i: self.one_in[which, span(i, step, 16)]],
        )
        self.two[which].start()

    def finish(self, dst):
        self.came.wait()
        step = block_rows(self.nr, self.nc)

        def store(i, value):
            dst[span(i, step, 16)] = value

        add_into(
            self.nr,
            step,
            store,
            [
                lambda i: self.buf[self.at(self.rects[0], i, step)],
                lambda i: self.two_in[0, span(i, step, 16)],
                lambda i: self.two_in[1, span(i, step, 16)],
            ],
        )


class Direct:
    def __init__(self, net, buf, rect, me, peer, came_in):
        self.buf, self.came_in = buf, came_in
        self.mine = rect(me)
        out, self.came = net.sending(came_in), net.landing(came_in)
        self.hops = [
            net.hop(buf.at[self.index(rect(lax.rem(me + k, 4)), 0, None)], came_in.at[k - 1], peer(k), out, self.came)
            for k in range(1, 4)
        ]

    def index(self, rect, offset, count):
        r0, nr, c0, nc = rect
        count = count or nr
        first = pl.ds(offset, count) if isinstance(r0, int) and isinstance(offset, int) else span(r0 + offset, count, 16)
        second = pl.ds(0, nc) if isinstance(c0, int) else span(c0, nc, 128)
        return (first, second)

    def begin(self):
        for k in (2, 1, 3):
            self.hops[k - 1].start()

    def finish(self, dst):
        self.came.wait()
        step = block_rows(self.mine[1], self.mine[3])

        def store(i, value):
            dst[span(i, step, 16)] = value

        def term(k):
            return lambda i: self.came_in[k, span(i, step, 16)]

        add_into(
            self.mine[1],
            step,
            store,
            [lambda i: self.buf[self.index(self.mine, i, step)]] + [term(k) for k in range(3)],
        )


def x_dev(d, step):
    return {"dp": lax.rem(d + step, NX)}


def y_dev(b, step):
    z, y = b // NY, lax.rem(b, NY)
    return {"band": z * NY + lax.rem(y + step, NY)}


def z_dev(b, step):
    z, y = b // NY, lax.rem(b, NY)
    return {"band": lax.rem(z + step, NZ) * NY + y}


def z_near(b, step):
    z, y = b // NY, lax.rem(b, NY)
    return {"band": (z // 4 * 4 + lax.rem(lax.rem(z, 4) + step, 4)) * NY + y}


def barrier(devices):
    sem = pltpu.get_barrier_semaphore()
    for device in devices:
        pl.semaphore_signal(sem, inc=1, device_id=device, device_id_type=MESH)
    pl.semaphore_wait(sem, len(devices))


def kernel(x_in, g_in, use_in, wm_in, wq_in, wo_in, gain_in,
           y_home, total, gain_total,
           x_ref, cot_ref, use_ref, wm, wq, wo, gain,
           y_ref, normed_ref, hidden_ref, proj_ref, prob_ref, mix_ref, dproj_ref,
           grads, gain_grads, core_in,
           ax_one, ax_two, qy_one, qy_two, ay_in, qx_in, a_sum, q_sum,
           y_sum, z_in,
           gain_core, gain_sum, gain_x, gain_y, gain_z, send, recv, local):
    d = lax.axis_index("dp")
    s = lax.axis_index("segment")
    b = lax.axis_index("band")
    z, y = b // NY, lax.rem(b, NY)
    other = 1 - s
    bands = NY * NZ
    nxt, prev = lax.rem(b + 1, bands), lax.rem(b + bands - 1, bands)
    core = {"segment": other}
    x_right, x_left = x_dev(d, 1), x_dev(d, NX - 1)
    y_right, y_left = y_dev(b, 1), y_dev(b, NY - 1)
    net = Net(send, recv, local)
    lo, hi = pl.ds(0, HALF), pl.ds(HALF, HALF)
    xd = [lax.rem(d + k, NX) for k in range(NX)]
    yd = [lax.rem(y + k, NY) for k in range(NY)]

    barrier(
        [core]
        + [x_dev(d, k) for k in range(1, NX)]
        + [y_dev(b, k) for k in range(1, NY)]
        + [z_dev(b, k) for k in range(1, NZ)]
        + [{"band": nxt}, {"band": prev}]
        + [{"band": nxt, "segment": other}, {"band": prev, "segment": other}]
    )

    shift = [
        net.hop(x_in.at[s, lo], x_ref.at[hi], {"band": prev}),
        net.hop(use_in.at[s], use_ref.at[1], {"band": prev}),
        net.hop(g_in.at[s, lo], cot_ref.at[hi], {"band": prev}),
    ]
    own = [
        net.keep(x_in.at[s, hi], x_ref.at[lo]),
        net.keep(use_in.at[s], use_ref.at[0]),
        net.keep(g_in.at[s, hi], cot_ref.at[lo]),
    ]
    gain[s, d] = jnp.broadcast_to(gain_in[...].astype(F32), (8, TOK))
    seven = gain_z.at[pl.ds(0, 7)]
    gain_out, gain_in_all = net.sending(seven), net.landing(gain.at[0, pl.ds(0, 3)])
    gain_in_core = net.landing(gain.at[0])
    gain_hops = [
        net.hop(gain.at[s, d], gain.at[s, d], x_dev(d, k), gain_out, gain_in_all) for k in range(1, NX)
    ]
    gain_core_hops = [net.hop(gain.at[s, xd[0]], gain.at[s, xd[0]], core, gain_out, gain_in_core)] + [
        net.hop(gain.at[s, xd[NX - k]], gain.at[s, xd[NX - k]], core, gain_out, gain_in_core)
        for k in range(1, NX)
    ]

    class Gather:
        def __init__(self, src, dst, size, sent_ref):
            wide = dst.shape[-1] // 4
            half, quarter, eighth = size // 2, size // 4, size // 8

            def block(owner, offset, count):
                return dst.at[s, span(owner * size + offset, count, count)]

            def y_strip(owner):
                return dst.at[s, span(owner * size + quarter, half, quarter), span(y * wide, wide)]

            def z_strip(owner):
                return dst.at[
                    s, span(owner * size + 3 * quarter, quarter), span(lax.rem(z, 4) * wide, wide)
                ]

            top = pl.ds(0, quarter)
            y_src = src.at[0, pl.ds(quarter, half), span(y * wide, wide)]
            z_src = src.at[0, pl.ds(3 * quarter, quarter), span(lax.rem(z, 4) * wide, wide)]
            out = net.sending(sent_ref)
            self.y_strips = [net.hop(y_src, y_strip(d), x_dev(d, k), out) for k in range(1, NX)]
            self.z_strips = [net.hop(z_src, z_strip(d), x_dev(d, k), out) for k in range(1, NX)]
            self.right = net.hop(src.at[0, top], block(d, 0, quarter), x_right, out)
            self.left = net.hop(src.at[0, top], block(d, 0, quarter), x_left, out)
            self.from_core = net.landing(dst.at[0])
            self.mine = net.hop(src.at[0], block(d, 0, size), core, out, self.from_core)
            self.local = net.keep(src.at[0], block(d, 0, size))
            owners = [xd[NX - k] for k in range(1, NX)]
            others = pl.ds(0, 3 * wide)
            self.y_came = [net.landing(dst.at[0, pl.ds(0, half), others]) for o in owners]
            self.z_came = [net.landing(dst.at[0, pl.ds(0, quarter), others]) for o in owners]
            self.y_spread = [
                [net.hop(y_strip(o), y_strip(o), y_dev(b, m), out, came) for m in range(1, NY)]
                for o, came in zip(owners, self.y_came)
            ]
            self.z_spread = [
                [net.hop(z_strip(o), z_strip(o), z_near(b, m), out, came) for m in range(1, 4)]
                for o, came in zip(owners, self.z_came)
            ]
            self.far_right = net.hop(block(xd[3], 0, eighth), block(xd[3], 0, eighth), x_right, out)
            self.far_left = net.hop(block(xd[1], eighth, eighth), block(xd[1], eighth, eighth), x_left, out)
            self.across = [
                net.hop(block(o, 0, size), block(o, 0, size), core, out, self.from_core)
                for o in owners
            ]

        def begin_strips(self):
            for k in (2, 1, 3):
                self.y_strips[k - 1].start()
                self.z_strips[k - 1].start()

        def begin_blocks(self):
            start([self.right, self.left, self.mine])
            self.local.start()

        def relay_strips(self):
            for k in (1, 3, 2):
                self.y_strips[k - 1].landed()
                start(self.y_spread[k - 1])
                self.z_strips[k - 1].landed()
                start(self.z_spread[k - 1])

        def relay(self):
            self.right.landed()
            self.far_right.start()
            self.left.landed()
            self.far_left.start()

        def pass_on(self):
            for k in (1, 3, 2):
                self.y_came[k - 1].wait()
                self.z_came[k - 1].wait()
                if k == 2:
                    landed([self.far_right, self.far_left])
                self.across[k - 1].start()

        def ready(self):
            self.from_core.wait()
            self.local.wait()

    merge = Gather(wm_in, wm, 2 * TOK, grads.at[:, :, pl.ds(0, 448), pl.ds(0, D)])
    qkv = Gather(wq_in, wq, TOK, grads.at[0, :, pl.ds(0, 448)])
    outw = Gather(wo_in, wo, TOK, grads.at[0, :, pl.ds(0, 448), pl.ds(0, D)])

    mine = grads.at[s]
    theirs = grads.at[other]
    a_order = [xd[k] for k in (2, 1, 3, 0)]
    q_order = [yd[k] for k in (2, 1, 3, 0)]

    def a_rows(j):
        return (0, span(j * TOK, TOK))

    def q_cols(j):
        return (1, pl.ds(0, D), span(j * PART, PART, 128))

    out = net.sending(core_in)
    swap_a = [net.hop(theirs.at[a_rows(j)], core_in.at[a_rows(j)], core, out) for j in a_order]
    swap_q = [net.hop(theirs.at[q_cols(j)], core_in.at[q_cols(j)], core, out) for j in q_order]
    gain_swap = net.hop(gain_grads.at[other], gain_core, core)
    ring_ax = Ring(net, mine.at[0], lambda j: (j * TOK, TOK, 0, WIDE), d, x_right, x_left, ax_one, ax_two,
                   core_in.at[0, pl.ds(0, 3 * TOK)])
    ring_qy = Ring(net, mine.at[1], lambda j: (0, D, j * PART, PART), y, y_right, y_left, qy_one, qy_two,
                   core_in.at[0, :, pl.ds(0, 3 * PART)])
    to_ay = Direct(net, a_sum, lambda j: (0, TOK, j * PART, PART), y, lambda k: y_dev(b, k), ay_in)
    to_qx = Direct(net, q_sum, lambda j: (j * TOK, TOK, 0, PART), d, lambda k: x_dev(d, k), qx_in)
    three = gain_x.at[pl.ds(0, 3)]
    out, gain_x_in = net.sending(three), net.landing(three)
    gain_x_hops = [
        net.hop(gain_sum.at[xd[k]], gain_x.at[k], x_dev(d, k), out, gain_x_in) for k in range(1, NX)
    ]
    out, gain_y_in = net.sending(three), net.landing(three)
    gain_y_hops = [
        net.hop(gain_y.at[0], gain_y.at[k], y_dev(b, k), out, gain_y_in) for k in range(1, NY)
    ]
    out, gain_z_in = net.sending(seven), net.landing(seven)
    gain_z_hops = [
        net.hop(gain_z.at[0], gain_z.at[k], z_dev(b, k), out, gain_z_in) for k in range(1, NZ)
    ]
    z_rows = span(z * TALL, TALL)
    both = pl.ds(0, 2)
    seven_pieces = z_in.at[pl.ds(0, 7)]
    out, z_came = net.sending(seven_pieces), net.landing(seven_pieces)
    z_hops = [
        [
            net.hop(
                y_sum.at[which, span(lax.rem(z + k, NZ) * TALL, TALL)], z_in.at[k, which],
                z_dev(b, k), out, z_came,
            )
            for k in (4, 3, 5, 2, 6, 1, 7)[-(NZ - 1):]
        ]
        for which in (0, 1)
    ]
    def piece(k):
        at = (both, span(lax.rem(z + NZ - k, NZ) * TALL, TALL), span(y * PART, PART, 128))
        return total.at[at]

    out = net.sending(seven_pieces)
    z_back = [net.hop(piece(0), piece(0), z_dev(b, k), out) for k in range(1, NZ)]
    three_parts = total.at[both, pl.ds(0, TOK), pl.ds(0, 3 * PART)]
    out, y_came = net.sending(three_parts), net.landing(three_parts)
    y_back = [
        [net.hop(piece(k), piece(k), y_dev(b, m), out, y_came) for m in range(1, NY)]
        for k in range(NZ)
    ]
    home = [
        net.hop(y_ref.at[other, lo], y_home.at[s, hi], core),
        net.hop(y_ref.at[s, hi], y_home.at[s, lo], {"band": nxt}),
        net.hop(y_ref.at[other, hi], y_home.at[s, lo], {"band": nxt, "segment": other}),
    ]
    stays = net.keep(y_ref.at[s, lo], y_home.at[s, hi])

    def core_sum(where, count, wide):
        step = block_rows(count, wide)

        def store(r, value):
            mine[where(r, step)] = value

        add_into(
            count, step, store, [lambda r: mine[where(r, step)], lambda r: core_in[where(r, step)]]
        )

    def a_core(i):
        swap_a[i].landed()
        core_sum(lambda r, step: (0, span(a_order[i] * TOK + r, step, 16)), TOK, WIDE)

    def q_core(i):
        swap_q[i].landed()
        core_sum(lambda r, step: (1, span(r, step, 16), span(q_order[i] * PART, PART, 128)), D, PART)

    def swap():
        start(swap_a)
        gain_swap.start()

    def stage1():
        q_core(0)
        start(ring_qy.one)
        a_core(0)
        start(ring_ax.one)
        for i in (1, 2):
            a_core(i)
            ring_ax.plain[i - 1].start()
            q_core(i)
            ring_qy.plain[i - 1].start()
        gain_swap.landed()
        gain_sum[...] = gain_grads[s] + gain_core[...]
        gain_x[0] = gain_sum[d]
        start(gain_x_hops)

    def stage2():
        for which in (0, 1):
            ring_ax.fold(which)
            ring_qy.fold(which)
        a_core(3)
        q_core(3)
        gain_x_in.wait()
        gain_y[0] = (gain_x[0] + gain_x[1]) + (gain_x[2] + gain_x[3])
        start(gain_y_hops)

    def stage3():
        ring_ax.finish(a_sum)
        to_ay.begin()
        ring_qy.finish(q_sum)
        to_qx.begin()
        gain_y_in.wait()
        gain_z[0] = (gain_y[0] + gain_y[1]) + (gain_y[2] + gain_y[3])
        start(gain_z_hops)

    def masks():
        lane = lax.broadcasted_iota(jnp.int32, (16, TOK), 1)
        sub = lax.broadcasted_iota(jnp.int32, (16, TOK), 0)
        spread = (lane % 16 == sub).astype(F32).astype(BF)
        lane8 = lax.broadcasted_iota(jnp.int32, (8, TOK), 1) // 16
        sub8 = lax.broadcasted_iota(jnp.int32, (8, TOK), 0)
        here = dot((use_ref[0] == 1).astype(F32).astype(BF), spread)
        there = dot((use_ref[1] == 1).astype(F32).astype(BF), spread)
        usable = jnp.sum(
            jnp.where(lane8 + 4 == sub8, here, 0.0) + jnp.where(lane8 - 4 == sub8, there, 0.0),
            axis=0, keepdims=True,
        )
        query = lax.broadcasted_iota(jnp.int32, (TOK, TOK), 0)
        key = lax.broadcasted_iota(jnp.int32, (TOK, TOK), 1)
        same_lon = (query % 16 // 8) == (key % 16 // 8)
        same_lat = ((query // HALF) == (key // HALF)) | jnp.logical_not(b == bands - 1)
        open_key = jnp.broadcast_to(usable, (TOK, TOK)) > 0.5
        return same_lon & same_lat & (open_key | (query == key))

    first = lax.broadcasted_iota(jnp.int32, (TOK, TOK), 1) < HALF
    zero = jnp.zeros((TOK, TOK), F32)
    head0 = jnp.where(first, zero + 1.0, zero).astype(BF)
    head1 = jnp.where(first, zero, zero + 1.0).astype(BF)

    def pair_cat(values):
        return jnp.concatenate([values * head0, values * head1], axis=0)

    def gain_row(sec):
        return jnp.concatenate([gain[sec, j][0:1] for j in range(4)], axis=1)

    def tile(sec, which, i):
        return proj_ref[sec, :, which * D + TOK * i : which * D + TOK * (i + 1)]

    def forward_merge(sec, x):
        update = dot(x, wm[sec, 0:D]) + dot(x, wm[sec, D : 2 * D])
        average = jnp.mean(update, axis=-1, keepdims=True)
        centered = update - average
        spread = jnp.mean(centered * centered, axis=-1, keepdims=True)
        inverse = lax.rsqrt(spread + EPSILON)
        normed = centered * inverse
        normed_ref[sec] = normed
        hidden_ref[sec] = (normed * gain_row(sec)).astype(BF)
        return update, inverse

    def forward_attend(sec, allowed):
        proj_ref[sec] = dot(hidden_ref[sec], wq[sec]).astype(BF)
        for i in range(HEADS // 2):
            scores = dot_nt(tile(sec, 0, i), pair_cat(tile(sec, 1, i))) * 0.125
            probs = []
            for h in range(2):
                one = jnp.where(allowed, scores[:, TOK * h : TOK * (h + 1)], MASKED)
                weights = jnp.exp(one - jnp.max(one, axis=-1, keepdims=True))
                probs.append(weights / jnp.sum(weights, axis=-1, keepdims=True))
            prob = jnp.concatenate(probs, axis=1).astype(BF)
            prob_ref[sec, i] = prob
            mix_ref[sec, :, TOK * i : TOK * (i + 1)] = dot(prob, pair_cat(tile(sec, 2, i))).astype(BF)

    def forward_out(sec, update):
        result = (update + dot(mix_ref[sec], wo[sec])).astype(BF)
        y_ref[sec] = result
        return result

    def backward_attend(sec, g):
        gm = dot_nt(g, wo[sec]).astype(BF)
        for i in range(HEADS // 2):
            q, k, v = tile(sec, 0, i), tile(sec, 1, i), tile(sec, 2, i)
            gm_pair = gm[:, TOK * i : TOK * (i + 1)]
            prob = prob_ref[sec, i]
            dprob = dot_nt(gm_pair, pair_cat(v))
            pieces = []
            for h in range(2):
                half = slice(TOK * h, TOK * (h + 1))
                p = prob[:, half].astype(F32)
                dp = dprob[:, half]
                pieces.append(p * (dp - jnp.sum(dp * p, axis=-1, keepdims=True)) * 0.125)
            dscore = jnp.concatenate(pieces, axis=1).astype(BF)
            dk = dot_tn(dscore, q)
            dv = dot_tn(prob, gm_pair)
            dproj_ref[:, TOK * i : TOK * (i + 1)] = dot(dscore, pair_cat(k)).astype(BF)
            dproj_ref[:, D + TOK * i : D + TOK * (i + 1)] = jnp.where(first, dk[:TOK], dk[TOK:]).astype(BF)
            dproj_ref[:, 2 * D + TOK * i : 2 * D + TOK * (i + 1)] = jnp.where(first, dv[:TOK], dv[TOK:]).astype(BF)

    def backward_terms(sec, x, g, inverse):
        dhidden = dot_nt(dproj_ref[...], wq[sec])
        normed = normed_ref[sec]
        dgain = jnp.sum(dhidden * normed, axis=0, keepdims=True)
        for j in range(4):
            gain_grads[sec, j] = jnp.broadcast_to(dgain[:, TOK * j : TOK * (j + 1)], (8, TOK))
        dnormed = dhidden * gain_row(sec)
        gu = (
            g.astype(F32)
            + inverse
            * (
                dnormed
                - jnp.mean(dnormed, axis=-1, keepdims=True)
                - normed * jnp.mean(dnormed * normed, axis=-1, keepdims=True)
            )
        ).astype(BF)
        for c in range(4):
            part = slice(TOK * c, TOK * (c + 1))
            grads[sec, 0, part, 2 * D : 3 * D] = dot_tn(mix_ref[sec, :, part], g).astype(BF)
            term = dot_tn(x[:, part], gu).astype(BF)
            for j in (c // 2, c // 2 + 2):
                grads[sec, 0, TOK * j : TOK * (j + 1), D * (c % 2) : D * (c % 2 + 1)] = term
        return gu

    def backward_qkv(sec):
        for c in range(4):
            part = slice(TOK * c, TOK * (c + 1))
            grads[sec, 1, part] = dot_tn(hidden_ref[sec, :, part], dproj_ref[...]).astype(BF)

    for part in (merge, qkv, outw):
        part.begin_strips()
    start(shift[:2] + gain_hops + gain_core_hops[:1])
    for part in (merge, qkv, outw):
        part.begin_blocks()
    for copy in own:
        copy.start()
    shift[2].start()
    for part in (merge, qkv, outw):
        part.relay_strips()
    for part in (merge, qkv, outw):
        part.relay()
    gain_in_all.wait()
    start(gain_core_hops[1:])
    merge.pass_on()
    qkv.pass_on()
    gain_in_core.wait()
    landed(shift)
    for copy in own:
        copy.wait()
    allowed = masks()
    x0 = x_ref[...]
    merge.ready()
    update0, inverse0 = forward_merge(0, x0)
    outw.pass_on()
    qkv.ready()
    forward_attend(0, allowed)
    outw.ready()
    y0 = forward_out(0, update0)
    update1, inverse1 = forward_merge(1, y0)
    forward_attend(1, allowed)
    forward_out(1, update1)
    start(home)
    stays.start()
    cot = cot_ref[...]
    backward_attend(1, cot)
    backward_qkv(1)
    pl.when(s == 0)(lambda: start(swap_q))
    gu1 = backward_terms(1, y0, cot, inverse1)

    @pl.when(s == 0)
    def _():
        swap()

    chain = dot_nt(gu1, wm[1, 0:D]).astype(BF).astype(F32)
    side = dot_nt(gu1, wm[1, D : 2 * D]).astype(BF).astype(F32)
    g0 = (chain + side).astype(BF)

    backward_attend(0, g0)
    backward_qkv(0)
    pl.when(s == 1)(lambda: start(swap_q))
    backward_terms(0, x0, g0, inverse0)

    @pl.when(s == 1)
    def _():
        swap()
        stage1()
        stage2()
        stage3()

    @pl.when(s == 0)
    def _():
        stage1()
        stage2()
        stage3()

    to_ay.finish(y_sum.at[0])
    start(z_hops[0])
    to_qx.finish(y_sum.at[1])
    start(z_hops[1])
    value = y_sum[both, z_rows].astype(F32)
    z_came.wait()
    for k in range(1, NZ):
        value = value + z_in[k].astype(F32)
    total[both, z_rows, span(y * PART, PART, 128)] = value.astype(BF)
    start(z_back)
    start(y_back[0])
    gain_z_in.wait()
    gain_value = gain_z[0]
    for k in range(1, NZ):
        gain_value = gain_value + gain_z[k]
    gain_total[...] = gain_value
    for k in (1, 7, 2, 6, 3, 5, 4):
        if k < NZ:
            z_back[k - 1].landed()
            start(y_back[k])
    landed(home)
    stays.wait()
    y_came.wait()
    net.drain()


def widen(home_in, total, gain_in, home, merge, qkv, out, gain):
    home[...] = home_in[...]
    merge[0] = total[0, :, 0:D].astype(F32)
    merge[1] = total[0, :, D : 2 * D].astype(F32)
    out[...] = total[0, :, 2 * D : 3 * D].astype(F32)
    qkv[...] = total[1].astype(F32)
    gain[...] = gain_in[0:1]


def vmem(count):
    return [pl.BlockSpec(memory_space=pltpu.VMEM)] * count


def anywhere(count):
    return [pl.BlockSpec(memory_space=pl.ANY)] * count


def shape(dims, dtype=BF):
    return jax.ShapeDtypeStruct(dims, dtype)


def body(fields, cell_mask, merge_weight, qkv_weight, out_weight, norm_gain, out_cotangent):
    x_in = fields.reshape(2, TOK, D)
    g_in = out_cotangent.reshape(2, TOK, D)
    use = cell_mask.reshape(2, 8, 16)
    home, total, gain_total = pl.pallas_call(
        kernel,
        out_shape=(shape((2, TOK, D)), shape((2, TOK, WIDE)), shape((8, TOK), F32)),
        in_specs=anywhere(6) + vmem(1),
        out_specs=vmem(3),
        scratch_shapes=[
            pltpu.VMEM((TOK, D), BF),
            pltpu.VMEM((TOK, D), BF),
            pltpu.VMEM((2, 8, 16), jnp.int32),
            pltpu.VMEM((2, 2 * D, D), BF),
            pltpu.VMEM((2, D, 3 * D), BF),
            pltpu.VMEM((2, D, D), BF),
            pltpu.VMEM((2, 4, 8, TOK), F32),
            pltpu.VMEM((2, TOK, D), BF),
            pltpu.VMEM((2, TOK, D), F32),
            pltpu.VMEM((2, TOK, D), BF),
            pltpu.VMEM((2, TOK, 3 * D), BF),
            pltpu.VMEM((2, HEADS // 2, TOK, 2 * TOK), BF),
            pltpu.VMEM((2, TOK, D), BF),
            pltpu.VMEM((TOK, 3 * D), BF),
            pltpu.VMEM((2, 2, D, WIDE), BF),
            pltpu.VMEM((2, 4, 8, TOK), F32),
            pltpu.VMEM((2, D, WIDE), BF),
            pltpu.VMEM((2, HALF, WIDE), BF),
            pltpu.VMEM((2, TOK, WIDE), BF),
            pltpu.VMEM((2, D // 2, PART), BF),
            pltpu.VMEM((2, D, PART), BF),
            pltpu.VMEM((3, TOK, PART), BF),
            pltpu.VMEM((3, TOK, PART), BF),
            pltpu.VMEM((TOK, WIDE), BF),
            pltpu.VMEM((D, PART), BF),
            pltpu.VMEM((2, TOK, PART), BF),
            pltpu.VMEM((NZ, 2, TALL, PART), BF),
            pltpu.VMEM((4, 8, TOK), F32),
            pltpu.VMEM((4, 8, TOK), F32),
            pltpu.VMEM((4, 8, TOK), F32),
            pltpu.VMEM((NY, 8, TOK), F32),
            pltpu.VMEM((NZ, 8, TOK), F32),
            pltpu.SemaphoreType.DMA((SENDS,)),
            pltpu.SemaphoreType.DMA((RECVS,)),
            pltpu.SemaphoreType.DMA((7,)),
        ],
        compiler_params=pltpu.CompilerParams(
            collective_id=0, has_side_effects=True, vmem_limit_bytes=VMEM_LIMIT
        ),
        name="step",
    )(x_in, g_in, use, merge_weight, qkv_weight, out_weight, norm_gain)
    home, merge_grad, qkv_grad, out_grad, gain_grad = pl.pallas_call(
        widen,
        grid=(2,),
        out_shape=(
            shape((2, TOK, D)), shape((2, TOK, D), F32), shape((TOK, 3 * D), F32),
            shape((TOK, D), F32), shape((1, TOK), F32),
        ),
        in_specs=[
            pl.BlockSpec((2, 64, D), lambda i: (0, i, 0)),
            pl.BlockSpec((2, 64, WIDE), lambda i: (0, i, 0)),
            pl.BlockSpec((8, TOK), lambda i: (0, 0)),
        ],
        out_specs=[
            pl.BlockSpec((2, 64, D), lambda i: (0, i, 0)),
            pl.BlockSpec((2, 64, D), lambda i: (0, i, 0)),
            pl.BlockSpec((64, 3 * D), lambda i: (i, 0)),
            pl.BlockSpec((64, D), lambda i: (i, 0)),
            pl.BlockSpec((1, TOK), lambda i: (0, 0)),
        ],
        compiler_params=pltpu.CompilerParams(vmem_limit_bytes=VMEM_LIMIT),
        name="widen",
    )(home, total, gain_total)
    merge_grad = merge_grad.reshape(2 * TOK, D)
    section_home = home.reshape(1, 1, 2, 8, 16, D)
    return (section_home, merge_grad[None], qkv_grad[None], out_grad[None], gain_grad)


def solution(mesh):
    return jax.shard_map(
        body,
        mesh=mesh,
        in_specs=(
            P("dp", None, "band", None, None),
            P("dp", None, "band", None),
            P("segment", "dp", None),
            P("segment", "dp", None),
            P("segment", "dp", None),
            P("segment", "dp"),
            P("dp", None, "band", None, None),
        ),
        out_specs=(
            P("segment", "dp", None, "band", None, None),
            P("segment", "dp", None),
            P("segment", "dp", None),
            P("segment", "dp", None),
            P("segment", "dp"),
        ),
        check_vma=False,
    )
```
